32 devices in a mesh: dp: 8 (over z, core), fsdp: 4 (over y, x).
Axes of the slice: x: 2, y: 2, z: 4, core: 2. Of those that a mesh axis runs over, the one named last changes fastest.
Arguments:
- frames: bfloat16 [32, 512, 1024], P(('dp', 'fsdp'))
- lengths: int32 [32], P(('dp', 'fsdp')), may hold values from 1 to 512, 12288 in all
- cotangent: bfloat16 [32, 512, 1024], P(('dp', 'fsdp')), may hold values from -6 to 6
- early_up: bfloat16 [1024, 4096], P('fsdp'), may hold values from -0.1875 to 0.1875
- early_down: bfloat16 [4096, 1024], P('fsdp'), may hold values from -0.09375 to 0.09375
- heads_in: bfloat16 [1024, 3072], P('fsdp'), may hold values from -0.1875 to 0.1875
- offset_proj: bfloat16 [1024, 1024], P('fsdp'), may hold values from -0.1875 to 0.1875
- heads_out: bfloat16 [1024, 1024], P('fsdp'), may hold values from -1 to 1
- pointwise_up: bfloat16 [1024, 2048], P('fsdp'), may hold values from -0.1875 to 0.1875
- pointwise_down: bfloat16 [1024, 1024], P('fsdp'), may hold values from -0.1875 to 0.1875
- late_up: bfloat16 [1024, 4096], P('fsdp'), may hold values from -0.1875 to 0.1875
- late_down: bfloat16 [4096, 1024], P('fsdp'), may hold values from -0.09375 to 0.09375
- depthwise: bfloat16 [5, 1024], P(None, 'fsdp'), may hold values from -2.5 to 2.5
- norm_gains: bfloat16 [6, 1024], P(None, 'fsdp'), may hold values from 0.5 to 1.5
- norm_shifts: bfloat16 [6, 1024], P(None, 'fsdp'), may hold values from -1.5 to 1.5
- score_bias: bfloat16 [2, 1024], P(None, 'fsdp'), may hold values from -3 to 3
Outputs:
- output: bfloat16 [32, 512, 1024], P(('dp', 'fsdp'))
- frames_grad: float32 [32, 512, 1024], P(('dp', 'fsdp'))
- early_up_grad: float32 [1024, 4096], P('fsdp')
- early_down_grad: float32 [4096, 1024], P('fsdp')
- heads_in_grad: float32 [1024, 3072], P('fsdp')
- offset_proj_grad: float32 [1024, 1024], P('fsdp')
- heads_out_grad: float32 [1024, 1024], P('fsdp')
- pointwise_up_grad: float32 [1024, 2048], P('fsdp')
- pointwise_down_grad: float32 [1024, 1024], P('fsdp')
- late_up_grad: float32 [1024, 4096], P('fsdp')
- late_down_grad: float32 [4096, 1024], P('fsdp')
- depthwise_grad: float32 [5, 1024], P(None, 'fsdp')
- norm_gains_grad: float32 [6, 1024], P(None, 'fsdp')
- norm_shifts_grad: float32 [6, 1024], P(None, 'fsdp')
- score_bias_grad: float32 [2, 1024], P(None, 'fsdp')
The draws below stay inside these ranges and needn't reach their ends.
Inputs may be any that keep to these rules, and one draw needn't show every extreme that they name: `lengths`: each item has 1 to 512 valid frames at its start; some item has exactly 512.
All inputs are finite; a program needn't handle non-finite values. No bound on the sum of `lengths` on one device may be relied on, other than what follows from the above.
Results may differ from the reference program's by a relative error of at most 0.03.
Values may be sent and summed in bfloat16 or wider, within the bound.
A program may use at most 320 MiB of HBM per device.

```python
import math
import jax
import jax.numpy as jnp
import numpy as np
from jax import lax

D = 1024
FF = 4096
HEADS = 8
KER = 5
SEQ = 512
ITEMS = 32


def draw_frames(key, part):
    key = jax.random.fold_in(key, 11)
    noise_key, offset_key = jax.random.split(key)
    ramp = jnp.arange(ITEMS).astype(jnp.float32) / max(ITEMS - 1, 1)
    noise = jax.random.normal(noise_key, (ITEMS, SEQ, D), jnp.float32)
    amplitude = 0.4 + 0.8 * ramp
    offset = jax.random.normal(offset_key, (ITEMS, 1, D), jnp.float32)
    return (noise + amplitude[:, None, None] * offset).astype(jnp.bfloat16)


def shard_levels(key, extent, cuts, least, high):
    level = 1.0
    for position, shards_of in cuts:
        draws = jax.random.uniform(jax.random.fold_in(jax.random.fold_in(key, 6), position), (shards_of,), jnp.float32, least / len(cuts), high / len(cuts))
        level = level * jnp.repeat(jnp.exp(draws), extent[position] // shards_of).reshape((-1,) + (1,) * (len(extent) - 1 - position))
    return level


def length_profile(number_of, total, reach, lean):
    loads = [(1 << 20) // math.isqrt(rank ** lean) + 1 for rank in range(2, number_of + 1)]
    spare, holding = total - reach - (number_of - 1), [1] * (number_of - 1)
    while spare > 0:
        movable = [i for i in range(number_of - 1) if holding[i] < reach]
        whole, remaining = sum([loads[i] for i in movable]), spare
        for i in movable:
            extra = min(reach - holding[i], max(1, remaining * loads[i] // whole), spare)
            holding[i] = holding[i] + extra
            spare = spare - extra
    return np.array([reach] + holding)


def uneven(stream_key, number_of, total, limit, lean):
    if number_of == 2:
        one = jax.random.randint(stream_key, (), max(1, total - limit), min(limit, total - 1) + 1)
        return jnp.stack([one, total - one])
    sizes = jnp.asarray(length_profile(number_of, total, limit, lean), jnp.int32)
    twos = (number_of - 1) // 2
    donor, receiver = sizes[1:1 + 2 * twos:2], sizes[2:2 + 2 * twos:2]
    margin = jnp.minimum(donor - 1, limit - receiver)
    shifted = jax.random.randint(jax.random.fold_in(stream_key, 1), (twos,), 0, 1 << 20) % (margin + 1)
    sizes = sizes.at[1:1 + 2 * twos:2].set(donor - shifted).at[2:2 + 2 * twos:2].set(receiver + shifted)
    return sizes[jax.random.permutation(jax.random.fold_in(stream_key, 2), number_of)]


def bell_draw(stream_key, dims, scale, bound, cuts=(), held_as=jnp.bfloat16):
    array = scale * jax.random.normal(stream_key, dims, jnp.float32)
    if cuts:
        array = array * shard_levels(stream_key, dims, cuts, -0.22, 0.18)
    return jnp.clip(array, -bound, bound).astype(held_as)


def setup_inputs(seed: int = 0) -> dict:
    arg_keys = jax.random.split(jax.random.key(seed), 17)
    return {
        "frames": draw_frames(jax.random.fold_in(arg_keys[16], 71), 0),
        "lengths": uneven(arg_keys[1], ITEMS, ITEMS * SEQ * 3 // 4, SEQ, 1).astype(jnp.int32),
        "cotangent": bell_draw(arg_keys[2], (ITEMS, SEQ, D), 1.0, 6.0, ((0, 32),)),
        "early_up": bell_draw(arg_keys[3], (D, FF), D ** -0.5, 0.1875, ((0, 4),)),
        "early_down": bell_draw(arg_keys[4], (FF, D), FF ** -0.5, 0.09375, ((0, 4),)),
        "heads_in": bell_draw(arg_keys[5], (D, 3 * D), D ** -0.5, 0.1875, ((0, 4),)),
        "offset_proj": bell_draw(arg_keys[6], (D, D), D ** -0.5, 0.1875, ((0, 4),)),
        "heads_out": bell_draw(arg_keys[7], (D, D), (max(16, D * 16 // SEQ)) ** -0.5, 1.0, ((0, 4),)),
        "pointwise_up": bell_draw(arg_keys[8], (D, 2 * D), D ** -0.5, 0.1875, ((0, 4),)),
        "pointwise_down": bell_draw(arg_keys[9], (D, D), D ** -0.5, 0.1875, ((0, 4),)),
        "late_up": bell_draw(arg_keys[10], (D, FF), D ** -0.5, 0.1875, ((0, 4),)),
        "late_down": bell_draw(arg_keys[11], (FF, D), FF ** -0.5, 0.09375, ((0, 4),)),
        "depthwise": bell_draw(arg_keys[12], (KER, D), KER ** -0.5, 2.5, ((1, 4),)),
        "norm_gains": jnp.clip(1.0 + 0.1 * jax.random.normal(arg_keys[13], (6, D), jnp.float32), 0.5, 1.5).astype(jnp.bfloat16),
        "norm_shifts": bell_draw(arg_keys[14], (6, D), 0.3, 1.5, ((1, 4),)),
        "score_bias": bell_draw(arg_keys[15], (2, D), 0.5, 3.0, ((1, 4),)),
    }


EPS = 1e-05
HIGH = lax.Precision.HIGHEST

@jax.custom_vjp
def low(v):
    return lax.optimization_barrier(v.astype(jnp.bfloat16)).astype(jnp.float32)

@jax.custom_vjp
def low_back(v):
    return v

def low_keep(v):
    return (low(v), None)

def low_pass(kept, grad):
    return (grad,)

def back_keep(v):
    return (v, None)

def back_low(kept, grad):
    return (low(grad),)
low.defvjp(low_keep, low_pass)
low_back.defvjp(back_keep, back_low)

def matmul(left, right):
    return jnp.dot(left, right, precision=HIGH, preferred_element_type=jnp.float32)

def layer_norm(values, gain, shift):
    center = values - lax.optimization_barrier(jnp.mean(values, axis=-1, keepdims=True))
    spread = lax.optimization_barrier(jnp.mean(center * center, axis=-1, keepdims=True))
    return center * lax.rsqrt(spread + EPS) * gain + shift

def position_table(span, width):
    rows = jnp.arange(2 * span - 1)
    distance = (span - 1 - rows).astype(jnp.float32)
    columns = jnp.arange(width // 2).astype(jnp.float32)
    rate = jnp.exp(columns * (-2.0 * math.log(10000.0) / width))
    angle = distance[:, None] * rate[None, :]
    return jnp.concatenate([jnp.sin(angle), jnp.cos(angle)], axis=1)

def rel_shift(placed):
    lead = placed.shape[:-2]
    span = placed.shape[-2]
    padded = jnp.pad(placed, [(0, 0)] * (placed.ndim - 1) + [(0, 1)])
    flat = padded.reshape(lead + (2 * span * span,))
    flat = flat[..., span - 1:span - 1 + span * (2 * span - 1)]
    return flat.reshape(lead + (span, 2 * span - 1))[..., :span]

def feed_forward(state, up_proj, down_proj, gain, shift):
    hidden = low(layer_norm(state, gain, shift))
    inner = low_back(matmul(hidden, up_proj))
    active = low(jax.nn.silu(inner))
    return state + 0.5 * low_back(matmul(active, down_proj))

def attention(state, valid, heads_in, offset_proj, heads_out, score_bias, gain, shift, table):
    span, width = state.shape
    head_size = width // HEADS
    hidden = low(layer_norm(state, gain, shift))
    joint = low_back(matmul(hidden, heads_in))
    query = joint[:, :width]
    keys = low(joint[:, width:2 * width]).reshape(span, HEADS, head_size)
    values = low(joint[:, 2 * width:]).reshape(span, HEADS, head_size)
    query_content = low(query + score_bias[0]).reshape(span, HEADS, head_size)
    query_offset = low(query + score_bias[1]).reshape(span, HEADS, head_size)
    offsets = low(low_back(matmul(table, offset_proj))).reshape(2 * span - 1, HEADS, head_size)
    content = jnp.einsum('she,the->hst', query_content, keys, precision=HIGH)
    placed = jnp.einsum('she,mhe->hsm', query_offset, offsets, precision=HIGH)
    raw = low_back(content + rel_shift(placed))
    scores = jnp.where(valid[None, None, :] > 0.5, raw * head_size ** (-0.5), -1e+30)
    probs = low(jax.nn.softmax(scores, axis=-1))
    mixed = jnp.einsum('hst,the->she', probs, values, precision=HIGH).reshape(span, width)
    mixed = low(low_back(mixed))
    return state + low_back(matmul(mixed, heads_out))

def glu_conv(lifted, kernel, valid):
    span = valid.shape[0]
    width = kernel.shape[1]
    gated = lifted[:, :width] * jax.nn.sigmoid(lifted[:, width:]) * valid[:, None]
    half = kernel.shape[0] // 2
    padded = jnp.pad(gated, ((half, half), (0, 0)))
    total = jnp.zeros_like(gated)
    for index in range(kernel.shape[0]):
        total = total + kernel[index] * padded[index:index + span]
    return total

def front_item(frame, valid, weights, table):
    early_up, early_down, heads_in, offset_proj, heads_out, pointwise_up, pointwise_down, late_up, late_down, depthwise, gains, shifts, score_bias = weights
    state = feed_forward(frame, early_up, early_down, gains[0], shifts[0])
    state = attention(state, valid, heads_in, offset_proj, heads_out, score_bias, gains[1], shifts[1], table)
    hidden = low(layer_norm(state, gains[2], shifts[2]))
    lifted = low_back(matmul(hidden, pointwise_up))
    return (state, glu_conv(lifted, depthwise, valid))

def back_item(state, convolved, valid, mean, inverse, weights):
    early_up, early_down, heads_in, offset_proj, heads_out, pointwise_up, pointwise_down, late_up, late_down, depthwise, gains, shifts, score_bias = weights
    normal = (convolved - mean) * inverse
    scaled = normal * gains[5] + shifts[5]
    swished = low(jax.nn.silu(scaled))
    state = state + low_back(matmul(swished, pointwise_down))
    state = feed_forward(state, late_up, late_down, gains[3], shifts[3])
    return layer_norm(state, gains[4], shifts[4]) * valid[:, None]

def reference(frames, lengths, cotangent, early_up, early_down, heads_in, offset_proj, heads_out, pointwise_up, pointwise_down, late_up, late_down, depthwise, norm_gains, norm_shifts, score_bias):
    valid = (jnp.arange(SEQ)[None, :] < lengths[:, None]).astype(jnp.float32)
    table = low(position_table(SEQ, D))
    params = tuple((weight.astype(jnp.float32) for weight in (early_up, early_down, heads_in, offset_proj, heads_out, pointwise_up, pointwise_down, late_up, late_down, depthwise, norm_gains, norm_shifts, score_bias)))

    def forward(inputs, weights):
        front = jax.checkpoint(lambda pair: front_item(pair[0], pair[1], weights, table))
        states, convolved = lax.map(front, (inputs, valid))
        mask = valid[:, :, None]
        count = jnp.sum(valid)
        mean = lax.optimization_barrier(jnp.sum(convolved * mask, axis=(0, 1))) / count
        inverse = lax.rsqrt(lax.optimization_barrier(jnp.sum(convolved * convolved * mask, axis=(0, 1))) / count - mean * mean + EPS)
        back = jax.checkpoint(lambda trio: back_item(trio[0], trio[1], trio[2], mean, inverse, weights))
        return lax.map(back, (states, convolved, valid))
    output, pullback = jax.vjp(forward, frames.astype(jnp.float32), params)
    frames_grad, grads = pullback(cotangent.astype(jnp.float32))
    return (output.astype(jnp.bfloat16), frames_grad, grads[0], grads[1], grads[2], grads[3], grads[4], grads[5], grads[6], grads[7], grads[8], grads[9], grads[10], grads[11], grads[12])
```

```python
import functools
import math
import types

import jax
import jax.numpy as jnp
import numpy as np
from jax import lax
from jax.experimental import pallas as pl
from jax.experimental.pallas import tpu as pltpu
from jax.sharding import PartitionSpec as P

MESH = pl.DeviceIdType.MESH


def flip(index, bit):
    return index + bit - 2 * bit * ((index // bit) % 2)


def bits_of(count):
    bits, bit = [], 1
    while bit < count:
        bits.append(bit)
        bit *= 2
    return bits


def span_of(bits):
    held = [0]
    for bit in bits:
        held = held + [h + bit for h in held]
    return held


def flips(index, mask):
    bit = 1
    while bit <= mask:
        if mask & bit:
            index = flip(index, bit)
        bit *= 2
    return index


def gather_items(shapes):
    items = []
    for w, (rows, cols) in enumerate(shapes):
        half = rows // 2
        row_step = min(half, 128 if w == len(shapes) - 1 else 256)
        col_step = cols if cols <= 2048 else (2048 if cols % 2048 == 0 else 1536)
        for row in range(0, half, row_step):
            for col in range(0, cols, col_step):
                tiles = col_step // 128
                side = tiles // 3
                if tiles % 3 == 2 and len(items) % 2:
                    side += 1
                items.append((w, row, row_step, col, side * 128, (tiles - 2 * side) * 128))
    return items


UR = 128


def unit_cols(count):
    return 2048 // count

LAG = 2
RING = 2 * LAG + 2
ZRING = 6
ORING = 32
CRING = 4


def outer(left, right):
    return lax.dot_general(left, right, (((0,), (0,)), ((), ())), preferred_element_type=jnp.float32)


def unpack_kernel(tiles, packed, *refs):
    wide_cols = packed.shape[3]
    many = len(tiles)
    outs, (held, load, store) = refs[:many], refs[2 * many :]
    wide = refs[many : 2 * many]
    copies, base = [], 0
    for w, (nr, nc) in enumerate(tiles):
        copy = pltpu.make_async_copy(packed.at[:, pl.ds(base, nr * nc)], held.at[:, pl.ds(base, nr * nc)], load.at[w])
        copy.start()
        copies.append(copy)
        base += nr * nc
    base, stores = 0, []
    for w, (nr, nc) in enumerate(tiles):
        copies[w].wait()
        for core in range(2):
            for col in range(nc):
                @pl.loop(0, nr)
                def _(row, w=w, core=core, col=col, base=base, nc=nc):
                    wide[w][pl.ds(pl.multiple_of(row * UR, UR), UR), (core * nc + col) * wide_cols : (core * nc + col + 1) * wide_cols] = (
                        held[core, base + row * nc + col].astype(jnp.float32))
        copy = pltpu.make_async_copy(wide[w], outs[w], store.at[w])
        copy.start()
        stores.append(copy)
        base += nr * nc
    for copy in stores:
        copy.wait()


def unpack(packed, count, shapes):
    any_ = pl.BlockSpec(memory_space=pl.ANY)
    out_shape = [jax.ShapeDtypeStruct((r // count, c), jnp.float32) for r, c in shapes]
    tiles = [(r // count // UR, c // 2 // packed.shape[3]) for r, c in shapes]
    dma = pltpu.SemaphoreType.DMA((len(shapes),))
    return pl.pallas_call(
        functools.partial(unpack_kernel, tiles),
        out_shape=out_shape,
        in_specs=[any_],
        out_specs=[any_] * len(shapes),
        scratch_shapes=[pltpu.VMEM(s.shape, s.dtype) for s in out_shape] + [pltpu.VMEM(packed.shape, packed.dtype), dma, dma],
        compiler_params=pltpu.CompilerParams(vmem_limit_bytes=60 * 2**20),
        name="unpack_gradients",
    )(packed)


def dot_nn(left, right):
    return lax.dot_general(left, right, (((1,), (0,)), ((), ())), preferred_element_type=jnp.float32)


def dot_nt(left, right):
    return lax.dot_general(left, right, (((1,), (1,)), ((), ())), preferred_element_type=jnp.float32)


def dot_tn(left, right):
    return lax.dot_general(left, right, (((0,), (0,)), ((), ())), preferred_element_type=jnp.float32)


EPS = 1e-05
COLS = 256


def sigmoid(v):
    return 0.5 * jnp.tanh(0.5 * v) + 0.5


def sum_scratch(count, depth, width):
    dma = pltpu.SemaphoreType.DMA((count + depth - 1,))
    return [pltpu.VMEM((8, width), jnp.float32), pltpu.VMEM((8, width), jnp.float32),
            pltpu.VMEM((count, 8, width), jnp.float32), pltpu.VMEM((depth, 8, width), jnp.float32), dma, dma]


CHUNK = 512
LEAD = 1
BUDGET = 9.0


def forward_kernel(count, depth, heads, shapes, items, saved_names, in_names, out_names, scratch_names, *refs):
    many = len(shapes)
    edges = np.cumsum([0, len(in_names), many, many, len(saved_names), len(out_names), len(scratch_names)])
    groups = [refs[i:j] for i, j in zip(edges[:-1], edges[1:])]
    shards, wholes, saved = groups[1], groups[2], groups[3]
    r = types.SimpleNamespace(**dict(zip(in_names, groups[0])), **dict(zip(out_names, groups[4])), **dict(zip(scratch_names, groups[5])))
    k = types.SimpleNamespace(**{name: i for i, name in enumerate(saved_names)})
    send, recv = r.send, r.recv
    bits = bits_of(count)
    dp, me = lax.axis_index("dp"), lax.axis_index("fsdp")
    core, place = lax.rem(dp, 2), dp // 2
    side = lax.rem(place, 2)
    mate, twin = flip(dp, 1), flip(dp, 2)
    span, width = r.frames.shape
    inner_width = saved[k.inner1].shape[1]
    size = width // heads
    scale = size ** -0.5

    barrier = pltpu.get_barrier_semaphore()
    pl.semaphore_signal(barrier, inc=1, device_id=(mate, me), device_id_type=MESH)
    for mask in range(1, count):
        pl.semaphore_signal(barrier, inc=1, device_id=(dp, flips(me, mask)), device_id_type=MESH)
    for j in range(1, depth):
        pl.semaphore_signal(barrier, inc=1, device_id=(lax.rem(dp + 2 * j, 2 * depth), me), device_id_type=MESH)
    pl.semaphore_wait(barrier, 1 + count - 1 + depth - 1)

    def remote(src, dst, send_sem, recv_sem, device):
        return pltpu.make_async_remote_copy(
            src_ref=src, dst_ref=dst, send_sem=send_sem, recv_sem=recv_sem, device_id=device, device_id_type=MESH)

    wide = r.small.shape[1]
    here = pl.ds(pl.multiple_of(me * wide, 128), wide)
    small_copies = [remote(r.small, r.small_held.at[:, here], r.small_send.at[mask], r.small_recv.at[mask], (dp, flips(me, mask)))
                    for mask in range(1, count)]
    for copy in small_copies:
        copy.start()
    own_copies = [remote(shards[w], wholes[w].at[pl.ds(pl.multiple_of(me * shapes[w][0], 16), shapes[w][0])],
                         r.own_send.at[w], r.own_recv.at[w], (mate, me)) for w in range(many)]
    steps = len(bits)
    kinds = 2 * steps + 3

    def parts(t):
        w, row, rows, col, edge, middle = items[t]
        base = core * (shapes[w][0] // 2) + row
        plane = pl.ds(pl.multiple_of(col + side * edge, 128), edge + middle)
        given = pl.ds(pl.multiple_of(col + side * (edge + middle), 128), edge)
        taken = pl.ds(pl.multiple_of(col + (1 - side) * (edge + middle), 128), edge)
        return w, base, rows, plane, given, taken, edge

    def block(w, owner, start, rows, cols):
        return wholes[w].at[pl.ds(pl.multiple_of(owner * shapes[w][0] + start, 16), rows), cols]

    def plane_send(t, step):
        w, base, rows, plane, *_ = parts(t)
        if step == 0 and (t == 0 or items[t - 1][0] != w):
            own_copies[w].start()
        for piece in range(2):
            order = bits if piece == 0 else bits[::-1]
            start, extent = base + piece * (rows // 2), rows // 2
            for mask in span_of(order[:step]):
                owner = flips(me, mask)
                src = (shards[w].at[pl.ds(pl.multiple_of(start, 16), extent), plane] if mask == 0
                       else block(w, owner, start, extent, plane))
                remote(src, block(w, owner, start, extent, plane), send.at[t, 2 * step + piece],
                       recv.at[t, 2 * step + piece], (dp, flips(me, order[step]))).start()

    def several(t, cols, kind, device):
        w, base, rows, *_ = parts(t)
        for mask in range(1, count):
            ref = block(w, flips(me, mask), base, rows, cols)
            remote(ref, ref, send.at[t, kind], recv.at[t, kind], device).start()

    def sizes(t, kind):
        _, _, rows, _, edge, middle = items[t]
        if kind < 2 * steps:
            return rows // 2 * 2 ** (kind // 2), edge + middle
        return rows * (count - 1), edge if kind != 2 * steps + 1 else edge + middle

    def wait(sems, t, kind):
        rows, cols = sizes(t, kind)
        if cols:
            ref = wholes[items[t][0]].at[pl.ds(0, rows), pl.ds(0, cols)]
            pltpu.make_async_copy(ref, ref, sems.at[t, kind]).wait()

    total = len(items)

    def gather_tick(tick):
        t = tick + LEAD
        if t < total and tick >= 0:
            plane_send(t, 0)
        for step in range(1, steps):
            t = tick - step
            if 0 <= t < total:
                wait(recv, t, 2 * step - 2)
                wait(recv, t, 2 * step - 1)
                plane_send(t, step)
        t = tick - steps
        if 0 <= t < total:
            wait(recv, t, 2 * steps - 2)
            wait(recv, t, 2 * steps - 1)
            _, _, _, plane, given, taken, edge = parts(t)
            if edge:
                several(t, given, 2 * steps, (twin, me))
            several(t, plane, 2 * steps + 1, (mate, me))
        t = tick - steps - 1
        if 0 <= t < total:
            wait(recv, t, 2 * steps)
            if parts(t)[6]:
                several(t, parts(t)[5], 2 * steps + 2, (mate, me))
        t = tick - steps - 2
        if 0 <= t < total:
            wait(recv, t, 2 * steps + 1)
            wait(recv, t, 2 * steps + 2)
            w = items[t][0]
            if t == 0 or items[t - 1][0] != w:
                own_copies[w].wait_recv()
            return t
        return None

    loads = {}

    def load(index, src, dst):
        loads[index] = pltpu.make_async_copy(src, dst, r.load_sem.at[index])
        loads[index].start()

    def ready(*need):
        for index in need:
            loads.pop(index).wait()

    def store(index, src):
        pltpu.make_async_copy(src, saved[index], r.store_sem.at[index]).start()

    stored = set()

    def stored_wait(index):
        pltpu.make_async_copy(saved[index], saved[index], r.store_sem.at[index]).wait()
        stored.add(index)

    gain = lambda n: r.small_all[n : n + 1]
    shift = lambda n: r.small_all[6 + n : 7 + n]

    def normed(v):
        center = v - jnp.mean(v, axis=-1, keepdims=True)
        return center * lax.rsqrt(jnp.mean(center * center, axis=-1, keepdims=True) + EPS)

    def norm_rows(src, n, dst):
        @pl.loop(0, span // 64)
        def _(i):
            rows = pl.ds(pl.multiple_of(i * 64, 64), 64)
            dst[rows] = (normed(src[rows].astype(jnp.float32)) * gain(n) + shift(n)).astype(jnp.bfloat16)

    def begin():
        r.small_held[:, here] = r.small[...]
        for copy in small_copies:
            copy.wait()
        r.small_all[...] = r.small_held[...].astype(jnp.float32)
        r.small_out[...] = r.small_all[...]
        norm_rows(r.frames, 0, r.hid1)
        store(k.hidden1, r.hid1)

    def up_half(hidden, part, parts_of):
        chunks = inner_width // CHUNK // parts_of

        @pl.loop(part * chunks, (part + 1) * chunks)
        def _(i):
            cols = pl.ds(pl.multiple_of(i * CHUNK, CHUNK), CHUNK)
            inner = dot_nn(hidden[...], r.up_vm[:, cols])
            r.inner_vm[:, cols] = inner.astype(jnp.bfloat16)
            r.active_vm[:, cols] = (inner * sigmoid(inner)).astype(jnp.bfloat16)

    def after_early():
        store(k.inner1, r.inner_vm)
        store(k.active1, r.active_vm)
        store(k.x1, r.xa)
        norm_rows(r.xa, 1, r.hid2)
        store(k.hidden2, r.hid2)

    def project(which):
        @pl.loop(0, width // CHUNK)
        def _(i):
            cols = pl.ds(pl.multiple_of(i * CHUNK, CHUNK), CHUNK)
            out = dot_nn(r.hid2[...], r.up_vm[:, pl.ds(pl.multiple_of(i * CHUNK + which * width, CHUNK), CHUNK)])
            if which == 0:
                r.content_vm[:, cols] = (out + r.small_all[12:13, cols]).astype(jnp.bfloat16)
                r.offset_vm[:, cols] = (out + r.small_all[13:14, cols]).astype(jnp.bfloat16)
            else:
                dst = r.keys_vm if which == 1 else r.values_vm
                dst[:, cols] = out.astype(jnp.bfloat16)
        if which == 0:
            store(k.content, r.content_vm)
            store(k.offset, r.offset_vm)
        else:
            store(k.keys, r.keys_vm) if which == 1 else store(k.values, r.values_vm)

    def place_offsets():
        ready(3, 4)

        @pl.loop(0, width // CHUNK)
        def _(i):
            cols = pl.ds(pl.multiple_of(i * CHUNK, CHUNK), CHUNK)
            out = dot_nn(r.table_vm[...], r.up_vm[:, pl.ds(pl.multiple_of(i * CHUNK + 3 * width, CHUNK), CHUNK)])
            r.offsets_vm[:, cols] = out.astype(jnp.bfloat16)
        store(k.offsets, r.offsets_vm)

    def attend(first, last):
        @pl.loop(first, last)
        def _(h):
            cols = pl.ds(pl.multiple_of(h * size, size), size)
            slot = lax.rem(h, 2)
            placed = dot_nt(r.offset_vm[:, cols], r.offsets_vm[:, cols])
            moved = pltpu.roll(placed, span + 1, 1, stride=1, stride_axis=0)[:, :span]
            raw = (dot_nt(r.content_vm[:, cols], r.keys_vm[:, cols]) + moved) * scale
            column = lax.broadcasted_iota(jnp.int32, raw.shape, 1)
            scores = jnp.where(column < r.length[0], raw, -1e30)
            grown = jnp.exp(scores - jnp.max(scores, axis=1, keepdims=True))
            probs = (grown * (1.0 / jnp.sum(grown, axis=1, keepdims=True))).astype(jnp.bfloat16)

            @pl.when(h >= 2)
            def _():
                pltpu.make_async_copy(r.probs_vm.at[slot], saved[k.probs].at[h], r.probs_sem.at[slot]).wait()
            r.probs_vm[slot] = probs
            pltpu.make_async_copy(r.probs_vm.at[slot], saved[k.probs].at[h], r.probs_sem.at[slot]).start()
            r.mixed_vm[:, cols] = dot_nn(probs, r.values_vm[:, cols]).astype(jnp.bfloat16)

    def after_attention():
        for slot in range(2):
            pltpu.make_async_copy(r.probs_vm.at[slot], saved[k.probs].at[0], r.probs_sem.at[slot]).wait()
        store(k.mixed, r.mixed_vm)
        ready(5)

        @pl.loop(0, width // 256)
        def _(i):
            cols = pl.ds(pl.multiple_of(i * 256, 256), 256)
            r.xb[:, cols] = r.xa[:, cols] + dot_nn(r.mixed_vm[...], r.down_vm[0:width, cols])
        store(k.x2, r.xb)
        norm_rows(r.xb, 2, r.hid3)
        store(k.hidden3, r.hid3)

    def valid_mask():
        return jnp.where(lax.broadcasted_iota(jnp.int32, (span, 1), 0) < r.length[0], 1.0, 0.0)

    taps = 5
    half = taps // 2

    def convolve():
        ready(6, 7)
        mask = valid_mask()
        r.padded[0:8] = jnp.zeros((8, 256), jnp.float32)
        r.padded[8 + span : 16 + span] = jnp.zeros((8, 256), jnp.float32)
        r.vec[...] = jnp.zeros_like(r.vec)
        r.vec[2:3] = jnp.full((1, width), 1.0, jnp.float32) * jnp.sum(mask)

        @pl.loop(0, width // 256)
        def _(i):
            cols = pl.ds(pl.multiple_of(i * 256, 256), 256)
            gates = pl.ds(pl.multiple_of(i * 256 + width, 256), 256)
            value = dot_nn(r.hid3[...], r.down_vm[width : 2 * width, cols])
            gate = dot_nn(r.hid3[...], r.down_vm[2 * width : 3 * width, cols])
            r.lifted_vm[:, cols] = value.astype(jnp.bfloat16)
            r.lifted_vm[:, gates] = gate.astype(jnp.bfloat16)
            r.padded[8 : 8 + span] = value * sigmoid(gate) * mask
            out = jnp.zeros((span, 256), jnp.float32)
            for tap in range(taps):
                out = out + r.small_all[14 + tap : 15 + tap, cols] * r.padded[8 + tap - half : 8 + tap - half + span]
            r.conv_vm[:, cols] = out
            masked = out * mask
            r.vec[0:1, cols] = jnp.sum(masked, axis=0, keepdims=True)
            r.vec[1:2, cols] = jnp.sum(masked * out, axis=0, keepdims=True)
        store(k.lifted, r.lifted_vm)
        store(k.convolved, r.conv_vm)

    pair_copy = remote(r.vec, r.pair, r.sum_send.at[0], r.sum_recv.at[0], (mate, me))
    plane_copies = [remote(r.plane.at[me], r.plane.at[me], r.sum_send.at[m], r.sum_recv.at[m], (dp, flips(me, m)))
                    for m in range(1, count)]
    line_copies = [remote(r.line.at[place], r.line.at[place], r.sum_send.at[count - 1 + j], r.sum_recv.at[count - 1 + j],
                          (lax.rem(dp + 2 * j, 2 * depth), me)) for j in range(1, depth)]

    def sum_pair():
        pair_copy.start()

    def sum_plane():
        pair_copy.wait()
        r.plane[me] = r.vec[...] + r.pair[...]
        for copy in plane_copies:
            copy.start()

    def sum_line():
        for copy in plane_copies:
            copy.wait()
        r.line[place] = functools.reduce(jnp.add, [r.plane[f] for f in range(count)])
        for copy in line_copies:
            copy.start()

    def after_conv():
        for copy in line_copies:
            copy.wait()
        sums = functools.reduce(jnp.add, [r.line[z] for z in range(depth)])
        frames = sums[2:3]
        mean = sums[0:1] / frames
        inverse = lax.rsqrt(sums[1:2] / frames - mean * mean + EPS)
        r.stats[...] = jnp.concatenate([mean, inverse, frames, jnp.zeros((5, width), jnp.float32)], axis=0)
        ready(8)

        @pl.loop(0, width // 256)
        def _(i):
            cols = pl.ds(pl.multiple_of(i * 256, 256), 256)
            normal = (r.conv_vm[:, cols] - r.stats[0:1, cols]) * r.stats[1:2, cols]
            scaled = normal * r.small_all[5:6, cols] + r.small_all[11:12, cols]
            r.swished_vm[:, cols] = (scaled * sigmoid(scaled)).astype(jnp.bfloat16)
        store(k.swished, r.swished_vm)
        stored_wait(k.x1)

        @pl.loop(0, width // 256)
        def _(i):
            cols = pl.ds(pl.multiple_of(i * 256, 256), 256)
            r.xa[:, cols] = r.xb[:, cols] + dot_nn(r.swished_vm[...], r.down_vm[3 * width : 4 * width, cols])

    def after_conv_norm():
        store(k.x3, r.xa)
        norm_rows(r.xa, 3, r.hid4)
        store(k.hidden4, r.hid4)
        stored_wait(k.inner1)
        stored_wait(k.active1)

    def late_done():
        store(k.inner4, r.inner_vm)
        store(k.active4, r.active_vm)
        stored_wait(k.x2)

    def final():
        r.edge_grads[...] = jnp.zeros_like(r.edge_grads)

        @pl.loop(0, span // 64)
        def _(i):
            start = pl.multiple_of(i * 64, 64)
            rows = pl.ds(start, 64)
            mask = jnp.where(start + lax.broadcasted_iota(jnp.int32, (64, 1), 0) < r.length[0], 1.0, 0.0)
            v = r.xb[rows]
            center = v - jnp.mean(v, axis=-1, keepdims=True)
            rate = lax.rsqrt(jnp.mean(center * center, axis=-1, keepdims=True) + EPS)
            normal = center * rate
            r.output[rows] = ((normal * gain(4) + shift(4)) * mask).astype(jnp.bfloat16)
            grad = r.cotangent[rows].astype(jnp.float32) * mask
            r.edge_grads[0:1] += jnp.sum(grad * normal, axis=0, keepdims=True)
            r.edge_grads[1:2] += jnp.sum(grad, axis=0, keepdims=True)
            inner = grad * gain(4)
            back = rate * (inner - jnp.mean(inner, axis=-1, keepdims=True)
                           - normal * jnp.mean(inner * normal, axis=-1, keepdims=True))
            r.xa[rows] = back
            r.branch_vm[rows] = (0.5 * back).astype(jnp.bfloat16)
        store(k.grad4, r.xa)
        store(k.branch4, r.branch_vm)

    def down_copies(t, w, sems):
        _, row, rows, *_ = items[t]
        shard, part = shapes[w][0], t - min(u for u in range(total) if items[u][0] == w)
        starts = [f * shard + c * (shard // 2) + row for f in range(count) for c in range(2)]
        return rows, starts, [pltpu.make_async_copy(wholes[w].at[pl.ds(start, rows)], r.down_vm.at[pl.ds(start, rows)], sems.at[part, i])
                              for i, start in enumerate(starts)]

    def down_fetch(t, w, sems):
        for copy in down_copies(t, w, sems)[2]:
            copy.start()

    def down_part(t, w, sems, src, dst):
        rows, starts, copies = down_copies(t, w, sems)
        for copy in copies:
            copy.wait()

        @pl.loop(0, width // 256)
        def _(i):
            cols = pl.ds(pl.multiple_of(i * 256, 256), 256)
            acc = functools.reduce(jnp.add, [dot_nn(r.active_vm[:, s : s + rows], r.down_vm[s : s + rows, cols]) for s in starts])
            dst[:, cols] = src[:, cols].astype(jnp.float32) + 0.5 * acc

    def before_final():
        stored_wait(k.x3)

    up, down = r.up_vm, r.down_vm
    last = [max(t for t in range(total) if items[t][0] == w) for w in range(many)]
    phases = []

    def phase(item, cost, *work):
        phases.append((item, cost, work))

    def fetch(index, src, dst):
        return lambda: load(index, src, dst)

    def call(function, *args):
        return lambda: function(*args)

    phase(-1, 1.5, begin)
    early = [t for t in range(total) if items[t][0] == 0]
    late = [t for t in range(total) if items[t][0] == 7]

    arrivals = []

    def up_loads(ts, w, index, after):
        for n, t in enumerate(ts):
            cols = pl.ds(items[t][3], 2 * items[t][4] + items[t][5])
            arrivals.append((t, after, fetch(index + n, wholes[w].at[:, cols], up.at[:, cols])))

    def down_loads(w, sems, after):
        for t in range(total):
            if items[t][0] == w:
                arrivals.append((t, after, call(down_fetch, t, w, sems)))

    up_loads(early, 0, 0, 0)
    for n, t in enumerate(early):
        phase(t, 3.2, call(ready, n), call(up_half, r.hid1, n, len(early)))
    up_over = len(phases)
    down_loads(1, r.early_sem, 0)
    firsts = [t for t in range(total) if items[t][0] == 1]
    for t in firsts:
        phase(t, 4.5 / len(firsts), call(down_part, t, 1, r.early_sem, r.frames if t == firsts[0] else r.xa, r.xa))
    down_over = len(phases)
    phase(last[1], 1.5, after_early)
    arrivals.append((last[2], up_over, fetch(10, wholes[2], up.at[:, pl.ds(0, 3 * width)])))
    phase(last[2], 2.5, call(ready, 10), call(project, 0), call(project, 1), call(project, 2))
    arrivals.append((last[3], up_over, lambda: (load(3, wholes[3], up.at[:, pl.ds(3 * width, width)]), load(4, r.table, r.table_vm))))
    phase(last[3], 3.0, place_offsets)
    lift_over = len(phases)
    for h in range(0, heads, 2):
        phase(last[3], 2.0, call(attend, h, h + 2))
    arrivals.append((last[4], down_over, fetch(5, wholes[4], down.at[pl.ds(0, width)])))
    phase(last[4], 2.0, after_attention)
    arrivals.append((last[5], down_over, lambda: (load(6, wholes[5].at[:, pl.ds(0, width)], down.at[pl.ds(width, width)]),
                                                  load(7, wholes[5].at[:, pl.ds(width, width)], down.at[pl.ds(2 * width, width)]))))
    phase(last[5], 5.5, convolve)
    phase(last[5], 0.1, sum_pair)
    arrivals.append((last[6], down_over, fetch(8, wholes[6], down.at[pl.ds(3 * width, width)])))
    phase(last[5], 2.0, sum_plane)
    phase(last[5], 3.0, sum_line)
    phase(last[6], 4.0, after_conv)
    conv_over = len(phases)
    phase(last[6], 1.0, after_conv_norm)
    up_loads(late, 7, 11, lift_over)
    for n, t in enumerate(late):
        phase(t, 3.2, call(ready, 11 + n), call(up_half, r.hid4, n, len(late)))
    phase(last[7], 0.1, late_done)
    down_loads(8, r.late_sem, conv_over)
    ends = [t for t in range(total) if items[t][0] == 8]
    for t in ends:
        phase(t, 2.0, call(down_part, t, 8, r.late_sem, r.xa if t == ends[0] else r.xb, r.xb))
    phase(total - 1, 4.0, before_final, final)
    over = 0

    def take_arrivals():
        kept = []
        for t, after, work in arrivals:
            if t <= done and after <= over:
                work()
            else:
                kept.append((t, after, work))
        arrivals[:] = kept

    for t in range(min(LEAD, total)):
        plane_send(t, 0)
    done = -1
    for tick in range(total + steps + 3):
        finished = gather_tick(tick)
        done = max(done, -1 if finished is None else finished)
        take_arrivals()
        budget = BUDGET
        while phases and phases[0][0] <= done and (budget > 0 or done == total - 1):
            _, cost, work = phases.pop(0)
            budget -= cost
            for step in work:
                step()
            over += 1
            take_arrivals()
    for index in range(len(saved) - 1):
        if index not in stored:
            stored_wait(index)
    for w in range(many):
        own_copies[w].wait_send()
    for t in range(total):
        for kind in range(kinds):
            wait(send, t, kind)


def forward(count, depth, heads, frames, cotangent, lengths, shards, small, table, collective_id=1):
    shapes = [s.shape for s in shards]
    items = gather_items(shapes)
    steps, many = len(bits_of(count)), len(shards)
    span, width = frames.shape
    inner = shapes[0][1]
    any_, vmem, smem = (pl.BlockSpec(memory_space=s) for s in (pl.ANY, pltpu.VMEM, pltpu.SMEM))
    bf, fl = jnp.bfloat16, jnp.float32
    S, dma = jax.ShapeDtypeStruct, pltpu.SemaphoreType.DMA
    V = lambda shape, dtype=bf: pltpu.VMEM(shape, dtype)
    ins = dict(length=(lengths, smem), frames=(frames, vmem), cotangent=(cotangent, vmem), table=(table, any_), small=(small, vmem))
    flat, flat32, tall = S((span, width), bf), S((span, width), fl), S((span, inner), bf)
    saved = dict(hidden1=flat, inner1=tall, active1=tall, x1=flat32, hidden2=flat, content=flat, offset=flat, keys=flat, values=flat,
                 offsets=S(table.shape, bf), mixed=flat, x2=flat32, hidden3=flat, lifted=S((span, 2 * width), bf), convolved=flat32,
                 swished=flat, x3=flat32, hidden4=flat, inner4=tall, active4=tall, grad4=flat32, branch4=flat,
                 probs=S((heads, span, span), bf))
    outs = dict(small_out=S((small.shape[0], width), fl), stats=S((8, width), fl), edge_grads=S((8, width), fl), output=flat)
    vec, pair, plane, line, sum_send, sum_recv = sum_scratch(count, depth, width)
    flat_vm, flat32_vm, gather_sems = V((span, width)), V((span, width), fl), dma((len(items), 2 * steps + 3))
    scratch = dict(
        send=gather_sems, recv=gather_sems, own_send=dma((many,)), own_recv=dma((many,)),
        small_send=dma((count,)), small_recv=dma((count,)), load_sem=dma((16,)), store_sem=dma((len(saved),)), probs_sem=dma((2,)),
        early_sem=dma((8, 2 * count)), late_sem=dma((8, 2 * count)),
        small_held=V((small.shape[0], width)), small_all=V((small.shape[0], width), fl),
        up_vm=V((width, inner)), down_vm=V((inner, width)), xa=flat32_vm, xb=flat32_vm,
        hid1=flat_vm, hid2=flat_vm, hid3=flat_vm, hid4=flat_vm, inner_vm=V((span, inner)), active_vm=V((span, inner)),
        content_vm=flat_vm, offset_vm=flat_vm, keys_vm=flat_vm, values_vm=flat_vm, table_vm=V(table.shape), offsets_vm=V(table.shape),
        probs_vm=V((2, span, span)), mixed_vm=flat_vm, lifted_vm=V((span, 2 * width)), conv_vm=flat32_vm, swished_vm=flat_vm,
        branch_vm=flat_vm, padded=V((span + 16, 256), fl),
        vec=vec, pair=pair, plane=plane, line=line, sum_send=sum_send, sum_recv=sum_recv)
    whole = [S((rows * count, cols), bf) for rows, cols in shapes]
    values = pl.pallas_call(
        functools.partial(forward_kernel, count, depth, heads, shapes, items, list(saved), list(ins), list(outs), list(scratch)),
        out_shape=whole + list(saved.values()) + list(outs.values()),
        in_specs=[b for _, b in ins.values()] + [any_] * many,
        out_specs=[any_] * (many + len(saved)) + [vmem] * len(outs),
        scratch_shapes=list(scratch.values()),
        compiler_params=pltpu.CompilerParams(collective_id=collective_id, has_side_effects=True, vmem_limit_bytes=63 * 2**20),
        name="forward",
    )(*[v for v, _ in ins.values()], *shards)
    return values[:many], types.SimpleNamespace(**dict(zip(list(saved) + list(outs), values[many:])))


COLS = 256
SLICE = 512


def backward_kernel(count, depth, heads, shapes, in_names, out_names, scratch_names, *refs):
    edges = np.cumsum([0, len(in_names), len(out_names), len(scratch_names)])
    groups = [refs[i:j] for i, j in zip(edges[:-1], edges[1:])]
    r = types.SimpleNamespace(**dict(zip(in_names, groups[0])), **dict(zip(out_names, groups[1])), **dict(zip(scratch_names, groups[2])))
    many, unit = len(shapes), unit_cols(count)
    lefts = [r.active4, r.hidden4, r.swished, r.hidden3, r.mixed, r.table, r.hidden2, r.active1, r.hidden1]
    rights = [r.branch4, r.inner_grad4, r.out_grad3, r.lifted_grad, r.out_grad2, r.offsets_grad, r.joint_grad, r.branch1, r.inner_grad1]
    bits = bits_of(count)
    steps, half = len(bits), depth // 2
    dp, me = lax.axis_index("dp"), lax.axis_index("fsdp")
    core, place = lax.rem(dp, 2), dp // 2
    mate = flip(dp, 1)
    low = place < half
    level = jnp.minimum(place, depth - 1 - place)
    inward = jnp.where(low, dp + 2, dp - 2)
    outward = jnp.where(low, dp - 2, dp + 2)
    span, width = r.grad4.shape
    inner_width = r.inner4.shape[1]
    size = width // heads
    scale = size ** -0.5

    def remote(src, dst, send, recv, device):
        return pltpu.make_async_remote_copy(
            src_ref=src, dst_ref=dst, send_sem=send, recv_sem=recv, device_id=device, device_id_type=MESH)

    def loading(src, dst, index):
        return pltpu.make_async_copy(src, dst, r.load_sem.at[index])

    def storing(src, dst, index):
        return pltpu.make_async_copy(src, dst, r.store_sem.at[index])

    units = [(rows // count // UR) * (cols // 2 // unit) for rows, cols, _ in shapes]
    bases = [int(b) for b in np.cumsum([0] + units)]
    whole = bases[-1]

    def unit_copies(w, i, slot):
        rows, cols, deep = shapes[w]
        rows, chunks = rows // count, cols // 2 // unit
        row, col = i // chunks, lax.rem(i, chunks)
        copies = []
        for m in range(count):
            src = lefts[w].at[:, pl.ds(pl.multiple_of(flips(me, m) * rows + row * UR, UR), UR)]
            copies.append(pltpu.make_async_copy(src, r.a_st.at[slot, pl.ds(0, deep), pl.ds(m * UR, UR)], r.st_sem.at[slot, m]))
        for n, owner in enumerate((1 - core, core)):
            src = rights[w].at[:, pl.ds(pl.multiple_of(owner * (cols // 2) + col * unit, unit), unit)]
            copies.append(pltpu.make_async_copy(src, r.b_st.at[slot, n, pl.ds(0, deep)], r.st_sem.at[slot, count + n]))
        return copies

    def fetch_unit(u):
        for w in range(many):
            @pl.when(jnp.logical_and(u >= bases[w], u < bases[w + 1]))
            def _(w=w):
                for copy in unit_copies(w, u - bases[w], lax.rem(u, 2)):
                    copy.start()

    def c_copy(u):
        s = lax.rem(u, CRING)
        return remote(r.snd_c.at[s], r.rcv_c.at[s], r.c_send.at[s], r.c_recv.at[s], (mate, me))

    def d_copy(j, piece, u):
        s = lax.rem(u, RING)
        order = bits if piece == 0 else bits[::-1]
        return remote(d_snd[j].at[s, piece], d_rcv[j].at[s, piece],
                      r.d_send.at[j, piece, s], r.d_recv.at[j, piece, s], (dp, flip(me, order[j])))

    d_snd = [r.d_snd0, r.d_snd1, r.d_snd2][:steps]
    d_rcv = [r.d_rcv0, r.d_rcv1, r.d_rcv2][:steps]

    def zi_copy(u):
        s = lax.rem(u, ZRING)
        return remote(r.z_snd.at[s], r.z_acc.at[s], r.zi_send.at[s], r.za_recv.at[s], (inward, me))

    def zm_copy(u):
        s = lax.rem(u, ZRING)
        return remote(r.z_snd.at[s], r.z_mid.at[s], r.zi_send.at[s], r.zm_recv.at[s], (inward, me))

    def loc_copy(u):
        s = lax.rem(u, ZRING)
        return pltpu.make_async_copy(r.total.at[s], r.packed.at[core, u], r.loc_sem.at[s])

    def mt_copy(u, src):
        s = lax.rem(u, ORING)
        return remote(src, r.packed.at[core, u], r.mt_send.at[s], r.mt_recv.at[s], (mate, me))

    def zo_copy(u, src):
        s = lax.rem(u, ORING)
        return remote(src, r.packed.at[core, u], r.zo_send.at[s], r.zo_recv.at[s], (outward, me))

    def first(u):
        slot, s = lax.rem(u, 2), lax.rem(u, CRING)
        depths = sorted(set(deep for *_, deep in shapes))
        for deep in depths:
            ws = [w for w in range(many) if shapes[w][2] == deep]
            cond = functools.reduce(jnp.logical_or, [jnp.logical_and(u >= bases[w], u < bases[w + 1]) for w in ws])

            @pl.when(cond)
            def _(deep=deep, w=ws[0]):
                for copy in unit_copies(w, 0, slot):
                    copy.wait()
                left = r.a_st[slot, 0:deep]
                r.snd_c[s] = outer(left, r.b_st[slot, 0, 0:deep]).astype(jnp.bfloat16).reshape(count, UR, unit)
                c_copy(u).start()
                r.own[lax.rem(u, RING)] = outer(left, r.b_st[slot, 1, 0:deep]).reshape(count, UR, unit)

    def rows_of(piece):
        return slice(piece * (UR // 2), (piece + 1) * (UR // 2))

    def second(u):
        c_copy(u).wait()
        s, c = lax.rem(u, RING), lax.rem(u, CRING)
        for piece in range(2):
            order = bits if piece == 0 else bits[::-1]
            rs = rows_of(piece)
            for k, m in enumerate(span_of(order[1:])):
                x = m + order[0]
                d_snd[0][s, piece, k] = (r.own[s, x, rs] + r.rcv_c[c, x, rs].astype(jnp.float32)).astype(jnp.bfloat16)
            d_copy(0, piece, u).start()
        for piece in range(2):
            order = bits if piece == 0 else bits[::-1]
            rs = rows_of(piece)
            for m in span_of(order[1:]):
                r.own[s, m, rs] = r.own[s, m, rs] + r.rcv_c[c, m, rs].astype(jnp.float32)

    def onward(j, u):
        s = lax.rem(u, RING)
        for piece in range(2):
            d_copy(j - 1, piece, u).wait()
            order = bits if piece == 0 else bits[::-1]
            rs = rows_of(piece)
            spans, keep = span_of(order[j:]), span_of(order[j + 1 :])
            for k, m in enumerate(spans):
                if m not in keep:
                    d_snd[j][s, piece, keep.index(m - order[j])] = (
                        r.own[s, m, rs] + d_rcv[j - 1][s, piece, k].astype(jnp.float32)).astype(jnp.bfloat16)
            d_copy(j, piece, u).start()
            for k, m in enumerate(spans):
                if m in keep:
                    r.own[s, m, rs] = r.own[s, m, rs] + d_rcv[j - 1][s, piece, k].astype(jnp.float32)

    def plane_done(u):
        s, z = lax.rem(u, RING), lax.rem(u, ZRING)
        for piece in range(2):
            d_copy(steps - 1, piece, u).wait()
            rs = rows_of(piece)
            r.zsum[z, rs] = r.own[s, 0, rs] + d_rcv[steps - 1][s, piece, 0].astype(jnp.float32)

        @pl.when(level == 0)
        def _():
            r.z_snd[z] = r.zsum[z].astype(jnp.bfloat16)
            if half == 1:
                zm_copy(u).start()
            else:
                zi_copy(u).start()

    def climb(j, u):
        z = lax.rem(u, ZRING)

        @pl.when(level == j - 1)
        def _():
            zi_copy(u).wait_send()

        @pl.when(level == j)
        def _():
            zi_copy(u).wait_recv()
            r.z_snd[z] = (r.zsum[z] + r.z_acc[z].astype(jnp.float32)).astype(jnp.bfloat16)
            if j == half - 1:
                zm_copy(u).start()
            else:
                zi_copy(u).start()

    def middle(u):
        z = lax.rem(u, ZRING)

        @pl.when(level == half - 1)
        def _():
            zm_copy(u).wait()
            r.total[z] = (r.z_snd[z].astype(jnp.float32) + r.z_mid[z].astype(jnp.float32)).astype(jnp.bfloat16)
            if half > 1:
                zo_copy(u, r.total.at[z]).start()
            mt_copy(u, r.total.at[z]).start()
            loc_copy(u).start()

    def descend(j, u):
        z = lax.rem(u, ZRING)

        @pl.when(level == half - j)
        def _():
            src = r.total.at[z] if j == 1 else r.packed.at[core, u]
            zo_copy(u, src).wait_send()

        @pl.when(level == half - 1 - j)
        def _():
            zo_copy(u, r.packed.at[core, u]).wait_recv()
            if j < half - 1:
                zo_copy(u, r.packed.at[core, u]).start()
            mt_copy(u, r.packed.at[core, u]).start()

    def finish(u):
        z = lax.rem(u, ZRING)

        @pl.when(level == half - 1)
        def _():
            loc_copy(u).wait()
        mt_copy(u, r.total.at[z]).wait()

    stages = [(1, second)]
    at = 1
    for j in range(1, steps):
        at += LAG
        stages.append((at, functools.partial(onward, j)))
    at += LAG
    stages.append((at, plane_done))
    for j in range(1, half):
        at += LAG
        stages.append((at, functools.partial(climb, j)))
    at += LAG
    stages.append((at, middle))
    for j in range(1, half):
        at += LAG
        stages.append((at, functools.partial(descend, j)))
    at += LAG
    stages.append((at, finish))

    slices = inner_width // SLICE

    def slice_streams(i, up, inner):
        slot, cols = lax.rem(i, 2), pl.ds(pl.multiple_of(i * SLICE, SLICE), SLICE)
        return (pltpu.make_async_copy(up.at[:, cols], r.up_st.at[slot], r.up_sem.at[slot]),
                pltpu.make_async_copy(inner.at[:, cols], r.in_st.at[slot], r.in_sem.at[slot]))

    def slice_store(i, dst):
        slot, cols = lax.rem(i, 2), pl.ds(pl.multiple_of(i * SLICE, SLICE), SLICE)
        return pltpu.make_async_copy(r.ig_st.at[slot], dst.at[:, cols], r.ig_sem.at[slot])

    def slices_begin(down, up, inner):
        for i in range(slices):
            rows = pl.ds(i * SLICE, SLICE)
            pltpu.make_async_copy(down.at[rows], r.w_vm.at[rows], r.w_sem.at[i]).start()
        for i in range(2):
            for copy in slice_streams(i, up, inner):
                copy.start()

    def slice_work(i, late):
        slot = lax.rem(i, 2)
        rows = pl.ds(pl.multiple_of(i * SLICE, SLICE), SLICE)
        pltpu.make_async_copy(r.late_down.at[rows], r.w_vm.at[rows], r.w_sem.at[i]).wait()
        for copy in slice_streams(i, r.late_up, r.inner4):
            copy.wait()

        @pl.when(i >= 2)
        def _():
            slice_store(i, r.inner_grad4).wait()

        @pl.loop(0, SLICE // COLS)
        def _(c):
            part = pl.ds(pl.multiple_of(c * COLS, COLS), COLS)
            active_grad = dot_nt(r.og[...], r.w_vm[pl.ds(pl.multiple_of(i * SLICE + c * COLS, COLS), COLS)])
            inner = r.in_st[slot, :, part].astype(jnp.float32)
            gate = sigmoid(inner)
            r.ig_st[slot, :, part] = (active_grad * (gate * (1.0 + inner * (1.0 - gate)))).astype(jnp.bfloat16)

        @pl.when(late)
        def _():
            slice_store(i, r.inner_grad4).start()

        @pl.when(jnp.logical_not(late))
        def _():
            slice_store(i, r.inner_grad1).start()

        @pl.loop(0, width // COLS)
        def _(c):
            part = pl.ds(pl.multiple_of(c * COLS, COLS), COLS)
            r.acc[:, part] += dot_nt(r.ig_st[slot], r.up_st[slot, part])

        @pl.when(jnp.logical_and(late, i < slices - 2))
        def _():
            for copy in slice_streams(i + 2, r.late_up, r.inner4):
                copy.start()

        @pl.when(jnp.logical_and(jnp.logical_not(late), i < slices - 2))
        def _():
            for copy in slice_streams(i + 2, r.early_up, r.inner1):
                copy.start()

    def slices_over(dst):
        for i in range(2):
            slice_store(i, dst).wait()

    def norm_back(n, factor):
        gain = r.small_all[pl.ds(n, 1)]
        r.sums[...] = jnp.zeros_like(r.sums)

        @pl.loop(0, span // 64)
        def _(i):
            rows = pl.ds(pl.multiple_of(i * 64, 64), 64)
            v, grad = r.x[rows], r.acc[rows]
            center = v - jnp.mean(v, axis=-1, keepdims=True)
            rate = lax.rsqrt(jnp.mean(center * center, axis=-1, keepdims=True) + EPS)
            normal = center * rate
            r.sums[0:1] += jnp.sum(grad * normal, axis=0, keepdims=True)
            r.sums[1:2] += jnp.sum(grad, axis=0, keepdims=True)
            inner = grad * gain
            back = r.grad[rows] + rate * (inner - jnp.mean(inner, axis=-1, keepdims=True)
                                          - normal * jnp.mean(inner * normal, axis=-1, keepdims=True))
            r.grad[rows] = back
            r.og[rows] = (factor * back).astype(jnp.bfloat16)
        r.small_buf[pl.ds(n, 1)] = r.sums[0:1]
        r.small_buf[pl.ds(n + 6, 1)] = r.sums[1:2]

    def valid_mask():
        return jnp.where(lax.broadcasted_iota(jnp.int32, (span, 1), 0) < r.length[0], 1.0, 0.0)

    taps = 5
    reach = taps // 2

    def conv_first(j):
        cols = pl.ds(pl.multiple_of(j * COLS, COLS), COLS)
        mask = valid_mask()
        swish_grad = dot_nt(r.og[...], r.w_vm[cols])
        normal = (r.x[:, cols] - r.stats[0:1, cols]) * r.stats[1:2, cols]
        scaled = normal * r.small_all[5:6, cols] + r.small_all[11:12, cols]
        gate = sigmoid(scaled)
        scaled_grad = swish_grad * (gate * (1.0 + scaled * (1.0 - gate)))
        r.acc[:, cols] = scaled_grad
        masked = scaled_grad * mask
        r.vec[0:1, cols] = jnp.sum(masked, axis=0, keepdims=True)
        r.vec[1:2, cols] = jnp.sum(masked * normal, axis=0, keepdims=True)

    def conv_second(j):
        cols = pl.ds(pl.multiple_of(j * COLS, COLS), COLS)
        gates = pl.ds(pl.multiple_of(j * COLS + width, COLS), COLS)
        mask = valid_mask()
        normal = (r.x[:, cols] - r.stats[0:1, cols]) * r.stats[1:2, cols]
        inner = mask * ((r.vec[0:1, cols] + normal * r.vec[1:2, cols]) / r.stats[2:3, cols])
        conv_grad = r.stats[1:2, cols] * r.small_all[5:6, cols] * (r.acc[:, cols] - inner)
        r.padded[8 : 8 + span] = conv_grad
        up, gate = r.lifted_vm[:, cols].astype(jnp.float32), sigmoid(r.lifted_vm[:, gates].astype(jnp.float32))
        r.gated[8 : 8 + span] = up * gate * mask
        total = jnp.zeros((span, COLS), jnp.float32)
        for tap in range(taps):
            total = total + r.small_all[14 + tap : 15 + tap, cols] * r.padded[8 - tap + reach : 8 - tap + reach + span]
            moved = r.gated[8 + tap - reach : 8 + tap - reach + span]
            r.small_buf[14 + tap : 15 + tap, cols] = jnp.sum(moved * conv_grad, axis=0, keepdims=True)
        total = total * mask
        r.lg_vm[:, cols] = (total * gate).astype(jnp.bfloat16)
        r.lg_vm[:, gates] = (total * up * gate * (1.0 - gate)).astype(jnp.bfloat16)

    pair_copy = remote(r.vec, r.pair, r.sum_send.at[0], r.sum_recv.at[0], (mate, me))
    plane_copies = [remote(r.plane.at[me], r.plane.at[me], r.sum_send.at[m], r.sum_recv.at[m], (dp, flips(me, m)))
                    for m in range(1, count)]
    line_to = [(lax.rem(dp + 2 * j, 2 * depth), me) for j in range(1, depth)]
    line_copies = [remote(r.line.at[place], r.line.at[place], r.sum_send.at[count + j], r.sum_recv.at[count + j], line_to[j])
                   for j in range(depth - 1)]

    def sum_plane():
        pair_copy.wait()
        r.plane[me] = r.vec[...] + r.pair[...]
        for copy in plane_copies:
            copy.start()

    def sum_line():
        for copy in plane_copies:
            copy.wait()
        r.line[place] = functools.reduce(jnp.add, [r.plane[f] for f in range(count)])
        for copy in line_copies:
            copy.start()

    def sum_over():
        for copy in line_copies:
            copy.wait()
        r.vec[...] = functools.reduce(jnp.add, [r.line[z] for z in range(depth)])

    def head_copies(h):
        slot, cols = lax.rem(h, 2), pl.ds(pl.multiple_of(h * size, size), size)
        copies = [pltpu.make_async_copy(src.at[:, cols], r.head_st.at[slot, n], r.head_sem.at[slot, n])
                  for n, src in enumerate((r.content, r.offset, r.keys, r.values))]
        copies.append(pltpu.make_async_copy(r.offsets.at[:, cols], r.place_st.at[slot], r.head_sem.at[slot, 4]))
        copies.append(pltpu.make_async_copy(r.probs.at[h], r.probs_st.at[slot], r.head_sem.at[slot, 5]))
        return copies

    def offsets_store(h):
        slot, cols = lax.rem(h, 2), pl.ds(pl.multiple_of(h * size, size), size)
        return pltpu.make_async_copy(r.turned_st.at[slot], r.offsets_grad.at[:, cols], r.turned_sem.at[slot])

    def attend_back(h):
        slot, cols = lax.rem(h, 2), pl.ds(pl.multiple_of(h * size, size), size)
        for copy in head_copies(h):
            copy.wait()

        @pl.when(h >= 2)
        def _():
            offsets_store(h).wait()
        content, offset, key, value = (r.head_st[slot, n] for n in range(4))
        mixed_grad, p = r.mg_vm[:, cols], r.probs_st[slot]
        key_cols = pl.ds(pl.multiple_of(h * size + width, size), size)
        value_cols = pl.ds(pl.multiple_of(h * size + 2 * width, size), size)
        prob_grad = dot_nt(mixed_grad, value)
        r.joint_vm[:, value_cols] = dot_tn(p, mixed_grad).astype(jnp.bfloat16)
        weights = p.astype(jnp.float32)
        product = weights * prob_grad
        score_grad = product - weights * jnp.sum(product, axis=1, keepdims=True)
        raw_grad = (score_grad * scale).astype(jnp.bfloat16)
        content_grad = dot_nn(raw_grad, key)
        r.joint_vm[:, key_cols] = dot_tn(raw_grad, content).astype(jnp.bfloat16)
        turn = r.turn[...]
        turned = dot_nn(turn, raw_grad)
        wide = jnp.concatenate([turned, jnp.zeros_like(turned)], axis=1)
        placed = pltpu.roll(wide, 0, 1, stride=1, stride_axis=0).astype(jnp.bfloat16)
        turned_offset = dot_nn(turn, offset).astype(jnp.bfloat16)
        r.turned_st[slot] = dot_tn(placed, turned_offset).astype(jnp.bfloat16)
        offsets_store(h).start()
        turned_grad = dot_nn(placed, r.place_st[slot])
        high = turned_grad.astype(jnp.bfloat16)
        small = (turned_grad - high.astype(jnp.float32)).astype(jnp.bfloat16)
        offset_grad = dot_nn(turn, high) + dot_nn(turn, small)
        r.joint_vm[:, cols] = (content_grad + offset_grad).astype(jnp.bfloat16)
        r.small_buf[12:13, cols] = jnp.sum(content_grad, axis=0, keepdims=True)
        r.small_buf[13:14, cols] = jnp.sum(turned_grad, axis=0, keepdims=True)

        @pl.when(h < heads - 2)
        def _():
            for copy in head_copies(h + 2):
                copy.start()

    narrow = r.small_out.shape[1]

    def columns(f):
        return pl.ds(pl.multiple_of(f * narrow, 128), narrow)

    small_pair = remote(r.small_buf, r.s_pair, r.s_send.at[0], r.s_recv.at[0], (mate, me))
    small_plane = [remote(r.s_both.at[:, columns(flips(me, m))], r.s_plane.at[me], r.s_send.at[m], r.s_recv.at[m], (dp, flips(me, m)))
                   for m in range(1, count)]
    small_line = [remote(r.s_line.at[place], r.s_line.at[place], r.s_send.at[count + j], r.s_recv.at[count + j], line_to[j])
                  for j in range(depth - 1)]

    def small_second():
        small_pair.wait()
        r.s_both[...] = r.small_buf[...] + r.s_pair[...]
        for copy in small_plane:
            copy.start()
        r.s_plane[me] = r.s_both[:, columns(me)]

    def small_third():
        for copy in small_plane:
            copy.wait()
        r.s_line[place] = functools.reduce(jnp.add, [r.s_plane[f] for f in range(count)])
        for copy in small_line:
            copy.start()

    def small_last():
        for copy in small_line:
            copy.wait()
        r.small_out[...] = functools.reduce(jnp.add, [r.s_line[z] for z in range(depth)])

    def block(n):
        return r.w_vm.at[pl.ds(n * width, width)]

    conv_loads = [loading(r.convolved, r.x, 2), loading(r.lifted, r.lifted_vm, 3), loading(r.pointwise_down, block(0), 4),
                  loading(r.pointwise_up.at[:, pl.ds(0, width)], block(1), 5),
                  loading(r.pointwise_up.at[:, pl.ds(width, width)], block(2), 6), loading(r.heads_out, block(3), 7)]
    query_loads = [loading(r.heads_in.at[:, pl.ds(n * width, width)], block(n), 9 + n) for n in range(3)]
    state_load, older_load = loading(r.x2, r.x, 8), loading(r.x1, r.x, 12)
    grad3_store, lifted_store = storing(r.og, r.out_grad3, 0), storing(r.lg_vm, r.lifted_grad, 1)
    grad2_store, joint_store = storing(r.og, r.out_grad2, 2), storing(r.joint_vm, r.joint_grad, 3)
    branch_store, frames_store = storing(r.og, r.branch1, 4), storing(r.grad, r.frames_grad, 5)

    def hidden_cols(first_col, last_col, parts):
        @pl.loop(first_col, last_col)
        def _(c):
            cols = pl.ds(pl.multiple_of(c * COLS, COLS), COLS)
            r.acc[:, cols] = functools.reduce(jnp.add, [
                dot_nt(src[:, a * width : (a + 1) * width], r.w_vm[pl.ds(pl.multiple_of(b * width + c * COLS, COLS), COLS)])
                for src, a, b in parts])

    def chain(tick):
        def when(*ticks):
            cond = functools.reduce(jnp.logical_or, [tick == t for t in ticks])
            return pl.when(cond)

        late = tick < 4

        @pl.when(jnp.logical_or(late, jnp.logical_and(tick >= 24, tick < 28)))
        def _():
            begin = 2 * jnp.where(late, tick, tick - 24)

            @pl.loop(0, 2)
            def _(k):
                slice_work(begin + k, late)

        @when(4)
        def _():
            slices_over(r.inner_grad4)
            for copy in conv_loads[2:]:
                copy.start()

        @when(31)
        def _():
            r.x[...] = r.frames[...].astype(jnp.float32)
            slices_over(r.inner_grad1)

        @when(4, 12, 23, 32)
        def _():
            n = jnp.where(tick == 4, 3, jnp.where(tick == 12, 2, jnp.where(tick == 23, 1, 0)))
            norm_back(n, jnp.where(tick == 23, 0.5, 1.0))

        @when(4)
        def _():
            grad3_store.start()
            conv_loads[0].start()
            conv_loads[1].start()

        @when(5)
        def _():
            for copy in conv_loads[:3]:
                copy.wait()

        @when(5, 6)
        def _():
            @pl.loop(0, 2)
            def _(k):
                conv_first(2 * (tick - 5) + k)

        @when(6)
        def _():
            r.small_buf[5:6] = r.vec[1:2]
            r.small_buf[11:12] = r.vec[0:1]
            pair_copy.start()

        when(7)(sum_plane)
        when(8)(sum_line)

        @when(9)
        def _():
            sum_over()

        @when(9, 10)
        def _():
            @pl.loop(0, 2)
            def _(k):
                conv_second(2 * (tick - 9) + k)

        @when(10)
        def _():
            lifted_store.start()
            state_load.start()
            grad3_store.wait()

        @when(11)
        def _():
            conv_loads[3].wait()
            conv_loads[4].wait()
            hidden_cols(0, width // COLS, [(r.lg_vm, 0, 1), (r.lg_vm, 1, 2)])
            state_load.wait()
            for h in range(2):
                for copy in head_copies(h):
                    copy.start()

        @when(12)
        def _():
            lifted_store.wait()
            grad2_store.start()
            older_load.start()
            conv_loads[5].wait()

            @pl.loop(0, width // COLS)
            def _(c):
                cols = pl.ds(pl.multiple_of(c * COLS, COLS), COLS)
                r.mg_vm[:, cols] = dot_nt(r.og[...], r.w_vm[pl.ds(pl.multiple_of(3 * width + c * COLS, COLS), COLS)]).astype(jnp.bfloat16)

        @when(13)
        def _():
            for copy in query_loads:
                copy.start()

        @pl.when(jnp.logical_and(tick >= 13, tick < 13 + heads))
        def _():
            attend_back(tick - 13)

        @when(13 + heads - 1)
        def _():
            joint_store.start()

        when(19)(grad2_store.wait)
        when(29)(branch_store.wait)
        joint_parts = [(r.joint_vm, n, n) for n in range(3)]

        @when(21)
        def _():
            for h in range(2):
                offsets_store(h).wait()
            for copy in query_loads:
                copy.wait()
            older_load.wait()

        @when(21, 22)
        def _():
            begin = (width // COLS // 2) * (tick - 21)
            hidden_cols(begin, begin + width // COLS // 2, joint_parts)

        @when(23)
        def _():
            joint_store.wait()
            branch_store.start()
            r.acc[...] = jnp.zeros_like(r.acc)
            slices_begin(r.early_down, r.early_up, r.inner1)

        @when(32)
        def _():
            frames_store.start()
            small_pair.start()

        when(34)(small_second)
        when(36)(small_third)

        @when(38)
        def _():
            small_last()
            frames_store.wait()

    barrier = pltpu.get_barrier_semaphore()
    pl.semaphore_signal(barrier, inc=1, device_id=(mate, me), device_id_type=MESH)
    for mask in range(1, count):
        pl.semaphore_signal(barrier, inc=1, device_id=(dp, flips(me, mask)), device_id_type=MESH)
    for device in line_to:
        pl.semaphore_signal(barrier, inc=1, device_id=device, device_id_type=MESH)
    starts = [loading(r.grad4, r.grad, 0), loading(r.x3, r.x, 1), loading(r.branch4, r.og, 13)]
    for copy in starts:
        copy.start()
    fetch_unit(jnp.int32(0))
    slices_begin(r.late_down, r.late_up, r.inner4)
    r.acc[...] = jnp.zeros_like(r.acc)
    r.small_buf[...] = jnp.zeros_like(r.small_buf)
    r.small_buf[4:5] = r.edge_grads[0:1]
    r.small_buf[10:11] = r.edge_grads[1:2]
    r.vec[...] = jnp.zeros_like(r.vec)
    for ref in (r.padded, r.gated):
        ref[0:8] = jnp.zeros((8, COLS), jnp.float32)
        ref[8 + span : 16 + span] = jnp.zeros((8, COLS), jnp.float32)
    row = lax.broadcasted_iota(jnp.int32, (span, span), 0)
    column = lax.broadcasted_iota(jnp.int32, (span, span), 1)
    r.turn[...] = jnp.where(row + column == span - 1, 1.0, 0.0).astype(jnp.bfloat16)
    pl.semaphore_wait(barrier, 1 + count - 1 + depth - 1)
    for copy in starts:
        copy.wait()

    @pl.loop(0, whole + at + 1)
    def _(tick):
        @pl.when(tick + 1 < whole)
        def _():
            fetch_unit(tick + 1)

        @pl.when(tick < whole)
        def _():
            first(tick)
        for lag, stage in stages:
            pl.when(jnp.logical_and(tick >= lag, tick - lag < whole))(functools.partial(stage, tick - lag))
        chain(tick)


def backward(count, depth, heads, frames, lengths, wholes, f, table, collective_id=2):
    early_up, early_down, heads_in, _, heads_out, pointwise_up, pointwise_down, late_up, late_down = wholes
    any_, vmem, smem = (pl.BlockSpec(memory_space=s) for s in (pl.ANY, pltpu.VMEM, pltpu.SMEM))
    bf, fl = jnp.bfloat16, jnp.float32
    S, dma = jax.ShapeDtypeStruct, pltpu.SemaphoreType.DMA
    V = lambda shape, dtype=bf: pltpu.VMEM(shape, dtype)
    span, width = frames.shape
    inner = early_up.shape[1]
    size, unit = width // heads, unit_cols(count)
    far = dict(
        table=table, early_up=early_up, early_down=early_down, heads_in=heads_in, heads_out=heads_out, pointwise_up=pointwise_up,
        pointwise_down=pointwise_down, late_up=late_up, late_down=late_down, active4=f.active4, branch4=f.branch4, inner4=f.inner4,
        hidden4=f.hidden4, grad4=f.grad4, x3=f.x3, convolved=f.convolved, lifted=f.lifted, swished=f.swished, hidden3=f.hidden3,
        x2=f.x2, mixed=f.mixed, content=f.content, offset=f.offset, keys=f.keys, values=f.values, probs=f.probs, offsets=f.offsets,
        hidden2=f.hidden2, x1=f.x1, active1=f.active1, inner1=f.inner1, hidden1=f.hidden1)
    near = dict(frames=frames, small_all=f.small_out, stats=f.stats, edge_grads=f.edge_grads)
    shapes = [(inner, width, span), (width, inner, span), (width, width, span), (width, 2 * width, span), (width, width, span),
              (width, width, table.shape[0]), (width, 3 * width, span), (inner, width, span), (width, inner, span)]
    units = sum((rows // count // UR) * (cols // 2 // unit) for rows, cols, _ in shapes)
    rows = f.small_out.shape[0]
    flat, tall = S((span, width), bf), S((span, inner), bf)
    far_outs = dict(packed=S((2, units, UR, unit), bf), frames_grad=S((span, width), fl), inner_grad4=tall, out_grad3=flat,
                    lifted_grad=S((span, 2 * width), bf), out_grad2=flat, offsets_grad=S(table.shape, bf),
                    joint_grad=S((span, 3 * width), bf), branch1=flat, inner_grad1=tall)
    near_outs = dict(small_out=S((rows, width // count), fl))
    vec, pair, plane, line, _, _ = sum_scratch(count, depth, width)
    bits = bits_of(count)
    deepest = max(deep for *_, deep in shapes)
    block_ring = V((CRING, count, UR, unit))
    z_ring = V((ZRING, UR, unit))
    scratch = dict(
        a_st=V((2, deepest, count * UR)), b_st=V((2, 2, deepest, unit)), st_sem=dma((2, count + 2)),
        own=V((RING, count, UR, unit), fl), snd_c=block_ring, rcv_c=block_ring,
        zsum=V((ZRING, UR, unit), fl), z_snd=z_ring, z_acc=z_ring, z_mid=z_ring, total=z_ring,
        c_send=dma((CRING,)), c_recv=dma((CRING,)), zi_send=dma((ZRING,)), za_recv=dma((ZRING,)), zm_recv=dma((ZRING,)),
        loc_sem=dma((ZRING,)), mt_send=dma((ORING,)), mt_recv=dma((ORING,)), zo_send=dma((ORING,)), zo_recv=dma((ORING,)),
        d_send=dma((len(bits), 2, RING)), d_recv=dma((len(bits), 2, RING)),
        s_pair=V((rows, width), fl), s_both=V((rows, width), fl), s_plane=V((count, rows, width // count), fl),
        s_line=V((depth, rows, width // count), fl), s_send=dma((count + depth,)), s_recv=dma((count + depth,)),
        load_sem=dma((14,)), store_sem=dma((6,)), small_buf=V((rows, width), fl), sums=V((8, width), fl),
        w_vm=V((inner, width)), w_sem=dma((inner // SLICE,)), up_st=V((2, width, SLICE)), up_sem=dma((2,)),
        in_st=V((2, span, SLICE)), in_sem=dma((2,)), ig_st=V((2, span, SLICE)), ig_sem=dma((2,)),
        grad=V((span, width), fl), acc=V((span, width), fl), x=V((span, width), fl), og=V((span, width)),
        lifted_vm=V((span, 2 * width)), lg_vm=V((span, 2 * width)), padded=V((span + 16, COLS), fl), gated=V((span + 16, COLS), fl),
        vec=vec, pair=pair, plane=plane, line=line, sum_send=dma((count + depth,)), sum_recv=dma((count + depth,)),
        head_st=V((2, 4, span, size)), place_st=V((2, table.shape[0], size)), probs_st=V((2, span, span)), head_sem=dma((2, 6)),
        turned_st=V((2, table.shape[0], size)), turned_sem=dma((2,)), joint_vm=V((span, 3 * width)), mg_vm=V((span, width)),
        turn=V((span, span)))
    tiny = V((8, 128))
    rings = [V((RING, 2, count // 2 ** (j + 1), UR // 2, unit)) if j < len(bits) else tiny for j in range(3)]
    scratch.update(d_snd0=rings[0], d_snd1=rings[1], d_snd2=rings[2], d_rcv0=rings[0], d_rcv1=rings[1], d_rcv2=rings[2])
    names = [["length"] + list(near) + list(far), list(far_outs) + list(near_outs), list(scratch)]
    values = pl.pallas_call(
        functools.partial(backward_kernel, count, depth, heads, shapes, *names),
        out_shape=list(far_outs.values()) + list(near_outs.values()),
        in_specs=[smem] + [vmem] * len(near) + [any_] * len(far),
        out_specs=[any_] * len(far_outs) + [vmem] * len(near_outs),
        scratch_shapes=list(scratch.values()),
        compiler_params=pltpu.CompilerParams(collective_id=collective_id, has_side_effects=True, vmem_limit_bytes=63 * 2**20 + 2**19),
        name="backward",
    )(lengths, *near.values(), *far.values())
    return values[0], values[1], values[-1], [s[:2] for s in shapes]


HEADS = 8


def position_table(span, width):
    distance = (span - 1 - np.arange(2 * span - 1)).astype(np.float32)
    rate = np.exp(np.arange(width // 2).astype(np.float32) * np.float32(-2.0 * math.log(10000.0) / width))
    angle = distance[:, None] * rate[None, :]
    table = np.concatenate([np.sin(angle), np.cos(angle)], axis=1)
    return np.concatenate([table, np.zeros((1, width), np.float32)]).astype(jnp.bfloat16)


def body(count, depth, frames, lengths, cotangent, early_up, early_down, heads_in, offset_proj, heads_out,
         pointwise_up, pointwise_down, late_up, late_down, depthwise, norm_gains, norm_shifts, score_bias):
    _, span, width = frames.shape
    taps = depthwise.shape[0]
    table = jnp.asarray(position_table(span, width))
    small = jnp.concatenate([norm_gains, norm_shifts, score_bias, depthwise], axis=0)
    rows = small.shape[0]
    small = jnp.pad(small, ((0, 32 - rows), (0, 0)))
    wholes, f = forward(count, depth, HEADS, frames[0], cotangent[0], lengths,
                [early_up, early_down, heads_in, offset_proj, heads_out, pointwise_up, pointwise_down, late_up, late_down],
                small, table)
    packed, frames_grad, small_sum, shapes = backward(count, depth, HEADS, frames[0], lengths, wholes, f, table)
    (late_down_grad, late_up_grad, pointwise_down_grad, pointwise_up_grad, heads_out_grad, offset_proj_grad, heads_in_grad,
     early_down_grad, early_up_grad) = unpack(packed, count, shapes)
    return (
        f.output[None], frames_grad[None], early_up_grad, early_down_grad, heads_in_grad, offset_proj_grad, heads_out_grad,
        pointwise_up_grad, pointwise_down_grad, late_up_grad, late_down_grad,
        small_sum[14 : 14 + taps], small_sum[0:6], small_sum[6:12], small_sum[12:14],
    )


def solution(mesh):
    item = P(("dp", "fsdp"), None, None)
    rows = P("fsdp", None)
    cols = P(None, "fsdp")
    in_specs = (item, P(("dp", "fsdp")), item) + (rows,) * 9 + (cols,) * 4
    out_specs = (item, item) + (rows,) * 9 + (cols,) * 4
    count, depth = mesh.shape["fsdp"], mesh.shape["dp"] // 2
    return jax.shard_map(functools.partial(body, count, depth), mesh=mesh, in_specs=in_specs, out_specs=out_specs, check_vma=False)
```

```python
import functools
import math
import types

import jax
import jax.numpy as jnp
import numpy as np
from jax import lax
from jax.experimental import pallas as pl
from jax.experimental.pallas import tpu as pltpu
from jax.sharding import PartitionSpec as P

MESH = pl.DeviceIdType.MESH


def flip(index, bit):
    return index + bit - 2 * bit * ((index // bit) % 2)


def bits_of(count):
    bits, bit = [], 1
    while bit < count:
        bits.append(bit)
        bit *= 2
    return bits


def span_of(bits):
    held = [0]
    for bit in bits:
        held = held + [h + bit for h in held]
    return held


def flips(index, mask):
    bit = 1
    while bit <= mask:
        if mask & bit:
            index = flip(index, bit)
        bit *= 2
    return index


def gather_items(shapes):
    items = []
    for w, (rows, cols) in enumerate(shapes):
        half = rows // 2
        row_step, col_step = min(half, 128), min(cols, 1024)
        for row in range(0, half, row_step):
            for col in range(0, cols, col_step):
                tiles = col_step // 128
                side = tiles // 3
                if tiles % 3 == 2 and len(items) % 2:
                    side += 1
                items.append((w, row, row_step, col, side * 128, (tiles - 2 * side) * 128))
    for k in (1, 2):
        w, row, rows, col, edge, middle = items[-k]
        items[-k] = (w, row, rows, col, 0, middle + 2 * edge)
    return items


UR = 128


def unit_cols(count):
    return 2048 // count

LAG = 2
RING = 2 * LAG + 2
ZRING = 6
ORING = 32
CRING = 4


def outer(left, right):
    return lax.dot_general(left, right, (((0,), (0,)), ((), ())), preferred_element_type=jnp.float32)


def unpack_kernel(tiles, cuts, packed, small, *refs):
    many, unit = len(tiles), packed.shape[3]
    outs, pieces = refs[:many], refs[many : many + len(cuts)]
    wide, (held, load, store) = refs[many + len(cuts) : 2 * many + len(cuts)], refs[2 * many + len(cuts) :]
    copies, base = [], 0
    for w, (nr, nc) in enumerate(tiles):
        copy = pltpu.make_async_copy(packed.at[:, pl.ds(base, nr * nc)], held.at[:, pl.ds(base, nr * nc)], load.at[w])
        copy.start()
        copies.append(copy)
        base += nr * nc
    for piece, (start, stop) in zip(pieces, cuts):
        piece[...] = small[start:stop]
    base, stores = 0, []
    for w, (nr, nc) in enumerate(tiles):
        copies[w].wait()
        for core in range(2):
            for col in range(nc):
                @pl.loop(0, nr)
                def _(row, w=w, core=core, col=col, base=base, nc=nc):
                    wide[w][pl.ds(pl.multiple_of(row * UR, UR), UR), (core * nc + col) * unit : (core * nc + col + 1) * unit] = (
                        held[core, base + row * nc + col].astype(jnp.float32))
        copy = pltpu.make_async_copy(wide[w], outs[w], store.at[w])
        copy.start()
        stores.append(copy)
        base += nr * nc
    for copy in stores:
        copy.wait()


def unpack(packed, small, cuts, count, shapes):
    any_, vmem = pl.BlockSpec(memory_space=pl.ANY), pl.BlockSpec(memory_space=pltpu.VMEM)
    out_shape = [jax.ShapeDtypeStruct((r // count, c), jnp.float32) for r, c in shapes]
    pieces = [jax.ShapeDtypeStruct((stop - start, small.shape[1]), jnp.float32) for start, stop in cuts]
    tiles = [(r // count // UR, c // 2 // packed.shape[3]) for r, c in shapes]
    dma = pltpu.SemaphoreType.DMA((len(shapes),))
    values = pl.pallas_call(
        functools.partial(unpack_kernel, tiles, cuts),
        out_shape=out_shape + pieces,
        in_specs=[any_, vmem],
        out_specs=[any_] * len(shapes) + [vmem] * len(cuts),
        scratch_shapes=[pltpu.VMEM(s.shape, s.dtype) for s in out_shape] + [pltpu.VMEM(packed.shape, packed.dtype), dma, dma],
        compiler_params=pltpu.CompilerParams(vmem_limit_bytes=60 * 2**20),
        name="unpack_gradients",
    )(packed, small)
    return values[: len(shapes)], values[len(shapes) :]


def dot_nn(left, right):
    return lax.dot_general(left, right, (((1,), (0,)), ((), ())), preferred_element_type=jnp.float32)


def dot_nt(left, right):
    return lax.dot_general(left, right, (((1,), (1,)), ((), ())), preferred_element_type=jnp.float32)


def dot_tn(left, right):
    return lax.dot_general(left, right, (((0,), (0,)), ((), ())), preferred_element_type=jnp.float32)


EPS = 1e-05
COLS = 256


def sigmoid(v):
    return 0.5 * jnp.tanh(0.5 * v) + 0.5


def sum_scratch(count, depth, width):
    dma = pltpu.SemaphoreType.DMA((count + depth - 1,))
    return [pltpu.VMEM((8, width), jnp.float32), pltpu.VMEM((8, width), jnp.float32),
            pltpu.VMEM((count, 8, width), jnp.float32), pltpu.VMEM((depth, 8, width), jnp.float32), dma, dma]


CHUNK = 512
LEAD, HOP, FAR = 2, 2, 3
BUDGET = 3.0


def forward_kernel(count, depth, heads, shapes, items, saved_names, in_names, out_names, scratch_names, *refs):
    many = len(shapes)
    edges = np.cumsum([0, len(in_names), many, many, len(saved_names), len(out_names), len(scratch_names)])
    groups = [refs[i:j] for i, j in zip(edges[:-1], edges[1:])]
    shards, wholes, saved = groups[1], groups[2], groups[3]
    r = types.SimpleNamespace(**dict(zip(in_names, groups[0])), **dict(zip(out_names, groups[4])), **dict(zip(scratch_names, groups[5])))
    k = types.SimpleNamespace(**{name: i for i, name in enumerate(saved_names)})
    send, recv = r.send, r.recv
    bits = bits_of(count)
    dp, me = lax.axis_index("dp"), lax.axis_index("fsdp")
    core, place = lax.rem(dp, 2), dp // 2
    side = lax.rem(place, 2)
    mate, twin = flip(dp, 1), flip(dp, 2)
    span, width = r.frames.shape
    inner_width = saved[k.inner1].shape[1]
    size = width // heads
    scale = size ** -0.5

    barrier = pltpu.get_barrier_semaphore()
    pl.semaphore_signal(barrier, inc=1, device_id=(mate, me), device_id_type=MESH)
    for mask in range(1, count):
        pl.semaphore_signal(barrier, inc=1, device_id=(dp, flips(me, mask)), device_id_type=MESH)
    for j in range(1, depth):
        pl.semaphore_signal(barrier, inc=1, device_id=(lax.rem(dp + 2 * j, 2 * depth), me), device_id_type=MESH)
    pl.semaphore_wait(barrier, 1 + count - 1 + depth - 1)

    def remote(src, dst, send_sem, recv_sem, device):
        return pltpu.make_async_remote_copy(
            src_ref=src, dst_ref=dst, send_sem=send_sem, recv_sem=recv_sem, device_id=device, device_id_type=MESH)

    wide = r.small.shape[1]
    here = pl.ds(pl.multiple_of(me * wide, 128), wide)
    small_copies = [remote(r.small, r.small_held.at[:, here], r.small_send.at[mask], r.small_recv.at[mask], (dp, flips(me, mask)))
                    for mask in range(1, count)]
    for copy in small_copies:
        copy.start()
    own_copies = [remote(shards[w], wholes[w].at[pl.ds(pl.multiple_of(me * shapes[w][0], 16), shapes[w][0])],
                         r.own_send.at[w], r.own_recv.at[w], (mate, me)) for w in range(many)]
    steps = len(bits)
    kinds = 2 * steps + 3

    def parts(t):
        w, row, rows, col, edge, middle = items[t]
        base = core * (shapes[w][0] // 2) + row
        plane = pl.ds(pl.multiple_of(col + side * edge, 128), edge + middle)
        given = pl.ds(pl.multiple_of(col + side * (edge + middle), 128), edge)
        taken = pl.ds(pl.multiple_of(col + (1 - side) * (edge + middle), 128), edge)
        return w, base, rows, plane, given, taken, edge

    def block(w, owner, start, rows, cols):
        return wholes[w].at[pl.ds(pl.multiple_of(owner * shapes[w][0] + start, 16), rows), cols]

    def plane_send(t, step):
        w, base, rows, plane, *_ = parts(t)
        if step == 0 and (t == 0 or items[t - 1][0] != w):
            own_copies[w].start()
        for piece in range(2):
            order = bits if piece == 0 else bits[::-1]
            start, extent = base + piece * (rows // 2), rows // 2
            for mask in span_of(order[:step]):
                owner = flips(me, mask)
                src = (shards[w].at[pl.ds(pl.multiple_of(start, 16), extent), plane] if mask == 0
                       else block(w, owner, start, extent, plane))
                remote(src, block(w, owner, start, extent, plane), send.at[t, 2 * step + piece],
                       recv.at[t, 2 * step + piece], (dp, flips(me, order[step]))).start()

    def several(t, cols, kind, device):
        w, base, rows, *_ = parts(t)
        for mask in range(1, count):
            ref = block(w, flips(me, mask), base, rows, cols)
            remote(ref, ref, send.at[t, kind], recv.at[t, kind], device).start()

    def sizes(t, kind):
        _, _, rows, _, edge, middle = items[t]
        if kind < 2 * steps:
            return rows // 2 * 2 ** (kind // 2), edge + middle
        return rows * (count - 1), edge if kind != 2 * steps + 1 else edge + middle

    def wait(sems, t, kind):
        rows, cols = sizes(t, kind)
        if cols:
            ref = wholes[items[t][0]].at[pl.ds(0, rows), pl.ds(0, cols)]
            pltpu.make_async_copy(ref, ref, sems.at[t, kind]).wait()

    total = len(items)

    place_of = [HOP * step for step in range(steps + 1)]
    beyond = place_of[-1] + FAR
    ticks = total + beyond + 2

    def gather_tick(tick):
        t = tick + LEAD
        if t < total and tick >= 0:
            plane_send(t, 0)
        for step in range(1, steps):
            t = tick - place_of[step]
            if 0 <= t < total:
                wait(recv, t, 2 * step - 2)
                wait(recv, t, 2 * step - 1)
                plane_send(t, step)
        t = tick - place_of[steps]
        if 0 <= t < total:
            wait(recv, t, 2 * steps - 2)
            wait(recv, t, 2 * steps - 1)
            _, _, _, plane, given, taken, edge = parts(t)
            if edge:
                several(t, given, 2 * steps, (twin, me))
            several(t, plane, 2 * steps + 1, (mate, me))
        t = tick - beyond
        if 0 <= t < total:
            wait(recv, t, 2 * steps)
            if parts(t)[6]:
                several(t, parts(t)[5], 2 * steps + 2, (mate, me))
        t = tick - beyond - 1
        if 0 <= t < total:
            wait(recv, t, 2 * steps + 1)
            wait(recv, t, 2 * steps + 2)
            w = items[t][0]
            if t == 0 or items[t - 1][0] != w:
                own_copies[w].wait_recv()
            return t
        return None

    loads = {}

    def load(index, src, dst):
        loads[index] = pltpu.make_async_copy(src, dst, r.load_sem.at[index])
        loads[index].start()

    def ready(*need):
        for index in need:
            loads.pop(index).wait()

    def store(index, src):
        pltpu.make_async_copy(src, saved[index], r.store_sem.at[index]).start()

    stored = set()

    def stored_wait(index):
        pltpu.make_async_copy(saved[index], saved[index], r.store_sem.at[index]).wait()
        stored.add(index)

    gain = lambda n: r.small_all[n : n + 1]
    shift = lambda n: r.small_all[6 + n : 7 + n]

    def normed(v):
        center = v - jnp.mean(v, axis=-1, keepdims=True)
        return center * lax.rsqrt(jnp.mean(center * center, axis=-1, keepdims=True) + EPS)

    def norm_rows(src, n, dst):
        @pl.loop(0, span // 64)
        def _(i):
            rows = pl.ds(pl.multiple_of(i * 64, 64), 64)
            dst[rows] = (normed(src[rows].astype(jnp.float32)) * gain(n) + shift(n)).astype(jnp.bfloat16)

    def begin():
        r.small_held[:, here] = r.small[...]
        for copy in small_copies:
            copy.wait()
        r.small_all[...] = r.small_held[...].astype(jnp.float32)
        r.small_out[...] = r.small_all[...]
        norm_rows(r.frames, 0, r.hid1)
        store(k.hidden1, r.hid1)

    def up_half(hidden, part, parts_of):
        chunks = inner_width // CHUNK // parts_of

        @pl.loop(part * chunks, (part + 1) * chunks)
        def _(i):
            cols = pl.ds(pl.multiple_of(i * CHUNK, CHUNK), CHUNK)
            inner = dot_nn(hidden[...], r.up_vm[:, cols])
            r.inner_vm[:, cols] = inner.astype(jnp.bfloat16)
            r.active_vm[:, cols] = (inner * sigmoid(inner)).astype(jnp.bfloat16)

    def after_early():
        store(k.inner1, r.inner_vm)
        store(k.active1, r.active_vm)
        store(k.x1, r.xa)
        norm_rows(r.xa, 1, r.hid2)
        store(k.hidden2, r.hid2)

    def project(which):
        @pl.loop(0, width // CHUNK)
        def _(i):
            cols = pl.ds(pl.multiple_of(i * CHUNK, CHUNK), CHUNK)
            out = dot_nn(r.hid2[...], r.up_vm[:, pl.ds(pl.multiple_of(i * CHUNK + which * width, CHUNK), CHUNK)])
            if which == 0:
                r.content_vm[:, cols] = (out + r.small_all[12:13, cols]).astype(jnp.bfloat16)
                r.offset_vm[:, cols] = (out + r.small_all[13:14, cols]).astype(jnp.bfloat16)
            else:
                dst = r.keys_vm if which == 1 else r.values_vm
                dst[:, cols] = out.astype(jnp.bfloat16)
        if which == 0:
            store(k.content, r.content_vm)
            store(k.offset, r.offset_vm)
        else:
            store(k.keys, r.keys_vm) if which == 1 else store(k.values, r.values_vm)

    def place_offsets():
        ready(3, 4)

        @pl.loop(0, width // CHUNK)
        def _(i):
            cols = pl.ds(pl.multiple_of(i * CHUNK, CHUNK), CHUNK)
            out = dot_nn(r.table_vm[...], r.up_vm[:, pl.ds(pl.multiple_of(i * CHUNK + 3 * width, CHUNK), CHUNK)])
            r.offsets_vm[:, cols] = out.astype(jnp.bfloat16)
        store(k.offsets, r.offsets_vm)

    def attend(first, last):
        @pl.loop(first, last)
        def _(h):
            cols = pl.ds(pl.multiple_of(h * size, size), size)
            slot = lax.rem(h, 2)
            placed = dot_nt(r.offset_vm[:, cols], r.offsets_vm[:, cols])
            moved = pltpu.roll(placed, span + 1, 1, stride=1, stride_axis=0)[:, :span]
            raw = (dot_nt(r.content_vm[:, cols], r.keys_vm[:, cols]) + moved) * scale
            column = lax.broadcasted_iota(jnp.int32, raw.shape, 1)
            scores = jnp.where(column < r.length[0], raw, -1e30)
            grown = jnp.exp(scores - jnp.max(scores, axis=1, keepdims=True))
            probs = (grown * (1.0 / jnp.sum(grown, axis=1, keepdims=True))).astype(jnp.bfloat16)

            @pl.when(h >= 2)
            def _():
                pltpu.make_async_copy(r.probs_vm.at[slot], saved[k.probs].at[h], r.probs_sem.at[slot]).wait()
            r.probs_vm[slot] = probs
            pltpu.make_async_copy(r.probs_vm.at[slot], saved[k.probs].at[h], r.probs_sem.at[slot]).start()
            r.mixed_vm[:, cols] = dot_nn(probs, r.values_vm[:, cols]).astype(jnp.bfloat16)

    def after_attention():
        for slot in range(2):
            pltpu.make_async_copy(r.probs_vm.at[slot], saved[k.probs].at[0], r.probs_sem.at[slot]).wait()
        store(k.mixed, r.mixed_vm)
        ready(5)

        @pl.loop(0, width // 256)
        def _(i):
            cols = pl.ds(pl.multiple_of(i * 256, 256), 256)
            r.xb[:, cols] = r.xa[:, cols] + dot_nn(r.mixed_vm[...], r.down_vm[0:width, cols])
        store(k.x2, r.xb)
        norm_rows(r.xb, 2, r.hid3)
        store(k.hidden3, r.hid3)

    def valid_mask():
        return jnp.where(lax.broadcasted_iota(jnp.int32, (span, 1), 0) < r.length[0], 1.0, 0.0)

    taps = 5
    half = taps // 2

    def convolve():
        ready(6, 7)
        mask = valid_mask()
        r.padded[0:8] = jnp.zeros((8, 256), jnp.float32)
        r.padded[8 + span : 16 + span] = jnp.zeros((8, 256), jnp.float32)
        r.vec[...] = jnp.zeros_like(r.vec)
        r.vec[2:3] = jnp.full((1, width), 1.0, jnp.float32) * jnp.sum(mask)

        @pl.loop(0, width // 256)
        def _(i):
            cols = pl.ds(pl.multiple_of(i * 256, 256), 256)
            gates = pl.ds(pl.multiple_of(i * 256 + width, 256), 256)
            value = dot_nn(r.hid3[...], r.down_vm[width : 2 * width, cols])
            gate = dot_nn(r.hid3[...], r.down_vm[2 * width : 3 * width, cols])
            r.lifted_vm[:, cols] = value.astype(jnp.bfloat16)
            r.lifted_vm[:, gates] = gate.astype(jnp.bfloat16)
            r.padded[8 : 8 + span] = value * sigmoid(gate) * mask
            out = jnp.zeros((span, 256), jnp.float32)
            for tap in range(taps):
                out = out + r.small_all[14 + tap : 15 + tap, cols] * r.padded[8 + tap - half : 8 + tap - half + span]
            r.conv_vm[:, cols] = out
            masked = out * mask
            r.vec[0:1, cols] = jnp.sum(masked, axis=0, keepdims=True)
            r.vec[1:2, cols] = jnp.sum(masked * out, axis=0, keepdims=True)
        store(k.lifted, r.lifted_vm)
        store(k.convolved, r.conv_vm)

    pair_copy = remote(r.vec, r.pair, r.sum_send.at[0], r.sum_recv.at[0], (mate, me))
    plane_copies = [remote(r.plane.at[me], r.plane.at[me], r.sum_send.at[m], r.sum_recv.at[m], (dp, flips(me, m)))
                    for m in range(1, count)]
    line_copies = [remote(r.line.at[place], r.line.at[place], r.sum_send.at[count - 1 + j], r.sum_recv.at[count - 1 + j],
                          (lax.rem(dp + 2 * j, 2 * depth), me)) for j in range(1, depth)]

    def sum_pair():
        pair_copy.start()

    def sum_plane():
        pair_copy.wait()
        r.plane[me] = r.vec[...] + r.pair[...]
        for copy in plane_copies:
            copy.start()

    def sum_line():
        for copy in plane_copies:
            copy.wait()
        r.line[place] = functools.reduce(jnp.add, [r.plane[f] for f in range(count)])
        for copy in line_copies:
            copy.start()

    def after_conv():
        for copy in line_copies:
            copy.wait()
        sums = functools.reduce(jnp.add, [r.line[z] for z in range(depth)])
        frames = sums[2:3]
        mean = sums[0:1] / frames
        inverse = lax.rsqrt(sums[1:2] / frames - mean * mean + EPS)
        r.stats[...] = jnp.concatenate([mean, inverse, frames, jnp.zeros((5, width), jnp.float32)], axis=0)
        ready(8)

        @pl.loop(0, width // 256)
        def _(i):
            cols = pl.ds(pl.multiple_of(i * 256, 256), 256)
            normal = (r.conv_vm[:, cols] - r.stats[0:1, cols]) * r.stats[1:2, cols]
            scaled = normal * r.small_all[5:6, cols] + r.small_all[11:12, cols]
            r.swished_vm[:, cols] = (scaled * sigmoid(scaled)).astype(jnp.bfloat16)
        store(k.swished, r.swished_vm)
        stored_wait(k.x1)

        @pl.loop(0, width // 256)
        def _(i):
            cols = pl.ds(pl.multiple_of(i * 256, 256), 256)
            r.xa[:, cols] = r.xb[:, cols] + dot_nn(r.swished_vm[...], r.down_vm[3 * width : 4 * width, cols])

    def after_conv_norm():
        store(k.x3, r.xa)
        norm_rows(r.xa, 3, r.hid4)
        store(k.hidden4, r.hid4)
        stored_wait(k.inner1)
        stored_wait(k.active1)

    def late_done():
        store(k.inner4, r.inner_vm)
        store(k.active4, r.active_vm)
        stored_wait(k.x2)

    def final():
        r.edge_grads[...] = jnp.zeros_like(r.edge_grads)

        @pl.loop(0, span // 64)
        def _(i):
            start = pl.multiple_of(i * 64, 64)
            rows = pl.ds(start, 64)
            mask = jnp.where(start + lax.broadcasted_iota(jnp.int32, (64, 1), 0) < r.length[0], 1.0, 0.0)
            v = r.xb[rows]
            center = v - jnp.mean(v, axis=-1, keepdims=True)
            rate = lax.rsqrt(jnp.mean(center * center, axis=-1, keepdims=True) + EPS)
            normal = center * rate
            r.output[rows] = ((normal * gain(4) + shift(4)) * mask).astype(jnp.bfloat16)
            grad = r.cotangent[rows].astype(jnp.float32) * mask
            r.edge_grads[0:1] += jnp.sum(grad * normal, axis=0, keepdims=True)
            r.edge_grads[1:2] += jnp.sum(grad, axis=0, keepdims=True)
            inner = grad * gain(4)
            back = rate * (inner - jnp.mean(inner, axis=-1, keepdims=True)
                           - normal * jnp.mean(inner * normal, axis=-1, keepdims=True))
            r.xa[rows] = back
            r.branch_vm[rows] = (0.5 * back).astype(jnp.bfloat16)
        store(k.grad4, r.xa)
        store(k.branch4, r.branch_vm)

    def down_copies(t, w, sems):
        _, row, rows, *_ = items[t]
        shard, part = shapes[w][0], t - min(u for u in range(total) if items[u][0] == w)
        starts = [f * shard + c * (shard // 2) + row for f in range(count) for c in range(2)]
        return rows, starts, [pltpu.make_async_copy(wholes[w].at[pl.ds(start, rows)], r.down_vm.at[pl.ds(start, rows)], sems.at[part, i])
                              for i, start in enumerate(starts)]

    def down_fetch(t, w, sems):
        for copy in down_copies(t, w, sems)[2]:
            copy.start()

    def down_part(t, w, sems, src, dst):
        rows, starts, copies = down_copies(t, w, sems)
        for copy in copies:
            copy.wait()

        @pl.loop(0, width // 256)
        def _(i):
            cols = pl.ds(pl.multiple_of(i * 256, 256), 256)
            acc = functools.reduce(jnp.add, [dot_nn(r.active_vm[:, s : s + rows], r.down_vm[s : s + rows, cols]) for s in starts])
            dst[:, cols] = src[:, cols].astype(jnp.float32) + 0.5 * acc

    def before_final():
        stored_wait(k.x3)

    up, down = r.up_vm, r.down_vm
    last = [max(t for t in range(total) if items[t][0] == w) for w in range(many)]
    phases = []

    def phase(item, cost, *work):
        phases.append((item, cost, work))

    def fetch(index, src, dst):
        return lambda: load(index, src, dst)

    def call(function, *args):
        return lambda: function(*args)

    phase(-1, 1.5, begin)
    early = [t for t in range(total) if items[t][0] == 0]
    late = [t for t in range(total) if items[t][0] == 7]

    arrivals = []

    def up_loads(ts, w, index, after):
        for n, t in enumerate(ts):
            cols = pl.ds(items[t][3], 2 * items[t][4] + items[t][5])
            arrivals.append((t, after, fetch(index + n, wholes[w].at[:, cols], up.at[:, cols])))

    def down_loads(w, sems, after):
        for t in range(total):
            if items[t][0] == w:
                arrivals.append((t, after, call(down_fetch, t, w, sems)))

    up_loads(early, 0, 0, 0)
    for n, t in enumerate(early):
        phase(t, 3.2, call(ready, n), call(up_half, r.hid1, n, len(early)))
    up_over = len(phases)
    down_loads(1, r.early_sem, 0)
    firsts = [t for t in range(total) if items[t][0] == 1]
    for t in firsts:
        phase(t, 4.5 / len(firsts), call(down_part, t, 1, r.early_sem, r.frames if t == firsts[0] else r.xa, r.xa))
    down_over = len(phases)
    phase(last[1], 1.5, after_early)
    arrivals.append((last[2], up_over, fetch(10, wholes[2], up.at[:, pl.ds(0, 3 * width)])))
    phase(last[2], 2.5, call(ready, 10), call(project, 0), call(project, 1), call(project, 2))
    arrivals.append((last[3], up_over, lambda: (load(3, wholes[3], up.at[:, pl.ds(3 * width, width)]), load(4, r.table, r.table_vm))))
    phase(last[3], 3.0, place_offsets)
    lift_over = len(phases)
    for h in range(0, heads, 2):
        phase(last[3], 2.0, call(attend, h, h + 2))
    arrivals.append((last[4], down_over, fetch(5, wholes[4], down.at[pl.ds(0, width)])))
    phase(last[4], 2.0, after_attention)
    arrivals.append((last[5], down_over, lambda: (load(6, wholes[5].at[:, pl.ds(0, width)], down.at[pl.ds(width, width)]),
                                                  load(7, wholes[5].at[:, pl.ds(width, width)], down.at[pl.ds(2 * width, width)]))))
    phase(last[5], 5.5, convolve)
    phase(last[5], 0.1, sum_pair)
    arrivals.append((last[6], down_over, fetch(8, wholes[6], down.at[pl.ds(3 * width, width)])))
    phase(last[5], 2.0, sum_plane)
    phase(last[5], 3.0, sum_line)
    phase(last[6], 4.0, after_conv)
    conv_over = len(phases)
    phase(last[6], 1.0, after_conv_norm)
    up_loads(late, 7, 11, lift_over)
    for n, t in enumerate(late):
        phase(t, 3.2, call(ready, 11 + n), call(up_half, r.hid4, n, len(late)))
    phase(last[7], 0.1, late_done)
    down_loads(8, r.late_sem, conv_over)
    ends = [t for t in range(total) if items[t][0] == 8]
    for t in ends:
        phase(t, 2.0, call(down_part, t, 8, r.late_sem, r.xa if t == ends[0] else r.xb, r.xb))
    phase(total - 1, 4.0, before_final, final)
    over = 0

    def take_arrivals():
        kept = []
        for t, after, work in arrivals:
            if t <= done and after <= over:
                work()
            else:
                kept.append((t, after, work))
        arrivals[:] = kept

    for t in range(min(LEAD, total)):
        plane_send(t, 0)
    done = -1
    for tick in range(ticks):
        finished = gather_tick(tick)
        done = max(done, -1 if finished is None else finished)
        take_arrivals()
        budget = BUDGET
        while phases and phases[0][0] <= done and (budget > 0 or done == total - 1):
            _, cost, work = phases.pop(0)
            budget -= cost
            for step in work:
                step()
            over += 1
            take_arrivals()
    for index in range(len(saved) - 1):
        if index not in stored:
            stored_wait(index)
    for w in range(many):
        own_copies[w].wait_send()
    for t in range(total):
        for kind in range(kinds):
            wait(send, t, kind)


def forward(count, depth, heads, frames, cotangent, lengths, shards, small, table, collective_id=1):
    shapes = [s.shape for s in shards]
    items = gather_items(shapes)
    steps, many = len(bits_of(count)), len(shards)
    span, width = frames.shape
    inner = shapes[0][1]
    any_, vmem, smem = (pl.BlockSpec(memory_space=s) for s in (pl.ANY, pltpu.VMEM, pltpu.SMEM))
    bf, fl = jnp.bfloat16, jnp.float32
    S, dma = jax.ShapeDtypeStruct, pltpu.SemaphoreType.DMA
    V = lambda shape, dtype=bf: pltpu.VMEM(shape, dtype)
    ins = dict(length=(lengths, smem), frames=(frames, vmem), cotangent=(cotangent, vmem), table=(table, any_), small=(small, vmem))
    flat, flat32, tall = S((span, width), bf), S((span, width), fl), S((span, inner), bf)
    saved = dict(hidden1=flat, inner1=tall, active1=tall, x1=flat32, hidden2=flat, content=flat, offset=flat, keys=flat, values=flat,
                 offsets=S(table.shape, bf), mixed=flat, x2=flat32, hidden3=flat, lifted=S((span, 2 * width), bf), convolved=flat32,
                 swished=flat, x3=flat32, hidden4=flat, inner4=tall, active4=tall, grad4=flat32, branch4=flat,
                 probs=S((heads, span, span), bf))
    outs = dict(small_out=S((small.shape[0], width), fl), stats=S((8, width), fl), edge_grads=S((8, width), fl), output=flat)
    vec, pair, plane, line, sum_send, sum_recv = sum_scratch(count, depth, width)
    flat_vm, flat32_vm, gather_sems = V((span, width)), V((span, width), fl), dma((len(items), 2 * steps + 3))
    scratch = dict(
        send=gather_sems, recv=gather_sems, own_send=dma((many,)), own_recv=dma((many,)),
        small_send=dma((count,)), small_recv=dma((count,)), load_sem=dma((16,)), store_sem=dma((len(saved),)), probs_sem=dma((2,)),
        early_sem=dma((8, 2 * count)), late_sem=dma((8, 2 * count)),
        small_held=V((small.shape[0], width)), small_all=V((small.shape[0], width), fl),
        up_vm=V((width, inner)), down_vm=V((inner, width)), xa=flat32_vm, xb=flat32_vm,
        hid1=flat_vm, hid2=flat_vm, hid3=flat_vm, hid4=flat_vm, inner_vm=V((span, inner)), active_vm=V((span, inner)),
        content_vm=flat_vm, offset_vm=flat_vm, keys_vm=flat_vm, values_vm=flat_vm, table_vm=V(table.shape), offsets_vm=V(table.shape),
        probs_vm=V((2, span, span)), mixed_vm=flat_vm, lifted_vm=V((span, 2 * width)), conv_vm=flat32_vm, swished_vm=flat_vm,
        branch_vm=flat_vm, padded=V((span + 16, 256), fl),
        vec=vec, pair=pair, plane=plane, line=line, sum_send=sum_send, sum_recv=sum_recv)
    whole = [S((rows * count, cols), bf) for rows, cols in shapes]
    values = pl.pallas_call(
        functools.partial(forward_kernel, count, depth, heads, shapes, items, list(saved), list(ins), list(outs), list(scratch)),
        out_shape=whole + list(saved.values()) + list(outs.values()),
        in_specs=[b for _, b in ins.values()] + [any_] * many,
        out_specs=[any_] * (many + len(saved)) + [vmem] * len(outs),
        scratch_shapes=list(scratch.values()),
        compiler_params=pltpu.CompilerParams(collective_id=collective_id, has_side_effects=True, vmem_limit_bytes=63 * 2**20),
        name="forward",
    )(*[v for v, _ in ins.values()], *shards)
    return values[:many], types.SimpleNamespace(**dict(zip(list(saved) + list(outs), values[many:])))


COLS = 256
SLICE = 512


def backward_kernel(count, depth, heads, shapes, in_names, out_names, scratch_names, *refs):
    edges = np.cumsum([0, len(in_names), len(out_names), len(scratch_names)])
    groups = [refs[i:j] for i, j in zip(edges[:-1], edges[1:])]
    r = types.SimpleNamespace(**dict(zip(in_names, groups[0])), **dict(zip(out_names, groups[1])), **dict(zip(scratch_names, groups[2])))
    many, unit = len(shapes), unit_cols(count)
    lefts = [r.active4, r.hidden4, r.swished, r.hidden3, r.mixed, r.table, r.hidden2, r.active1, r.hidden1]
    rights = [r.branch4, r.inner_grad4, r.out_grad3, r.lifted_grad, r.out_grad2, r.offsets_grad, r.joint_grad, r.branch1, r.inner_grad1]
    bits = bits_of(count)
    steps, half = len(bits), depth // 2
    dp, me = lax.axis_index("dp"), lax.axis_index("fsdp")
    core, place = lax.rem(dp, 2), dp // 2
    mate = flip(dp, 1)
    low = place < half
    level = jnp.minimum(place, depth - 1 - place)
    inward = jnp.where(low, dp + 2, dp - 2)
    outward = jnp.where(low, dp - 2, dp + 2)
    span, width = r.grad4.shape
    inner_width = r.inner4.shape[1]
    size = width // heads
    scale = size ** -0.5

    def remote(src, dst, send, recv, device):
        return pltpu.make_async_remote_copy(
            src_ref=src, dst_ref=dst, send_sem=send, recv_sem=recv, device_id=device, device_id_type=MESH)

    def loading(src, dst, index):
        return pltpu.make_async_copy(src, dst, r.load_sem.at[index])

    def storing(src, dst, index):
        return pltpu.make_async_copy(src, dst, r.store_sem.at[index])

    units = [(rows // count // UR) * (cols // 2 // unit) for rows, cols, _ in shapes]
    bases = [int(b) for b in np.cumsum([0] + units)]
    whole = bases[-1]

    def unit_copies(w, i, slot):
        rows, cols, deep = shapes[w]
        rows, chunks = rows // count, cols // 2 // unit
        row, col = i // chunks, lax.rem(i, chunks)
        copies = []
        for m in range(count):
            src = lefts[w].at[:, pl.ds(pl.multiple_of(flips(me, m) * rows + row * UR, UR), UR)]
            copies.append(pltpu.make_async_copy(src, r.a_st.at[slot, pl.ds(0, deep), pl.ds(m * UR, UR)], r.st_sem.at[slot, m]))
        for n, owner in enumerate((1 - core, core)):
            src = rights[w].at[:, pl.ds(pl.multiple_of(owner * (cols // 2) + col * unit, unit), unit)]
            copies.append(pltpu.make_async_copy(src, r.b_st.at[slot, n, pl.ds(0, deep)], r.st_sem.at[slot, count + n]))
        return copies

    def fetch_unit(u):
        for w in range(many):
            @pl.when(jnp.logical_and(u >= bases[w], u < bases[w + 1]))
            def _(w=w):
                for copy in unit_copies(w, u - bases[w], lax.rem(u, 2)):
                    copy.start()

    def c_copy(u):
        s = lax.rem(u, CRING)
        return remote(r.snd_c.at[s], r.rcv_c.at[s], r.c_send.at[s], r.c_recv.at[s], (mate, me))

    def d_copy(j, piece, u):
        s = lax.rem(u, RING)
        order = bits if piece == 0 else bits[::-1]
        return remote(d_snd[j].at[s, piece], d_rcv[j].at[s, piece],
                      r.d_send.at[j, piece, s], r.d_recv.at[j, piece, s], (dp, flip(me, order[j])))

    d_snd = [r.d_snd0, r.d_snd1, r.d_snd2][:steps]
    d_rcv = [r.d_rcv0, r.d_rcv1, r.d_rcv2][:steps]

    def zi_copy(u):
        s = lax.rem(u, ZRING)
        return remote(r.z_snd.at[s], r.z_acc.at[s], r.zi_send.at[s], r.za_recv.at[s], (inward, me))

    def zm_copy(u):
        s = lax.rem(u, ZRING)
        return remote(r.z_snd.at[s], r.z_mid.at[s], r.zi_send.at[s], r.zm_recv.at[s], (inward, me))

    def loc_copy(u):
        s = lax.rem(u, ZRING)
        return pltpu.make_async_copy(r.total.at[s], r.packed.at[core, u], r.loc_sem.at[s])

    def mt_copy(u, src):
        s = lax.rem(u, ORING)
        return remote(src, r.packed.at[core, u], r.mt_send.at[s], r.mt_recv.at[s], (mate, me))

    def zo_copy(u, src):
        s = lax.rem(u, ORING)
        return remote(src, r.packed.at[core, u], r.zo_send.at[s], r.zo_recv.at[s], (outward, me))

    def first(u):
        slot, s = lax.rem(u, 2), lax.rem(u, CRING)
        depths = sorted(set(deep for *_, deep in shapes))
        for deep in depths:
            ws = [w for w in range(many) if shapes[w][2] == deep]
            cond = functools.reduce(jnp.logical_or, [jnp.logical_and(u >= bases[w], u < bases[w + 1]) for w in ws])

            @pl.when(cond)
            def _(deep=deep, w=ws[0]):
                for copy in unit_copies(w, 0, slot):
                    copy.wait()
                left = r.a_st[slot, 0:deep]
                r.snd_c[s] = outer(left, r.b_st[slot, 0, 0:deep]).astype(jnp.bfloat16).reshape(count, UR, unit)
                c_copy(u).start()
                r.own[lax.rem(u, RING)] = outer(left, r.b_st[slot, 1, 0:deep]).reshape(count, UR, unit)

    def rows_of(piece):
        return slice(piece * (UR // 2), (piece + 1) * (UR // 2))

    def second(u):
        c_copy(u).wait()
        s, c = lax.rem(u, RING), lax.rem(u, CRING)
        for piece in range(2):
            order = bits if piece == 0 else bits[::-1]
            rs = rows_of(piece)
            for k, m in enumerate(span_of(order[1:])):
                x = m + order[0]
                d_snd[0][s, piece, k] = (r.own[s, x, rs] + r.rcv_c[c, x, rs].astype(jnp.float32)).astype(jnp.bfloat16)
            d_copy(0, piece, u).start()
        for piece in range(2):
            order = bits if piece == 0 else bits[::-1]
            rs = rows_of(piece)
            for m in span_of(order[1:]):
                r.own[s, m, rs] = r.own[s, m, rs] + r.rcv_c[c, m, rs].astype(jnp.float32)

    def onward(j, u):
        s = lax.rem(u, RING)
        for piece in range(2):
            d_copy(j - 1, piece, u).wait()
            order = bits if piece == 0 else bits[::-1]
            rs = rows_of(piece)
            spans, keep = span_of(order[j:]), span_of(order[j + 1 :])
            for k, m in enumerate(spans):
                if m not in keep:
                    d_snd[j][s, piece, keep.index(m - order[j])] = (
                        r.own[s, m, rs] + d_rcv[j - 1][s, piece, k].astype(jnp.float32)).astype(jnp.bfloat16)
            d_copy(j, piece, u).start()
            for k, m in enumerate(spans):
                if m in keep:
                    r.own[s, m, rs] = r.own[s, m, rs] + d_rcv[j - 1][s, piece, k].astype(jnp.float32)

    def plane_done(u):
        s, z = lax.rem(u, RING), lax.rem(u, ZRING)
        for piece in range(2):
            d_copy(steps - 1, piece, u).wait()
            rs = rows_of(piece)
            r.zsum[z, rs] = r.own[s, 0, rs] + d_rcv[steps - 1][s, piece, 0].astype(jnp.float32)

        @pl.when(level == 0)
        def _():
            r.z_snd[z] = r.zsum[z].astype(jnp.bfloat16)
            if half == 1:
                zm_copy(u).start()
            else:
                zi_room(u)
                zi_copy(u).start()

    def zi_room(u):
        @pl.when(u >= ZRING)
        def _():
            pl.semaphore_wait(r.z_free, 1)

    def climb(j, u):
        z = lax.rem(u, ZRING)

        @pl.when(level == j - 1)
        def _():
            zi_copy(u).wait_send()

        @pl.when(level == j)
        def _():
            zi_copy(u).wait_recv()
            r.z_snd[z] = (r.zsum[z] + r.z_acc[z].astype(jnp.float32)).astype(jnp.bfloat16)

            @pl.when(u < whole - ZRING)
            def _():
                pl.semaphore_signal(r.z_free, inc=1, device_id=(outward, me), device_id_type=MESH)
            if j == half - 1:
                zm_copy(u).start()
            else:
                zi_room(u)
                zi_copy(u).start()

    def middle(u):
        z = lax.rem(u, ZRING)

        @pl.when(level == half - 1)
        def _():
            zm_copy(u).wait()
            r.total[z] = (r.z_snd[z].astype(jnp.float32) + r.z_mid[z].astype(jnp.float32)).astype(jnp.bfloat16)
            if half > 1:
                zo_copy(u, r.total.at[z]).start()
            mt_copy(u, r.total.at[z]).start()
            loc_copy(u).start()

    def descend(j, u):
        z = lax.rem(u, ZRING)

        @pl.when(level == half - j)
        def _():
            src = r.total.at[z] if j == 1 else r.packed.at[core, u]
            zo_copy(u, src).wait_send()

        @pl.when(level == half - 1 - j)
        def _():
            zo_copy(u, r.packed.at[core, u]).wait_recv()
            if j < half - 1:
                zo_copy(u, r.packed.at[core, u]).start()
            mt_copy(u, r.packed.at[core, u]).start()

    def finish(u):
        z = lax.rem(u, ZRING)

        @pl.when(level == half - 1)
        def _():
            loc_copy(u).wait()
        mt_copy(u, r.total.at[z]).wait()

    stages = [(1, second)]
    at = 1
    for j in range(1, steps):
        at += LAG
        stages.append((at, functools.partial(onward, j)))
    at += LAG
    stages.append((at, plane_done))
    for j in range(1, half):
        at += LAG
        stages.append((at, functools.partial(climb, j)))
    at += LAG
    stages.append((at, middle))
    for j in range(1, half):
        at += LAG
        stages.append((at, functools.partial(descend, j)))
    at += LAG
    stages.append((at, finish))

    slices = inner_width // SLICE

    def slice_streams(i, up, inner):
        slot, cols = lax.rem(i, 2), pl.ds(pl.multiple_of(i * SLICE, SLICE), SLICE)
        return (pltpu.make_async_copy(up.at[:, cols], r.up_st.at[slot], r.up_sem.at[slot]),
                pltpu.make_async_copy(inner.at[:, cols], r.in_st.at[slot], r.in_sem.at[slot]))

    def slice_store(i, dst):
        slot, cols = lax.rem(i, 2), pl.ds(pl.multiple_of(i * SLICE, SLICE), SLICE)
        return pltpu.make_async_copy(r.ig_st.at[slot], dst.at[:, cols], r.ig_sem.at[slot])

    def slices_begin(down, up, inner):
        for i in range(slices):
            rows = pl.ds(i * SLICE, SLICE)
            pltpu.make_async_copy(down.at[rows], r.w_vm.at[rows], r.w_sem.at[i]).start()
        for i in range(2):
            for copy in slice_streams(i, up, inner):
                copy.start()

    def slice_work(i, late):
        slot = lax.rem(i, 2)
        rows = pl.ds(pl.multiple_of(i * SLICE, SLICE), SLICE)
        pltpu.make_async_copy(r.late_down.at[rows], r.w_vm.at[rows], r.w_sem.at[i]).wait()
        for copy in slice_streams(i, r.late_up, r.inner4):
            copy.wait()

        @pl.when(i >= 2)
        def _():
            slice_store(i, r.inner_grad4).wait()

        @pl.loop(0, SLICE // COLS)
        def _(c):
            part = pl.ds(pl.multiple_of(c * COLS, COLS), COLS)
            active_grad = dot_nt(r.og[...], r.w_vm[pl.ds(pl.multiple_of(i * SLICE + c * COLS, COLS), COLS)])
            inner = r.in_st[slot, :, part].astype(jnp.float32)
            gate = sigmoid(inner)
            r.ig_st[slot, :, part] = (active_grad * (gate * (1.0 + inner * (1.0 - gate)))).astype(jnp.bfloat16)

        @pl.when(late)
        def _():
            slice_store(i, r.inner_grad4).start()

        @pl.when(jnp.logical_not(late))
        def _():
            slice_store(i, r.inner_grad1).start()

        @pl.loop(0, width // COLS)
        def _(c):
            part = pl.ds(pl.multiple_of(c * COLS, COLS), COLS)
            r.acc[:, part] += dot_nt(r.ig_st[slot], r.up_st[slot, part])

        @pl.when(jnp.logical_and(late, i < slices - 2))
        def _():
            for copy in slice_streams(i + 2, r.late_up, r.inner4):
                copy.start()

        @pl.when(jnp.logical_and(jnp.logical_not(late), i < slices - 2))
        def _():
            for copy in slice_streams(i + 2, r.early_up, r.inner1):
                copy.start()

    def slices_over(dst):
        for i in range(2):
            slice_store(i, dst).wait()

    def norm_back(n, factor):
        gain = r.small_all[pl.ds(n, 1)]
        r.sums[...] = jnp.zeros_like(r.sums)

        @pl.loop(0, span // 64)
        def _(i):
            rows = pl.ds(pl.multiple_of(i * 64, 64), 64)
            v, grad = r.x[rows], r.acc[rows]
            center = v - jnp.mean(v, axis=-1, keepdims=True)
            rate = lax.rsqrt(jnp.mean(center * center, axis=-1, keepdims=True) + EPS)
            normal = center * rate
            r.sums[0:1] += jnp.sum(grad * normal, axis=0, keepdims=True)
            r.sums[1:2] += jnp.sum(grad, axis=0, keepdims=True)
            inner = grad * gain
            back = r.grad[rows] + rate * (inner - jnp.mean(inner, axis=-1, keepdims=True)
                                          - normal * jnp.mean(inner * normal, axis=-1, keepdims=True))
            r.grad[rows] = back
            r.og[rows] = (factor * back).astype(jnp.bfloat16)
        r.small_buf[pl.ds(n, 1)] = r.sums[0:1]
        r.small_buf[pl.ds(n + 6, 1)] = r.sums[1:2]

    def valid_mask():
        return jnp.where(lax.broadcasted_iota(jnp.int32, (span, 1), 0) < r.length[0], 1.0, 0.0)

    taps = 5
    reach = taps // 2

    def conv_first(j):
        cols = pl.ds(pl.multiple_of(j * COLS, COLS), COLS)
        mask = valid_mask()
        swish_grad = dot_nt(r.og[...], r.w_vm[cols])
        normal = (r.x[:, cols] - r.stats[0:1, cols]) * r.stats[1:2, cols]
        scaled = normal * r.small_all[5:6, cols] + r.small_all[11:12, cols]
        gate = sigmoid(scaled)
        scaled_grad = swish_grad * (gate * (1.0 + scaled * (1.0 - gate)))
        r.acc[:, cols] = scaled_grad
        masked = scaled_grad * mask
        r.vec[0:1, cols] = jnp.sum(masked, axis=0, keepdims=True)
        r.vec[1:2, cols] = jnp.sum(masked * normal, axis=0, keepdims=True)

    def conv_second(j):
        cols = pl.ds(pl.multiple_of(j * COLS, COLS), COLS)
        gates = pl.ds(pl.multiple_of(j * COLS + width, COLS), COLS)
        mask = valid_mask()
        normal = (r.x[:, cols] - r.stats[0:1, cols]) * r.stats[1:2, cols]
        inner = mask * ((r.vec[0:1, cols] + normal * r.vec[1:2, cols]) / r.stats[2:3, cols])
        conv_grad = r.stats[1:2, cols] * r.small_all[5:6, cols] * (r.acc[:, cols] - inner)
        r.padded[8 : 8 + span] = conv_grad
        up, gate = r.lifted_vm[:, cols].astype(jnp.float32), sigmoid(r.lifted_vm[:, gates].astype(jnp.float32))
        r.gated[8 : 8 + span] = up * gate * mask
        total = jnp.zeros((span, COLS), jnp.float32)
        for tap in range(taps):
            total = total + r.small_all[14 + tap : 15 + tap, cols] * r.padded[8 - tap + reach : 8 - tap + reach + span]
            moved = r.gated[8 + tap - reach : 8 + tap - reach + span]
            r.small_buf[14 + tap : 15 + tap, cols] = jnp.sum(moved * conv_grad, axis=0, keepdims=True)
        total = total * mask
        r.lg_vm[:, cols] = (total * gate).astype(jnp.bfloat16)
        r.lg_vm[:, gates] = (total * up * gate * (1.0 - gate)).astype(jnp.bfloat16)

    pair_copy = remote(r.vec, r.pair, r.sum_send.at[0], r.sum_recv.at[0], (mate, me))
    plane_copies = [remote(r.plane.at[me], r.plane.at[me], r.sum_send.at[m], r.sum_recv.at[m], (dp, flips(me, m)))
                    for m in range(1, count)]
    line_to = [(lax.rem(dp + 2 * j, 2 * depth), me) for j in range(1, depth)]
    line_copies = [remote(r.line.at[place], r.line.at[place], r.sum_send.at[count + j], r.sum_recv.at[count + j], line_to[j])
                   for j in range(depth - 1)]

    def sum_plane():
        pair_copy.wait()
        r.plane[me] = r.vec[...] + r.pair[...]
        for copy in plane_copies:
            copy.start()

    def sum_line():
        for copy in plane_copies:
            copy.wait()
        r.line[place] = functools.reduce(jnp.add, [r.plane[f] for f in range(count)])
        for copy in line_copies:
            copy.start()

    def sum_over():
        for copy in line_copies:
            copy.wait()
        r.vec[...] = functools.reduce(jnp.add, [r.line[z] for z in range(depth)])

    def head_copies(h):
        slot, cols = lax.rem(h, 2), pl.ds(pl.multiple_of(h * size, size), size)
        copies = [pltpu.make_async_copy(src.at[:, cols], r.head_st.at[slot, n], r.head_sem.at[slot, n])
                  for n, src in enumerate((r.content, r.offset, r.keys, r.values))]
        copies.append(pltpu.make_async_copy(r.offsets.at[:, cols], r.place_st.at[slot], r.head_sem.at[slot, 4]))
        copies.append(pltpu.make_async_copy(r.probs.at[h], r.probs_st.at[slot], r.head_sem.at[slot, 5]))
        return copies

    def offsets_store(h):
        slot, cols = lax.rem(h, 2), pl.ds(pl.multiple_of(h * size, size), size)
        return pltpu.make_async_copy(r.turned_st.at[slot], r.offsets_grad.at[:, cols], r.turned_sem.at[slot])

    def attend_back(h):
        slot, cols = lax.rem(h, 2), pl.ds(pl.multiple_of(h * size, size), size)
        for copy in head_copies(h):
            copy.wait()

        @pl.when(h >= 2)
        def _():
            offsets_store(h).wait()
        content, offset, key, value = (r.head_st[slot, n] for n in range(4))
        mixed_grad, p = r.mg_vm[:, cols], r.probs_st[slot]
        key_cols = pl.ds(pl.multiple_of(h * size + width, size), size)
        value_cols = pl.ds(pl.multiple_of(h * size + 2 * width, size), size)
        prob_grad = dot_nt(mixed_grad, value)
        r.joint_vm[:, value_cols] = dot_tn(p, mixed_grad).astype(jnp.bfloat16)
        weights = p.astype(jnp.float32)
        product = weights * prob_grad
        score_grad = product - weights * jnp.sum(product, axis=1, keepdims=True)
        raw_grad = (score_grad * scale).astype(jnp.bfloat16)
        content_grad = dot_nn(raw_grad, key)
        r.joint_vm[:, key_cols] = dot_tn(raw_grad, content).astype(jnp.bfloat16)
        turn = r.turn[...]
        turned = dot_nn(turn, raw_grad)
        wide = jnp.concatenate([turned, jnp.zeros_like(turned)], axis=1)
        placed = pltpu.roll(wide, 0, 1, stride=1, stride_axis=0).astype(jnp.bfloat16)
        turned_offset = dot_nn(turn, offset).astype(jnp.bfloat16)
        r.turned_st[slot] = dot_tn(placed, turned_offset).astype(jnp.bfloat16)
        offsets_store(h).start()
        turned_grad = dot_nn(placed, r.place_st[slot])
        high = turned_grad.astype(jnp.bfloat16)
        small = (turned_grad - high.astype(jnp.float32)).astype(jnp.bfloat16)
        offset_grad = dot_nn(turn, high) + dot_nn(turn, small)
        r.joint_vm[:, cols] = (content_grad + offset_grad).astype(jnp.bfloat16)
        r.small_buf[12:13, cols] = jnp.sum(content_grad, axis=0, keepdims=True)
        r.small_buf[13:14, cols] = jnp.sum(turned_grad, axis=0, keepdims=True)

        @pl.when(h < heads - 2)
        def _():
            for copy in head_copies(h + 2):
                copy.start()

    narrow = r.small_out.shape[1]

    def columns(f):
        return pl.ds(pl.multiple_of(f * narrow, 128), narrow)

    small_pair = remote(r.small_buf, r.s_pair, r.s_send.at[0], r.s_recv.at[0], (mate, me))
    small_plane = [remote(r.s_both.at[:, columns(flips(me, m))], r.s_plane.at[me], r.s_send.at[m], r.s_recv.at[m], (dp, flips(me, m)))
                   for m in range(1, count)]
    small_line = [remote(r.s_line.at[place], r.s_line.at[place], r.s_send.at[count + j], r.s_recv.at[count + j], line_to[j])
                  for j in range(depth - 1)]

    def small_second():
        small_pair.wait()
        r.s_both[...] = r.small_buf[...] + r.s_pair[...]
        for copy in small_plane:
            copy.start()
        r.s_plane[me] = r.s_both[:, columns(me)]

    def small_third():
        for copy in small_plane:
            copy.wait()
        r.s_line[place] = functools.reduce(jnp.add, [r.s_plane[f] for f in range(count)])
        for copy in small_line:
            copy.start()

    def small_last():
        for copy in small_line:
            copy.wait()
        r.small_out[...] = functools.reduce(jnp.add, [r.s_line[z] for z in range(depth)])

    def block(n):
        return r.w_vm.at[pl.ds(n * width, width)]

    conv_loads = [loading(r.convolved, r.x, 2), loading(r.lifted, r.lifted_vm, 3), loading(r.pointwise_down, block(0), 4),
                  loading(r.pointwise_up.at[:, pl.ds(0, width)], block(1), 5),
                  loading(r.pointwise_up.at[:, pl.ds(width, width)], block(2), 6), loading(r.heads_out, block(3), 7)]
    query_loads = [loading(r.heads_in.at[:, pl.ds(n * width, width)], block(n), 9 + n) for n in range(3)]
    state_load, older_load = loading(r.x2, r.x, 8), loading(r.x1, r.x, 12)
    grad3_store, lifted_store = storing(r.og, r.out_grad3, 0), storing(r.lg_vm, r.lifted_grad, 1)
    grad2_store, joint_store = storing(r.og, r.out_grad2, 2), storing(r.joint_vm, r.joint_grad, 3)
    branch_store, frames_store = storing(r.og, r.branch1, 4), storing(r.grad, r.frames_grad, 5)

    def hidden_cols(first_col, last_col, parts):
        @pl.loop(first_col, last_col)
        def _(c):
            cols = pl.ds(pl.multiple_of(c * COLS, COLS), COLS)
            r.acc[:, cols] = functools.reduce(jnp.add, [
                dot_nt(src[:, a * width : (a + 1) * width], r.w_vm[pl.ds(pl.multiple_of(b * width + c * COLS, COLS), COLS)])
                for src, a, b in parts])

    def chain(tick):
        def when(*ticks):
            cond = functools.reduce(jnp.logical_or, [tick == t for t in ticks])
            return pl.when(cond)

        late, begin_late = tick < 6, jnp.where(tick < 2, 2 * tick, tick + 2)
        several_late = tick < 2
        tick = tick - 2

        @pl.when(jnp.logical_or(late, jnp.logical_and(tick >= 24, tick < 24 + slices)))
        def _():
            begin = jnp.where(late, begin_late, tick - 24)

            @pl.loop(0, jnp.where(several_late, 2, 1))
            def _(k):
                slice_work(begin + k, late)

        @when(4)
        def _():
            slices_over(r.inner_grad4)
            for copy in conv_loads[2:]:
                copy.start()

        @when(32)
        def _():
            r.x[...] = r.frames[...].astype(jnp.float32)
            slices_over(r.inner_grad1)

        @when(4, 12, 23, 32)
        def _():
            n = jnp.where(tick == 4, 3, jnp.where(tick == 12, 2, jnp.where(tick == 23, 1, 0)))
            norm_back(n, jnp.where(tick == 23, 0.5, 1.0))

        @when(4)
        def _():
            grad3_store.start()
            conv_loads[0].start()
            conv_loads[1].start()

        @when(5)
        def _():
            for copy in conv_loads[:3]:
                copy.wait()

        @when(5, 6)
        def _():
            @pl.loop(0, 2)
            def _(k):
                conv_first(2 * (tick - 5) + k)

        @when(6)
        def _():
            r.small_buf[5:6] = r.vec[1:2]
            r.small_buf[11:12] = r.vec[0:1]
            pair_copy.start()

        when(7)(sum_plane)
        when(8)(sum_line)

        @when(9)
        def _():
            sum_over()

        @when(9, 10)
        def _():
            @pl.loop(0, 2)
            def _(k):
                conv_second(2 * (tick - 9) + k)

        @when(10)
        def _():
            lifted_store.start()
            state_load.start()
            grad3_store.wait()

        @when(11)
        def _():
            conv_loads[3].wait()
            conv_loads[4].wait()
            hidden_cols(0, width // COLS, [(r.lg_vm, 0, 1), (r.lg_vm, 1, 2)])
            state_load.wait()
            for h in range(2):
                for copy in head_copies(h):
                    copy.start()

        @when(12)
        def _():
            lifted_store.wait()
            grad2_store.start()
            older_load.start()
            conv_loads[5].wait()

            @pl.loop(0, width // COLS)
            def _(c):
                cols = pl.ds(pl.multiple_of(c * COLS, COLS), COLS)
                r.mg_vm[:, cols] = dot_nt(r.og[...], r.w_vm[pl.ds(pl.multiple_of(3 * width + c * COLS, COLS), COLS)]).astype(jnp.bfloat16)

        @when(13)
        def _():
            for copy in query_loads:
                copy.start()

        @pl.when(jnp.logical_and(tick >= 13, tick < 13 + heads))
        def _():
            attend_back(tick - 13)

        @when(13 + heads - 1)
        def _():
            joint_store.start()
            for h in range(2):
                offsets_store(h).wait()

        when(16)(grad2_store.wait)
        when(27)(branch_store.wait)
        joint_parts = [(r.joint_vm, n, n) for n in range(3)]

        @when(21)
        def _():
            for copy in query_loads:
                copy.wait()
            older_load.wait()

        @when(21, 22)
        def _():
            begin = (width // COLS // 2) * (tick - 21)
            hidden_cols(begin, begin + width // COLS // 2, joint_parts)

        when(22)(joint_store.wait)

        @when(23)
        def _():
            branch_store.start()
            r.acc[...] = jnp.zeros_like(r.acc)
            slices_begin(r.early_down, r.early_up, r.inner1)

        @when(32)
        def _():
            frames_store.start()
            small_pair.start()

        when(34)(small_second)
        when(36)(small_third)

        @when(38)
        def _():
            small_last()
            frames_store.wait()

    barrier = pltpu.get_barrier_semaphore()
    pl.semaphore_signal(barrier, inc=1, device_id=(mate, me), device_id_type=MESH)
    for mask in range(1, count):
        pl.semaphore_signal(barrier, inc=1, device_id=(dp, flips(me, mask)), device_id_type=MESH)
    for device in line_to:
        pl.semaphore_signal(barrier, inc=1, device_id=device, device_id_type=MESH)
    starts = [loading(r.grad4, r.grad, 0), loading(r.x3, r.x, 1), loading(r.branch4, r.og, 13)]
    for copy in starts:
        copy.start()
    fetch_unit(jnp.int32(0))
    slices_begin(r.late_down, r.late_up, r.inner4)
    r.acc[...] = jnp.zeros_like(r.acc)
    r.small_buf[...] = jnp.zeros_like(r.small_buf)
    r.small_buf[4:5] = r.edge_grads[0:1]
    r.small_buf[10:11] = r.edge_grads[1:2]
    r.vec[...] = jnp.zeros_like(r.vec)
    for ref in (r.padded, r.gated):
        ref[0:8] = jnp.zeros((8, COLS), jnp.float32)
        ref[8 + span : 16 + span] = jnp.zeros((8, COLS), jnp.float32)
    row = lax.broadcasted_iota(jnp.int32, (span, span), 0)
    column = lax.broadcasted_iota(jnp.int32, (span, span), 1)
    r.turn[...] = jnp.where(row + column == span - 1, 1.0, 0.0).astype(jnp.bfloat16)
    pl.semaphore_wait(barrier, 1 + count - 1 + depth - 1)
    for copy in starts:
        copy.wait()

    @pl.loop(0, whole + at + 1)
    def _(tick):
        @pl.when(tick + 1 < whole)
        def _():
            fetch_unit(tick + 1)

        @pl.when(tick < whole)
        def _():
            first(tick)
        for lag, stage in stages:
            pl.when(jnp.logical_and(tick >= lag, tick - lag < whole))(functools.partial(stage, tick - lag))
        chain(tick)


def backward(count, depth, heads, frames, lengths, wholes, f, table, collective_id=2):
    early_up, early_down, heads_in, _, heads_out, pointwise_up, pointwise_down, late_up, late_down = wholes
    any_, vmem, smem = (pl.BlockSpec(memory_space=s) for s in (pl.ANY, pltpu.VMEM, pltpu.SMEM))
    bf, fl = jnp.bfloat16, jnp.float32
    S, dma = jax.ShapeDtypeStruct, pltpu.SemaphoreType.DMA
    V = lambda shape, dtype=bf: pltpu.VMEM(shape, dtype)
    span, width = frames.shape
    inner = early_up.shape[1]
    size, unit = width // heads, unit_cols(count)
    far = dict(
        table=table, early_up=early_up, early_down=early_down, heads_in=heads_in, heads_out=heads_out, pointwise_up=pointwise_up,
        pointwise_down=pointwise_down, late_up=late_up, late_down=late_down, active4=f.active4, branch4=f.branch4, inner4=f.inner4,
        hidden4=f.hidden4, grad4=f.grad4, x3=f.x3, convolved=f.convolved, lifted=f.lifted, swished=f.swished, hidden3=f.hidden3,
        x2=f.x2, mixed=f.mixed, content=f.content, offset=f.offset, keys=f.keys, values=f.values, probs=f.probs, offsets=f.offsets,
        hidden2=f.hidden2, x1=f.x1, active1=f.active1, inner1=f.inner1, hidden1=f.hidden1)
    near = dict(frames=frames, small_all=f.small_out, stats=f.stats, edge_grads=f.edge_grads)
    shapes = [(inner, width, span), (width, inner, span), (width, width, span), (width, 2 * width, span), (width, width, span),
              (width, width, table.shape[0]), (width, 3 * width, span), (inner, width, span), (width, inner, span)]
    units = sum((rows // count // UR) * (cols // 2 // unit) for rows, cols, _ in shapes)
    rows = f.small_out.shape[0]
    flat, tall = S((span, width), bf), S((span, inner), bf)
    far_outs = dict(packed=S((2, units, UR, unit), bf), frames_grad=S((span, width), fl), inner_grad4=tall, out_grad3=flat,
                    lifted_grad=S((span, 2 * width), bf), out_grad2=flat, offsets_grad=S(table.shape, bf),
                    joint_grad=S((span, 3 * width), bf), branch1=flat, inner_grad1=tall)
    near_outs = dict(small_out=S((rows, width // count), fl))
    vec, pair, plane, line, _, _ = sum_scratch(count, depth, width)
    bits = bits_of(count)
    deepest = max(deep for *_, deep in shapes)
    block_ring = V((CRING, count, UR, unit))
    z_ring = V((ZRING, UR, unit))
    scratch = dict(
        a_st=V((2, deepest, count * UR)), b_st=V((2, 2, deepest, unit)), st_sem=dma((2, count + 2)),
        own=V((RING, count, UR, unit), fl), snd_c=block_ring, rcv_c=block_ring,
        zsum=V((ZRING, UR, unit), fl), z_snd=z_ring, z_acc=z_ring, z_mid=z_ring, total=z_ring,
        c_send=dma((CRING,)), c_recv=dma((CRING,)), zi_send=dma((ZRING,)), za_recv=dma((ZRING,)), zm_recv=dma((ZRING,)), z_free=pltpu.SemaphoreType.REGULAR,
        loc_sem=dma((ZRING,)), mt_send=dma((ORING,)), mt_recv=dma((ORING,)), zo_send=dma((ORING,)), zo_recv=dma((ORING,)),
        d_send=dma((len(bits), 2, RING)), d_recv=dma((len(bits), 2, RING)),
        s_pair=V((rows, width), fl), s_both=V((rows, width), fl), s_plane=V((count, rows, width // count), fl),
        s_line=V((depth, rows, width // count), fl), s_send=dma((count + depth,)), s_recv=dma((count + depth,)),
        load_sem=dma((14,)), store_sem=dma((6,)), small_buf=V((rows, width), fl), sums=V((8, width), fl),
        w_vm=V((inner, width)), w_sem=dma((inner // SLICE,)), up_st=V((2, width, SLICE)), up_sem=dma((2,)),
        in_st=V((2, span, SLICE)), in_sem=dma((2,)), ig_st=V((2, span, SLICE)), ig_sem=dma((2,)),
        grad=V((span, width), fl), acc=V((span, width), fl), x=V((span, width), fl), og=V((span, width)),
        lifted_vm=V((span, 2 * width)), lg_vm=V((span, 2 * width)), padded=V((span + 16, COLS), fl), gated=V((span + 16, COLS), fl),
        vec=vec, pair=pair, plane=plane, line=line, sum_send=dma((count + depth,)), sum_recv=dma((count + depth,)),
        head_st=V((2, 4, span, size)), place_st=V((2, table.shape[0], size)), probs_st=V((2, span, span)), head_sem=dma((2, 6)),
        turned_st=V((2, table.shape[0], size)), turned_sem=dma((2,)), joint_vm=V((span, 3 * width)), mg_vm=V((span, width)),
        turn=V((span, span)))
    tiny = V((8, 128))
    rings = [V((RING, 2, count // 2 ** (j + 1), UR // 2, unit)) if j < len(bits) else tiny for j in range(3)]
    scratch.update(d_snd0=rings[0], d_snd1=rings[1], d_snd2=rings[2], d_rcv0=rings[0], d_rcv1=rings[1], d_rcv2=rings[2])
    names = [["length"] + list(near) + list(far), list(far_outs) + list(near_outs), list(scratch)]
    values = pl.pallas_call(
        functools.partial(backward_kernel, count, depth, heads, shapes, *names),
        out_shape=list(far_outs.values()) + list(near_outs.values()),
        in_specs=[smem] + [vmem] * len(near) + [any_] * len(far),
        out_specs=[any_] * len(far_outs) + [vmem] * len(near_outs),
        scratch_shapes=list(scratch.values()),
        compiler_params=pltpu.CompilerParams(collective_id=collective_id, has_side_effects=True, vmem_limit_bytes=63 * 2**20 + 2**19),
        name="backward",
    )(lengths, *near.values(), *far.values())
    return values[0], values[1], values[-1], [s[:2] for s in shapes]


HEADS = 8


def position_table(span, width):
    distance = (span - 1 - np.arange(2 * span - 1)).astype(np.float32)
    rate = np.exp(np.arange(width // 2).astype(np.float32) * np.float32(-2.0 * math.log(10000.0) / width))
    angle = distance[:, None] * rate[None, :]
    table = np.concatenate([np.sin(angle), np.cos(angle)], axis=1)
    return np.concatenate([table, np.zeros((1, width), np.float32)]).astype(jnp.bfloat16)


def body(count, depth, frames, lengths, cotangent, early_up, early_down, heads_in, offset_proj, heads_out,
         pointwise_up, pointwise_down, late_up, late_down, depthwise, norm_gains, norm_shifts, score_bias):
    _, span, width = frames.shape
    taps = depthwise.shape[0]
    table = jnp.asarray(position_table(span, width))
    small = jnp.concatenate([norm_gains, norm_shifts, score_bias, depthwise], axis=0)
    rows = small.shape[0]
    small = jnp.pad(small, ((0, 32 - rows), (0, 0)))
    wholes, f = forward(count, depth, HEADS, frames[0], cotangent[0], lengths,
                [early_up, early_down, heads_in, offset_proj, heads_out, pointwise_up, pointwise_down, late_up, late_down],
                small, table)
    packed, frames_grad, small_sum, shapes = backward(count, depth, HEADS, frames[0], lengths, wholes, f, table)
    grads, pieces = unpack(packed, small_sum, [(14, 14 + taps), (0, 6), (6, 12), (12, 14)], count, shapes)
    (late_down_grad, late_up_grad, pointwise_down_grad, pointwise_up_grad, heads_out_grad, offset_proj_grad, heads_in_grad,
     early_down_grad, early_up_grad) = grads
    return (
        f.output[None], frames_grad[None], early_up_grad, early_down_grad, heads_in_grad, offset_proj_grad, heads_out_grad,
        pointwise_up_grad, pointwise_down_grad, late_up_grad, late_down_grad, *pieces,
    )


def solution(mesh):
    item = P(("dp", "fsdp"), None, None)
    rows = P("fsdp", None)
    cols = P(None, "fsdp")
    in_specs = (item, P(("dp", "fsdp")), item) + (rows,) * 9 + (cols,) * 4
    out_specs = (item, item) + (rows,) * 9 + (cols,) * 4
    count, depth = mesh.shape["fsdp"], mesh.shape["dp"] // 2
    return jax.shard_map(functools.partial(body, count, depth), mesh=mesh, in_specs=in_specs, out_specs=out_specs, check_vma=False)
```

```python
import functools
import math
import types

import jax
import jax.numpy as jnp
import numpy as np
from jax import lax
from jax.experimental import pallas as pl
from jax.experimental.pallas import tpu as pltpu
from jax.sharding import PartitionSpec as P

MESH = pl.DeviceIdType.MESH


def flip(index, bit):
    return index + bit - 2 * bit * ((index // bit) % 2)


def bits_of(count):
    bits, bit = [], 1
    while bit < count:
        bits.append(bit)
        bit *= 2
    return bits


def span_of(bits):
    held = [0]
    for bit in bits:
        held = held + [h + bit for h in held]
    return held


def flips(index, mask):
    bit = 1
    while bit <= mask:
        if mask & bit:
            index = flip(index, bit)
        bit *= 2
    return index


def gather_items(shapes):
    items = []
    for w, (rows, cols) in enumerate(shapes):
        half = rows // 2
        row_step, col_step = min(half, 128), min(cols, 1024)
        for row in range(0, half, row_step):
            for col in range(0, cols, col_step):
                tiles = col_step // 128
                side = tiles // 3
                if tiles % 3 == 2 and len(items) % 2:
                    side += 1
                items.append((w, row, row_step, col, side * 128, (tiles - 2 * side) * 128))
    for k in (1, 2):
        w, row, rows, col, edge, middle = items[-k]
        items[-k] = (w, row, rows, col, 0, middle + 2 * edge)
    return items


UR = 128


def unit_cols(count):
    return 2048 // count

LAG = 2
RING = 2 * LAG + 2
ZRING = 6
ORING = 32
CRING = 4


def outer(left, right):
    return lax.dot_general(left, right, (((0,), (0,)), ((), ())), preferred_element_type=jnp.float32)


def unpack_kernel(tiles, cuts, packed, small, *refs):
    many, unit = len(tiles), packed.shape[3]
    outs, pieces = refs[:many], refs[many : many + len(cuts)]
    wide, (held, load, store) = refs[many + len(cuts) : 2 * many + len(cuts)], refs[2 * many + len(cuts) :]
    copies, base = [], 0
    for w, (nr, nc) in enumerate(tiles):
        copy = pltpu.make_async_copy(packed.at[:, pl.ds(base, nr * nc)], held.at[:, pl.ds(base, nr * nc)], load.at[w])
        copy.start()
        copies.append(copy)
        base += nr * nc
    for piece, (start, stop) in zip(pieces, cuts):
        piece[...] = small[start:stop]
    base, stores = 0, []
    for w, (nr, nc) in enumerate(tiles):
        copies[w].wait()
        for core in range(2):
            for col in range(nc):
                @pl.loop(0, nr)
                def _(row, w=w, core=core, col=col, base=base, nc=nc):
                    wide[w][pl.ds(pl.multiple_of(row * UR, UR), UR), (core * nc + col) * unit : (core * nc + col + 1) * unit] = (
                        held[core, base + row * nc + col].astype(jnp.float32))
        copy = pltpu.make_async_copy(wide[w], outs[w], store.at[w])
        copy.start()
        stores.append(copy)
        base += nr * nc
    for copy in stores:
        copy.wait()


def unpack(packed, small, cuts, count, shapes):
    any_, vmem = pl.BlockSpec(memory_space=pl.ANY), pl.BlockSpec(memory_space=pltpu.VMEM)
    out_shape = [jax.ShapeDtypeStruct((r // count, c), jnp.float32) for r, c in shapes]
    pieces = [jax.ShapeDtypeStruct((stop - start, small.shape[1]), jnp.float32) for start, stop in cuts]
    tiles = [(r // count // UR, c // 2 // packed.shape[3]) for r, c in shapes]
    dma = pltpu.SemaphoreType.DMA((len(shapes),))
    values = pl.pallas_call(
        functools.partial(unpack_kernel, tiles, cuts),
        out_shape=out_shape + pieces,
        in_specs=[any_, vmem],
        out_specs=[any_] * len(shapes) + [vmem] * len(cuts),
        scratch_shapes=[pltpu.VMEM(s.shape, s.dtype) for s in out_shape] + [pltpu.VMEM(packed.shape, packed.dtype), dma, dma],
        compiler_params=pltpu.CompilerParams(vmem_limit_bytes=60 * 2**20),
        name="unpack_gradients",
    )(packed, small)
    return values[: len(shapes)], values[len(shapes) :]


def dot_nn(left, right):
    return lax.dot_general(left, right, (((1,), (0,)), ((), ())), preferred_element_type=jnp.float32)


def dot_nt(left, right):
    return lax.dot_general(left, right, (((1,), (1,)), ((), ())), preferred_element_type=jnp.float32)


def dot_tn(left, right):
    return lax.dot_general(left, right, (((0,), (0,)), ((), ())), preferred_element_type=jnp.float32)


EPS = 1e-05
COLS = 256


def sigmoid(v):
    return 0.5 * jnp.tanh(0.5 * v) + 0.5


def sum_scratch(count, depth, width):
    dma = pltpu.SemaphoreType.DMA((count + depth - 1,))
    return [pltpu.VMEM((8, width), jnp.float32), pltpu.VMEM((8, width), jnp.float32),
            pltpu.VMEM((count, 8, width), jnp.float32), pltpu.VMEM((depth, 8, width), jnp.float32), dma, dma]


CHUNK = 512
LEAD, HOP, FAR = 2, 2, 2
BUDGET = 3.0


def forward_kernel(count, depth, heads, shapes, items, saved_names, in_names, out_names, scratch_names, *refs):
    many = len(shapes)
    edges = np.cumsum([0, len(in_names), many, many, len(saved_names), len(out_names), len(scratch_names)])
    groups = [refs[i:j] for i, j in zip(edges[:-1], edges[1:])]
    shards, wholes, saved = groups[1], groups[2], groups[3]
    r = types.SimpleNamespace(**dict(zip(in_names, groups[0])), **dict(zip(out_names, groups[4])), **dict(zip(scratch_names, groups[5])))
    k = types.SimpleNamespace(**{name: i for i, name in enumerate(saved_names)})
    send, recv = r.send, r.recv
    bits = bits_of(count)
    dp, me = lax.axis_index("dp"), lax.axis_index("fsdp")
    core, place = lax.rem(dp, 2), dp // 2
    side = lax.rem(place, 2)
    mate, twin = flip(dp, 1), flip(dp, 2)
    span, width = r.frames.shape
    inner_width = saved[k.inner1].shape[1]
    size = width // heads
    scale = size ** -0.5

    barrier = pltpu.get_barrier_semaphore()
    pl.semaphore_signal(barrier, inc=1, device_id=(mate, me), device_id_type=MESH)
    for mask in range(1, count):
        pl.semaphore_signal(barrier, inc=1, device_id=(dp, flips(me, mask)), device_id_type=MESH)
    for j in range(1, depth):
        pl.semaphore_signal(barrier, inc=1, device_id=(lax.rem(dp + 2 * j, 2 * depth), me), device_id_type=MESH)
    pl.semaphore_wait(barrier, 1 + count - 1 + depth - 1)

    def remote(src, dst, send_sem, recv_sem, device):
        return pltpu.make_async_remote_copy(
            src_ref=src, dst_ref=dst, send_sem=send_sem, recv_sem=recv_sem, device_id=device, device_id_type=MESH)

    wide = r.small.shape[1]
    here = pl.ds(pl.multiple_of(me * wide, 128), wide)
    small_copies = [remote(r.small, r.small_held.at[:, here], r.small_send.at[mask], r.small_recv.at[mask], (dp, flips(me, mask)))
                    for mask in range(1, count)]
    for copy in small_copies:
        copy.start()
    own_copies = [remote(shards[w], wholes[w].at[pl.ds(pl.multiple_of(me * shapes[w][0], 16), shapes[w][0])],
                         r.own_send.at[w], r.own_recv.at[w], (mate, me)) for w in range(many)]
    steps = len(bits)
    kinds = 2 * steps + 3

    def parts(t):
        w, row, rows, col, edge, middle = items[t]
        base = core * (shapes[w][0] // 2) + row
        plane = pl.ds(pl.multiple_of(col + side * edge, 128), edge + middle)
        given = pl.ds(pl.multiple_of(col + side * (edge + middle), 128), edge)
        taken = pl.ds(pl.multiple_of(col + (1 - side) * (edge + middle), 128), edge)
        return w, base, rows, plane, given, taken, edge

    def block(w, owner, start, rows, cols):
        return wholes[w].at[pl.ds(pl.multiple_of(owner * shapes[w][0] + start, 16), rows), cols]

    def plane_send(t, step):
        w, base, rows, plane, *_ = parts(t)
        if step == 0 and (t == 0 or items[t - 1][0] != w):
            own_copies[w].start()
        for piece in range(2):
            order = bits if piece == 0 else bits[::-1]
            start, extent = base + piece * (rows // 2), rows // 2
            for mask in span_of(order[:step]):
                owner = flips(me, mask)
                src = (shards[w].at[pl.ds(pl.multiple_of(start, 16), extent), plane] if mask == 0
                       else block(w, owner, start, extent, plane))
                remote(src, block(w, owner, start, extent, plane), send.at[t, 2 * step + piece],
                       recv.at[t, 2 * step + piece], (dp, flips(me, order[step]))).start()

    def several(t, cols, kind, device):
        w, base, rows, *_ = parts(t)
        for mask in range(1, count):
            ref = block(w, flips(me, mask), base, rows, cols)
            remote(ref, ref, send.at[t, kind], recv.at[t, kind], device).start()

    def sizes(t, kind):
        _, _, rows, _, edge, middle = items[t]
        if kind < 2 * steps:
            return rows // 2 * 2 ** (kind // 2), edge + middle
        return rows * (count - 1), edge if kind != 2 * steps + 1 else edge + middle

    def wait(sems, t, kind):
        rows, cols = sizes(t, kind)
        if cols:
            ref = wholes[items[t][0]].at[pl.ds(0, rows), pl.ds(0, cols)]
            pltpu.make_async_copy(ref, ref, sems.at[t, kind]).wait()

    total = len(items)

    place_of = [HOP * step for step in range(steps + 1)]
    beyond = place_of[-1] + FAR
    ticks = total + beyond + 2

    def gather_tick(tick):
        t = tick + LEAD
        if t < total and tick >= 0:
            plane_send(t, 0)
        for step in range(1, steps):
            t = tick - place_of[step]
            if 0 <= t < total:
                wait(recv, t, 2 * step - 2)
                wait(recv, t, 2 * step - 1)
                plane_send(t, step)
        t = tick - place_of[steps]
        if 0 <= t < total:
            wait(recv, t, 2 * steps - 2)
            wait(recv, t, 2 * steps - 1)
            _, _, _, plane, given, taken, edge = parts(t)
            if edge:
                several(t, given, 2 * steps, (twin, me))
            several(t, plane, 2 * steps + 1, (mate, me))
        t = tick - beyond
        if 0 <= t < total:
            wait(recv, t, 2 * steps)
            if parts(t)[6]:
                several(t, parts(t)[5], 2 * steps + 2, (mate, me))
        t = tick - beyond - 1
        if 0 <= t < total:
            wait(recv, t, 2 * steps + 1)
            wait(recv, t, 2 * steps + 2)
            w = items[t][0]
            if t == 0 or items[t - 1][0] != w:
                own_copies[w].wait_recv()
            return t
        return None

    loads = {}

    def load(index, src, dst):
        loads[index] = pltpu.make_async_copy(src, dst, r.load_sem.at[index])
        loads[index].start()

    def ready(*need):
        for index in need:
            loads.pop(index).wait()

    def store(index, src):
        pltpu.make_async_copy(src, saved[index], r.store_sem.at[index]).start()

    stored = set()

    def stored_wait(index):
        pltpu.make_async_copy(saved[index], saved[index], r.store_sem.at[index]).wait()
        stored.add(index)

    gain = lambda n: r.small_all[n : n + 1]
    shift = lambda n: r.small_all[6 + n : 7 + n]

    def normed(v):
        center = v - jnp.mean(v, axis=-1, keepdims=True)
        return center * lax.rsqrt(jnp.mean(center * center, axis=-1, keepdims=True) + EPS)

    def norm_rows(src, n, dst):
        @pl.loop(0, span // 64)
        def _(i):
            rows = pl.ds(pl.multiple_of(i * 64, 64), 64)
            dst[rows] = (normed(src[rows].astype(jnp.float32)) * gain(n) + shift(n)).astype(jnp.bfloat16)

    def begin():
        r.small_held[:, here] = r.small[...]
        for copy in small_copies:
            copy.wait()
        r.small_all[...] = r.small_held[...].astype(jnp.float32)
        r.small_out[...] = r.small_all[...]
        norm_rows(r.frames, 0, r.hid1)
        store(k.hidden1, r.hid1)

    def up_half(hidden, part, parts_of):
        chunks = inner_width // CHUNK // parts_of

        @pl.loop(part * chunks, (part + 1) * chunks)
        def _(i):
            cols = pl.ds(pl.multiple_of(i * CHUNK, CHUNK), CHUNK)
            inner = dot_nn(hidden[...], r.up_vm[:, cols])
            r.inner_vm[:, cols] = inner.astype(jnp.bfloat16)
            r.active_vm[:, cols] = (inner * sigmoid(inner)).astype(jnp.bfloat16)

    def after_early():
        store(k.inner1, r.inner_vm)
        store(k.active1, r.active_vm)
        store(k.x1, r.xa)
        norm_rows(r.xa, 1, r.hid2)
        store(k.hidden2, r.hid2)

    def project(which):
        @pl.loop(0, width // CHUNK)
        def _(i):
            cols = pl.ds(pl.multiple_of(i * CHUNK, CHUNK), CHUNK)
            out = dot_nn(r.hid2[...], r.up_vm[:, pl.ds(pl.multiple_of(i * CHUNK + which * width, CHUNK), CHUNK)])
            if which == 0:
                r.content_vm[:, cols] = (out + r.small_all[12:13, cols]).astype(jnp.bfloat16)
                r.offset_vm[:, cols] = (out + r.small_all[13:14, cols]).astype(jnp.bfloat16)
            else:
                dst = r.keys_vm if which == 1 else r.values_vm
                dst[:, cols] = out.astype(jnp.bfloat16)
        if which == 0:
            store(k.content, r.content_vm)
            store(k.offset, r.offset_vm)
        else:
            store(k.keys, r.keys_vm) if which == 1 else store(k.values, r.values_vm)

    def place_offsets():
        ready(3, 4)

        @pl.loop(0, width // CHUNK)
        def _(i):
            cols = pl.ds(pl.multiple_of(i * CHUNK, CHUNK), CHUNK)
            out = dot_nn(r.table_vm[...], r.up_vm[:, pl.ds(pl.multiple_of(i * CHUNK + 3 * width, CHUNK), CHUNK)])
            r.offsets_vm[:, cols] = out.astype(jnp.bfloat16)
        store(k.offsets, r.offsets_vm)

    def attend(first, last):
        @pl.loop(first, last)
        def _(h):
            cols = pl.ds(pl.multiple_of(h * size, size), size)
            slot = lax.rem(h, 2)
            placed = dot_nt(r.offset_vm[:, cols], r.offsets_vm[:, cols])
            moved = pltpu.roll(placed, span + 1, 1, stride=1, stride_axis=0)[:, :span]
            raw = (dot_nt(r.content_vm[:, cols], r.keys_vm[:, cols]) + moved) * scale
            column = lax.broadcasted_iota(jnp.int32, raw.shape, 1)
            scores = jnp.where(column < r.length[0], raw, -1e30)
            grown = jnp.exp(scores - jnp.max(scores, axis=1, keepdims=True))
            probs = (grown * (1.0 / jnp.sum(grown, axis=1, keepdims=True))).astype(jnp.bfloat16)

            @pl.when(h >= 2)
            def _():
                pltpu.make_async_copy(r.probs_vm.at[slot], saved[k.probs].at[h], r.probs_sem.at[slot]).wait()
            r.probs_vm[slot] = probs
            pltpu.make_async_copy(r.probs_vm.at[slot], saved[k.probs].at[h], r.probs_sem.at[slot]).start()
            r.mixed_vm[:, cols] = dot_nn(probs, r.values_vm[:, cols]).astype(jnp.bfloat16)

    def after_attention():
        for slot in range(2):
            pltpu.make_async_copy(r.probs_vm.at[slot], saved[k.probs].at[0], r.probs_sem.at[slot]).wait()
        store(k.mixed, r.mixed_vm)
        ready(5)

        @pl.loop(0, width // 256)
        def _(i):
            cols = pl.ds(pl.multiple_of(i * 256, 256), 256)
            r.xb[:, cols] = r.xa[:, cols] + dot_nn(r.mixed_vm[...], r.down_vm[0:width, cols])
        store(k.x2, r.xb)
        norm_rows(r.xb, 2, r.hid3)
        store(k.hidden3, r.hid3)

    def valid_mask():
        return jnp.where(lax.broadcasted_iota(jnp.int32, (span, 1), 0) < r.length[0], 1.0, 0.0)

    taps = 5
    half = taps // 2

    def convolve():
        ready(6, 7)
        mask = valid_mask()
        r.padded[0:8] = jnp.zeros((8, 256), jnp.float32)
        r.padded[8 + span : 16 + span] = jnp.zeros((8, 256), jnp.float32)
        r.vec[...] = jnp.zeros_like(r.vec)
        r.vec[2:3] = jnp.full((1, width), 1.0, jnp.float32) * jnp.sum(mask)

        @pl.loop(0, width // 256)
        def _(i):
            cols = pl.ds(pl.multiple_of(i * 256, 256), 256)
            gates = pl.ds(pl.multiple_of(i * 256 + width, 256), 256)
            value = dot_nn(r.hid3[...], r.down_vm[width : 2 * width, cols])
            gate = dot_nn(r.hid3[...], r.down_vm[2 * width : 3 * width, cols])
            r.lifted_vm[:, cols] = value.astype(jnp.bfloat16)
            r.lifted_vm[:, gates] = gate.astype(jnp.bfloat16)
            r.padded[8 : 8 + span] = value * sigmoid(gate) * mask
            out = jnp.zeros((span, 256), jnp.float32)
            for tap in range(taps):
                out = out + r.small_all[14 + tap : 15 + tap, cols] * r.padded[8 + tap - half : 8 + tap - half + span]
            r.conv_vm[:, cols] = out
            masked = out * mask
            r.vec[0:1, cols] = jnp.sum(masked, axis=0, keepdims=True)
            r.vec[1:2, cols] = jnp.sum(masked * out, axis=0, keepdims=True)
        store(k.lifted, r.lifted_vm)
        store(k.convolved, r.conv_vm)

    pair_copy = remote(r.vec, r.pair, r.sum_send.at[0], r.sum_recv.at[0], (mate, me))
    plane_copies = [remote(r.plane.at[me], r.plane.at[me], r.sum_send.at[m], r.sum_recv.at[m], (dp, flips(me, m)))
                    for m in range(1, count)]
    line_copies = [remote(r.line.at[place], r.line.at[place], r.sum_send.at[count - 1 + j], r.sum_recv.at[count - 1 + j],
                          (lax.rem(dp + 2 * j, 2 * depth), me)) for j in range(1, depth)]

    def sum_pair():
        pair_copy.start()

    def sum_plane():
        pair_copy.wait()
        r.plane[me] = r.vec[...] + r.pair[...]
        for copy in plane_copies:
            copy.start()

    def sum_line():
        for copy in plane_copies:
            copy.wait()
        r.line[place] = functools.reduce(jnp.add, [r.plane[f] for f in range(count)])
        for copy in line_copies:
            copy.start()

    def after_conv():
        for copy in line_copies:
            copy.wait()
        sums = functools.reduce(jnp.add, [r.line[z] for z in range(depth)])
        frames = sums[2:3]
        mean = sums[0:1] / frames
        inverse = lax.rsqrt(sums[1:2] / frames - mean * mean + EPS)
        r.stats[...] = jnp.concatenate([mean, inverse, frames, jnp.zeros((5, width), jnp.float32)], axis=0)
        ready(8)

        @pl.loop(0, width // 256)
        def _(i):
            cols = pl.ds(pl.multiple_of(i * 256, 256), 256)
            normal = (r.conv_vm[:, cols] - r.stats[0:1, cols]) * r.stats[1:2, cols]
            scaled = normal * r.small_all[5:6, cols] + r.small_all[11:12, cols]
            r.swished_vm[:, cols] = (scaled * sigmoid(scaled)).astype(jnp.bfloat16)
        store(k.swished, r.swished_vm)
        stored_wait(k.x1)

        @pl.loop(0, width // 256)
        def _(i):
            cols = pl.ds(pl.multiple_of(i * 256, 256), 256)
            r.xa[:, cols] = r.xb[:, cols] + dot_nn(r.swished_vm[...], r.down_vm[3 * width : 4 * width, cols])

    def after_conv_norm():
        store(k.x3, r.xa)
        norm_rows(r.xa, 3, r.hid4)
        store(k.hidden4, r.hid4)
        stored_wait(k.inner1)
        stored_wait(k.active1)

    def late_done():
        store(k.inner4, r.inner_vm)
        store(k.active4, r.active_vm)
        stored_wait(k.x2)

    def final():
        r.edge_grads[...] = jnp.zeros_like(r.edge_grads)

        @pl.loop(0, span // 64)
        def _(i):
            start = pl.multiple_of(i * 64, 64)
            rows = pl.ds(start, 64)
            mask = jnp.where(start + lax.broadcasted_iota(jnp.int32, (64, 1), 0) < r.length[0], 1.0, 0.0)
            v = r.xb[rows]
            center = v - jnp.mean(v, axis=-1, keepdims=True)
            rate = lax.rsqrt(jnp.mean(center * center, axis=-1, keepdims=True) + EPS)
            normal = center * rate
            r.output[rows] = ((normal * gain(4) + shift(4)) * mask).astype(jnp.bfloat16)
            grad = r.cotangent[rows].astype(jnp.float32) * mask
            r.edge_grads[0:1] += jnp.sum(grad * normal, axis=0, keepdims=True)
            r.edge_grads[1:2] += jnp.sum(grad, axis=0, keepdims=True)
            inner = grad * gain(4)
            back = rate * (inner - jnp.mean(inner, axis=-1, keepdims=True)
                           - normal * jnp.mean(inner * normal, axis=-1, keepdims=True))
            r.xa[rows] = back
            r.branch_vm[rows] = (0.5 * back).astype(jnp.bfloat16)
        store(k.grad4, r.xa)
        store(k.branch4, r.branch_vm)

    def down_copies(t, w, sems):
        _, row, rows, *_ = items[t]
        shard, part = shapes[w][0], t - min(u for u in range(total) if items[u][0] == w)
        starts = [f * shard + c * (shard // 2) + row for f in range(count) for c in range(2)]
        return rows, starts, [pltpu.make_async_copy(wholes[w].at[pl.ds(start, rows)], r.down_vm.at[pl.ds(start, rows)], sems.at[part, i])
                              for i, start in enumerate(starts)]

    def down_fetch(t, w, sems):
        for copy in down_copies(t, w, sems)[2]:
            copy.start()

    def down_part(t, w, sems, src, dst):
        rows, starts, copies = down_copies(t, w, sems)
        for copy in copies:
            copy.wait()

        @pl.loop(0, width // 256)
        def _(i):
            cols = pl.ds(pl.multiple_of(i * 256, 256), 256)
            acc = functools.reduce(jnp.add, [dot_nn(r.active_vm[:, s : s + rows], r.down_vm[s : s + rows, cols]) for s in starts])
            dst[:, cols] = src[:, cols].astype(jnp.float32) + 0.5 * acc

    def before_final():
        stored_wait(k.x3)

    up, down = r.up_vm, r.down_vm
    last = [max(t for t in range(total) if items[t][0] == w) for w in range(many)]
    phases = []

    def phase(item, cost, *work):
        phases.append((item, cost, work))

    def fetch(index, src, dst):
        return lambda: load(index, src, dst)

    def call(function, *args):
        return lambda: function(*args)

    phase(-1, 1.5, begin)
    early = [t for t in range(total) if items[t][0] == 0]
    late = [t for t in range(total) if items[t][0] == 7]

    arrivals = []

    def up_loads(ts, w, index, after):
        for n, t in enumerate(ts):
            cols = pl.ds(items[t][3], 2 * items[t][4] + items[t][5])
            arrivals.append((t, after, fetch(index + n, wholes[w].at[:, cols], up.at[:, cols])))

    def down_loads(w, sems, after):
        for t in range(total):
            if items[t][0] == w:
                arrivals.append((t, after, call(down_fetch, t, w, sems)))

    up_loads(early, 0, 0, 0)
    for n, t in enumerate(early):
        phase(t, 3.2, call(ready, n), call(up_half, r.hid1, n, len(early)))
    up_over = len(phases)
    down_loads(1, r.early_sem, 0)
    firsts = [t for t in range(total) if items[t][0] == 1]
    for t in firsts:
        phase(t, 4.5 / len(firsts), call(down_part, t, 1, r.early_sem, r.frames if t == firsts[0] else r.xa, r.xa))
    down_over = len(phases)
    phase(last[1], 1.5, after_early)
    arrivals.append((last[2], up_over, fetch(10, wholes[2], up.at[:, pl.ds(0, 3 * width)])))
    phase(last[2], 2.5, call(ready, 10), call(project, 0), call(project, 1), call(project, 2))
    arrivals.append((last[3], up_over, lambda: (load(3, wholes[3], up.at[:, pl.ds(3 * width, width)]), load(4, r.table, r.table_vm))))
    phase(last[3], 3.0, place_offsets)
    lift_over = len(phases)
    for h in range(0, heads, 2):
        phase(last[3], 2.0, call(attend, h, h + 2))
    arrivals.append((last[4], down_over, fetch(5, wholes[4], down.at[pl.ds(0, width)])))
    phase(last[4], 2.0, after_attention)
    arrivals.append((last[5], down_over, lambda: (load(6, wholes[5].at[:, pl.ds(0, width)], down.at[pl.ds(width, width)]),
                                                  load(7, wholes[5].at[:, pl.ds(width, width)], down.at[pl.ds(2 * width, width)]))))
    phase(last[5], 5.5, convolve)
    phase(last[5], 0.1, sum_pair)
    arrivals.append((last[6], down_over, fetch(8, wholes[6], down.at[pl.ds(3 * width, width)])))
    phase(last[5], 2.0, sum_plane)
    phase(last[5], 3.0, sum_line)
    phase(last[6], 4.0, after_conv)
    conv_over = len(phases)
    phase(last[6], 1.0, after_conv_norm)
    up_loads(late, 7, 11, lift_over)
    for n, t in enumerate(late):
        phase(t, 3.2, call(ready, 11 + n), call(up_half, r.hid4, n, len(late)))
    phase(last[7], 0.1, late_done)
    down_loads(8, r.late_sem, conv_over)
    ends = [t for t in range(total) if items[t][0] == 8]
    for t in ends:
        phase(t, 2.0, call(down_part, t, 8, r.late_sem, r.xa if t == ends[0] else r.xb, r.xb))
    phase(total - 1, 4.0, before_final, final)
    over = 0

    def take_arrivals():
        kept = []
        for t, after, work in arrivals:
            if t <= done and after <= over:
                work()
            else:
                kept.append((t, after, work))
        arrivals[:] = kept

    for t in range(min(LEAD, total)):
        plane_send(t, 0)
    done = -1
    for tick in range(ticks):
        finished = gather_tick(tick)
        done = max(done, -1 if finished is None else finished)
        take_arrivals()
        budget = BUDGET
        while phases and phases[0][0] <= done and (budget > 0 or done == total - 1):
            _, cost, work = phases.pop(0)
            budget -= cost
            for step in work:
                step()
            over += 1
            take_arrivals()
    for index in range(len(saved) - 1):
        if index not in stored:
            stored_wait(index)
    for w in range(many):
        own_copies[w].wait_send()
    for t in range(total):
        for kind in range(kinds):
            wait(send, t, kind)


def forward(count, depth, heads, frames, cotangent, lengths, shards, small, table, collective_id=1):
    shapes = [s.shape for s in shards]
    items = gather_items(shapes)
    steps, many = len(bits_of(count)), len(shards)
    span, width = frames.shape
    inner = shapes[0][1]
    any_, vmem, smem = (pl.BlockSpec(memory_space=s) for s in (pl.ANY, pltpu.VMEM, pltpu.SMEM))
    bf, fl = jnp.bfloat16, jnp.float32
    S, dma = jax.ShapeDtypeStruct, pltpu.SemaphoreType.DMA
    V = lambda shape, dtype=bf: pltpu.VMEM(shape, dtype)
    ins = dict(length=(lengths, smem), frames=(frames, vmem), cotangent=(cotangent, vmem), table=(table, any_), small=(small, vmem))
    flat, flat32, tall = S((span, width), bf), S((span, width), fl), S((span, inner), bf)
    saved = dict(hidden1=flat, inner1=tall, active1=tall, x1=flat32, hidden2=flat, content=flat, offset=flat, keys=flat, values=flat,
                 offsets=S(table.shape, bf), mixed=flat, x2=flat32, hidden3=flat, lifted=S((span, 2 * width), bf), convolved=flat32,
                 swished=flat, x3=flat32, hidden4=flat, inner4=tall, active4=tall, grad4=flat32, branch4=flat,
                 probs=S((heads, span, span), bf))
    outs = dict(small_out=S((small.shape[0], width), fl), stats=S((8, width), fl), edge_grads=S((8, width), fl), output=flat)
    vec, pair, plane, line, sum_send, sum_recv = sum_scratch(count, depth, width)
    flat_vm, flat32_vm, gather_sems = V((span, width)), V((span, width), fl), dma((len(items), 2 * steps + 3))
    scratch = dict(
        send=gather_sems, recv=gather_sems, own_send=dma((many,)), own_recv=dma((many,)),
        small_send=dma((count,)), small_recv=dma((count,)), load_sem=dma((16,)), store_sem=dma((len(saved),)), probs_sem=dma((2,)),
        early_sem=dma((8, 2 * count)), late_sem=dma((8, 2 * count)),
        small_held=V((small.shape[0], width)), small_all=V((small.shape[0], width), fl),
        up_vm=V((width, inner)), down_vm=V((inner, width)), xa=flat32_vm, xb=flat32_vm,
        hid1=flat_vm, hid2=flat_vm, hid3=flat_vm, hid4=flat_vm, inner_vm=V((span, inner)), active_vm=V((span, inner)),
        content_vm=flat_vm, offset_vm=flat_vm, keys_vm=flat_vm, values_vm=flat_vm, table_vm=V(table.shape), offsets_vm=V(table.shape),
        probs_vm=V((2, span, span)), mixed_vm=flat_vm, lifted_vm=V((span, 2 * width)), conv_vm=flat32_vm, swished_vm=flat_vm,
        branch_vm=flat_vm, padded=V((span + 16, 256), fl),
        vec=vec, pair=pair, plane=plane, line=line, sum_send=sum_send, sum_recv=sum_recv)
    whole = [S((rows * count, cols), bf) for rows, cols in shapes]
    values = pl.pallas_call(
        functools.partial(forward_kernel, count, depth, heads, shapes, items, list(saved), list(ins), list(outs), list(scratch)),
        out_shape=whole + list(saved.values()) + list(outs.values()),
        in_specs=[b for _, b in ins.values()] + [any_] * many,
        out_specs=[any_] * (many + len(saved)) + [vmem] * len(outs),
        scratch_shapes=list(scratch.values()),
        compiler_params=pltpu.CompilerParams(collective_id=collective_id, has_side_effects=True, vmem_limit_bytes=63 * 2**20),
        name="forward",
    )(*[v for v, _ in ins.values()], *shards)
    return values[:many], types.SimpleNamespace(**dict(zip(list(saved) + list(outs), values[many:])))


COLS = 256
SLICE = 512


def backward_kernel(count, depth, heads, shapes, in_names, out_names, scratch_names, *refs):
    edges = np.cumsum([0, len(in_names), len(out_names), len(scratch_names)])
    groups = [refs[i:j] for i, j in zip(edges[:-1], edges[1:])]
    r = types.SimpleNamespace(**dict(zip(in_names, groups[0])), **dict(zip(out_names, groups[1])), **dict(zip(scratch_names, groups[2])))
    many, unit = len(shapes), unit_cols(count)
    lefts = [r.active4, r.hidden4, r.swished, r.hidden3, r.mixed, r.table, r.hidden2, r.active1, r.hidden1]
    rights = [r.branch4, r.inner_grad4, r.out_grad3, r.lifted_grad, r.out_grad2, r.offsets_grad, r.joint_grad, r.branch1, r.inner_grad1]
    bits = bits_of(count)
    steps, half = len(bits), depth // 2
    dp, me = lax.axis_index("dp"), lax.axis_index("fsdp")
    core, place = lax.rem(dp, 2), dp // 2
    mate = flip(dp, 1)
    low = place < half
    level = jnp.minimum(place, depth - 1 - place)
    inward = jnp.where(low, dp + 2, dp - 2)
    outward = jnp.where(low, dp - 2, dp + 2)
    span, width = r.grad4.shape
    inner_width = r.inner4.shape[1]
    size = width // heads
    scale = size ** -0.5

    def remote(src, dst, send, recv, device):
        return pltpu.make_async_remote_copy(
            src_ref=src, dst_ref=dst, send_sem=send, recv_sem=recv, device_id=device, device_id_type=MESH)

    def loading(src, dst, index):
        return pltpu.make_async_copy(src, dst, r.load_sem.at[index])

    def storing(src, dst, index):
        return pltpu.make_async_copy(src, dst, r.store_sem.at[index])

    units = [(rows // count // UR) * (cols // 2 // unit) for rows, cols, _ in shapes]
    bases = [int(b) for b in np.cumsum([0] + units)]
    whole = bases[-1]

    def unit_copies(w, i, slot):
        rows, cols, deep = shapes[w]
        rows, chunks = rows // count, cols // 2 // unit
        row, col = i // chunks, lax.rem(i, chunks)
        copies = []
        for m in range(count):
            src = lefts[w].at[:, pl.ds(pl.multiple_of(flips(me, m) * rows + row * UR, UR), UR)]
            copies.append(pltpu.make_async_copy(src, r.a_st.at[slot, pl.ds(0, deep), pl.ds(m * UR, UR)], r.st_sem.at[slot, m]))
        for n, owner in enumerate((1 - core, core)):
            src = rights[w].at[:, pl.ds(pl.multiple_of(owner * (cols // 2) + col * unit, unit), unit)]
            copies.append(pltpu.make_async_copy(src, r.b_st.at[slot, n, pl.ds(0, deep)], r.st_sem.at[slot, count + n]))
        return copies

    def fetch_unit(u):
        for w in range(many):
            @pl.when(jnp.logical_and(u >= bases[w], u < bases[w + 1]))
            def _(w=w):
                for copy in unit_copies(w, u - bases[w], lax.rem(u, 2)):
                    copy.start()

    def c_copy(u):
        s = lax.rem(u, CRING)
        return remote(r.snd_c.at[s], r.rcv_c.at[s], r.c_send.at[s], r.c_recv.at[s], (mate, me))

    def d_copy(j, piece, u):
        s = lax.rem(u, RING)
        order = bits if piece == 0 else bits[::-1]
        return remote(d_snd[j].at[s, piece], d_rcv[j].at[s, piece],
                      r.d_send.at[j, piece, s], r.d_recv.at[j, piece, s], (dp, flip(me, order[j])))

    d_snd = [r.d_snd0, r.d_snd1, r.d_snd2][:steps]
    d_rcv = [r.d_rcv0, r.d_rcv1, r.d_rcv2][:steps]

    def zi_copy(u):
        s = lax.rem(u, ZRING)
        return remote(r.z_snd.at[s], r.z_acc.at[s], r.zi_send.at[s], r.za_recv.at[s], (inward, me))

    def zm_copy(u):
        s = lax.rem(u, ZRING)
        return remote(r.z_snd.at[s], r.z_mid.at[s], r.zi_send.at[s], r.zm_recv.at[s], (inward, me))

    def loc_copy(u):
        s = lax.rem(u, ZRING)
        return pltpu.make_async_copy(r.total.at[s], r.packed.at[core, u], r.loc_sem.at[s])

    def mt_copy(u, src):
        s = lax.rem(u, ORING)
        return remote(src, r.packed.at[core, u], r.mt_send.at[s], r.mt_recv.at[s], (mate, me))

    def zo_copy(u, src):
        s = lax.rem(u, ORING)
        return remote(src, r.packed.at[core, u], r.zo_send.at[s], r.zo_recv.at[s], (outward, me))

    def first(u):
        slot, s = lax.rem(u, 2), lax.rem(u, CRING)
        depths = sorted(set(deep for *_, deep in shapes))
        for deep in depths:
            ws = [w for w in range(many) if shapes[w][2] == deep]
            cond = functools.reduce(jnp.logical_or, [jnp.logical_and(u >= bases[w], u < bases[w + 1]) for w in ws])

            @pl.when(cond)
            def _(deep=deep, w=ws[0]):
                for copy in unit_copies(w, 0, slot):
                    copy.wait()
                left = r.a_st[slot, 0:deep]
                r.snd_c[s] = outer(left, r.b_st[slot, 0, 0:deep]).astype(jnp.bfloat16).reshape(count, UR, unit)
                c_copy(u).start()
                r.own[lax.rem(u, RING)] = outer(left, r.b_st[slot, 1, 0:deep]).reshape(count, UR, unit)

    def rows_of(piece):
        return slice(piece * (UR // 2), (piece + 1) * (UR // 2))

    def second(u):
        c_copy(u).wait()
        s, c = lax.rem(u, RING), lax.rem(u, CRING)
        for piece in range(2):
            order = bits if piece == 0 else bits[::-1]
            rs = rows_of(piece)
            for k, m in enumerate(span_of(order[1:])):
                x = m + order[0]
                d_snd[0][s, piece, k] = (r.own[s, x, rs] + r.rcv_c[c, x, rs].astype(jnp.float32)).astype(jnp.bfloat16)
            d_copy(0, piece, u).start()
        for piece in range(2):
            order = bits if piece == 0 else bits[::-1]
            rs = rows_of(piece)
            for m in span_of(order[1:]):
                r.own[s, m, rs] = r.own[s, m, rs] + r.rcv_c[c, m, rs].astype(jnp.float32)

    def onward(j, u):
        s = lax.rem(u, RING)
        for piece in range(2):
            d_copy(j - 1, piece, u).wait()
            order = bits if piece == 0 else bits[::-1]
            rs = rows_of(piece)
            spans, keep = span_of(order[j:]), span_of(order[j + 1 :])
            for k, m in enumerate(spans):
                if m not in keep:
                    d_snd[j][s, piece, keep.index(m - order[j])] = (
                        r.own[s, m, rs] + d_rcv[j - 1][s, piece, k].astype(jnp.float32)).astype(jnp.bfloat16)
            d_copy(j, piece, u).start()
            for k, m in enumerate(spans):
                if m in keep:
                    r.own[s, m, rs] = r.own[s, m, rs] + d_rcv[j - 1][s, piece, k].astype(jnp.float32)

    def plane_done(u):
        s, z = lax.rem(u, RING), lax.rem(u, ZRING)
        for piece in range(2):
            d_copy(steps - 1, piece, u).wait()
            rs = rows_of(piece)
            r.zsum[z, rs] = r.own[s, 0, rs] + d_rcv[steps - 1][s, piece, 0].astype(jnp.float32)

        @pl.when(level == 0)
        def _():
            r.z_snd[z] = r.zsum[z].astype(jnp.bfloat16)
            if half == 1:
                zm_copy(u).start()
            else:
                zi_room(u)
                zi_copy(u).start()

    def zi_room(u):
        @pl.when(u >= ZRING)
        def _():
            pl.semaphore_wait(r.z_free, 1)

    def climb(j, u):
        z = lax.rem(u, ZRING)

        @pl.when(level == j - 1)
        def _():
            zi_copy(u).wait_send()

        @pl.when(level == j)
        def _():
            zi_copy(u).wait_recv()
            r.z_snd[z] = (r.zsum[z] + r.z_acc[z].astype(jnp.float32)).astype(jnp.bfloat16)

            @pl.when(u < whole - ZRING)
            def _():
                pl.semaphore_signal(r.z_free, inc=1, device_id=(outward, me), device_id_type=MESH)
            if j == half - 1:
                zm_copy(u).start()
            else:
                zi_room(u)
                zi_copy(u).start()

    def middle(u):
        z = lax.rem(u, ZRING)

        @pl.when(level == half - 1)
        def _():
            zm_copy(u).wait()
            r.total[z] = (r.z_snd[z].astype(jnp.float32) + r.z_mid[z].astype(jnp.float32)).astype(jnp.bfloat16)
            if half > 1:
                zo_copy(u, r.total.at[z]).start()
            mt_copy(u, r.total.at[z]).start()
            loc_copy(u).start()

    def descend(j, u):
        z = lax.rem(u, ZRING)

        @pl.when(level == half - j)
        def _():
            src = r.total.at[z] if j == 1 else r.packed.at[core, u]
            zo_copy(u, src).wait_send()

        @pl.when(level == half - 1 - j)
        def _():
            zo_copy(u, r.packed.at[core, u]).wait_recv()
            if j < half - 1:
                zo_copy(u, r.packed.at[core, u]).start()
            mt_copy(u, r.packed.at[core, u]).start()

    def finish(u):
        z = lax.rem(u, ZRING)

        @pl.when(level == half - 1)
        def _():
            loc_copy(u).wait()
        mt_copy(u, r.total.at[z]).wait()

    stages = [(1, second)]
    at = 1
    for j in range(1, steps):
        at += LAG
        stages.append((at, functools.partial(onward, j)))
    at += LAG
    stages.append((at, plane_done))
    for j in range(1, half):
        at += LAG
        stages.append((at, functools.partial(climb, j)))
    at += LAG
    stages.append((at, middle))
    for j in range(1, half):
        at += LAG
        stages.append((at, functools.partial(descend, j)))
    at += LAG
    stages.append((at, finish))

    slices = inner_width // SLICE

    def slice_streams(i, up, inner):
        slot, cols = lax.rem(i, 2), pl.ds(pl.multiple_of(i * SLICE, SLICE), SLICE)
        return (pltpu.make_async_copy(up.at[:, cols], r.up_st.at[slot], r.up_sem.at[slot]),
                pltpu.make_async_copy(inner.at[:, cols], r.in_st.at[slot], r.in_sem.at[slot]))

    def slice_store(i, dst):
        slot, cols = lax.rem(i, 2), pl.ds(pl.multiple_of(i * SLICE, SLICE), SLICE)
        return pltpu.make_async_copy(r.ig_st.at[slot], dst.at[:, cols], r.ig_sem.at[slot])

    def slices_begin(down, up, inner):
        for i in range(slices):
            rows = pl.ds(i * SLICE, SLICE)
            pltpu.make_async_copy(down.at[rows], r.w_vm.at[rows], r.w_sem.at[i]).start()
        for i in range(2):
            for copy in slice_streams(i, up, inner):
                copy.start()

    def slice_work(i, late):
        slot = lax.rem(i, 2)
        rows = pl.ds(pl.multiple_of(i * SLICE, SLICE), SLICE)
        pltpu.make_async_copy(r.late_down.at[rows], r.w_vm.at[rows], r.w_sem.at[i]).wait()
        for copy in slice_streams(i, r.late_up, r.inner4):
            copy.wait()

        @pl.when(i >= 2)
        def _():
            slice_store(i, r.inner_grad4).wait()

        @pl.loop(0, SLICE // COLS)
        def _(c):
            part = pl.ds(pl.multiple_of(c * COLS, COLS), COLS)
            active_grad = dot_nt(r.og[...], r.w_vm[pl.ds(pl.multiple_of(i * SLICE + c * COLS, COLS), COLS)])
            inner = r.in_st[slot, :, part].astype(jnp.float32)
            gate = sigmoid(inner)
            r.ig_st[slot, :, part] = (active_grad * (gate * (1.0 + inner * (1.0 - gate)))).astype(jnp.bfloat16)

        @pl.when(late)
        def _():
            slice_store(i, r.inner_grad4).start()

        @pl.when(jnp.logical_not(late))
        def _():
            slice_store(i, r.inner_grad1).start()

        @pl.loop(0, width // COLS)
        def _(c):
            part = pl.ds(pl.multiple_of(c * COLS, COLS), COLS)
            r.acc[:, part] += dot_nt(r.ig_st[slot], r.up_st[slot, part])

        @pl.when(jnp.logical_and(late, i < slices - 2))
        def _():
            for copy in slice_streams(i + 2, r.late_up, r.inner4):
                copy.start()

        @pl.when(jnp.logical_and(jnp.logical_not(late), i < slices - 2))
        def _():
            for copy in slice_streams(i + 2, r.early_up, r.inner1):
                copy.start()

    def slices_over(dst):
        for i in range(2):
            slice_store(i, dst).wait()

    def norm_back(n, factor):
        gain = r.small_all[pl.ds(n, 1)]
        r.sums[...] = jnp.zeros_like(r.sums)

        @pl.loop(0, span // 64)
        def _(i):
            rows = pl.ds(pl.multiple_of(i * 64, 64), 64)
            v, grad = r.x[rows], r.acc[rows]
            center = v - jnp.mean(v, axis=-1, keepdims=True)
            rate = lax.rsqrt(jnp.mean(center * center, axis=-1, keepdims=True) + EPS)
            normal = center * rate
            r.sums[0:1] += jnp.sum(grad * normal, axis=0, keepdims=True)
            r.sums[1:2] += jnp.sum(grad, axis=0, keepdims=True)
            inner = grad * gain
            back = r.grad[rows] + rate * (inner - jnp.mean(inner, axis=-1, keepdims=True)
                                          - normal * jnp.mean(inner * normal, axis=-1, keepdims=True))
            r.grad[rows] = back
            r.og[rows] = (factor * back).astype(jnp.bfloat16)
        r.small_buf[pl.ds(n, 1)] = r.sums[0:1]
        r.small_buf[pl.ds(n + 6, 1)] = r.sums[1:2]

    def valid_mask():
        return jnp.where(lax.broadcasted_iota(jnp.int32, (span, 1), 0) < r.length[0], 1.0, 0.0)

    taps = 5
    reach = taps // 2

    def conv_first(j):
        cols = pl.ds(pl.multiple_of(j * COLS, COLS), COLS)
        mask = valid_mask()
        swish_grad = dot_nt(r.og[...], r.w_vm[cols])
        normal = (r.x[:, cols] - r.stats[0:1, cols]) * r.stats[1:2, cols]
        scaled = normal * r.small_all[5:6, cols] + r.small_all[11:12, cols]
        gate = sigmoid(scaled)
        scaled_grad = swish_grad * (gate * (1.0 + scaled * (1.0 - gate)))
        r.acc[:, cols] = scaled_grad
        masked = scaled_grad * mask
        r.vec[0:1, cols] = jnp.sum(masked, axis=0, keepdims=True)
        r.vec[1:2, cols] = jnp.sum(masked * normal, axis=0, keepdims=True)

    def conv_second(j):
        cols = pl.ds(pl.multiple_of(j * COLS, COLS), COLS)
        gates = pl.ds(pl.multiple_of(j * COLS + width, COLS), COLS)
        mask = valid_mask()
        normal = (r.x[:, cols] - r.stats[0:1, cols]) * r.stats[1:2, cols]
        inner = mask * ((r.vec[0:1, cols] + normal * r.vec[1:2, cols]) / r.stats[2:3, cols])
        conv_grad = r.stats[1:2, cols] * r.small_all[5:6, cols] * (r.acc[:, cols] - inner)
        r.padded[8 : 8 + span] = conv_grad
        up, gate = r.lifted_vm[:, cols].astype(jnp.float32), sigmoid(r.lifted_vm[:, gates].astype(jnp.float32))
        r.gated[8 : 8 + span] = up * gate * mask
        total = jnp.zeros((span, COLS), jnp.float32)
        for tap in range(taps):
            total = total + r.small_all[14 + tap : 15 + tap, cols] * r.padded[8 - tap + reach : 8 - tap + reach + span]
            moved = r.gated[8 + tap - reach : 8 + tap - reach + span]
            r.small_buf[14 + tap : 15 + tap, cols] = jnp.sum(moved * conv_grad, axis=0, keepdims=True)
        total = total * mask
        r.lg_vm[:, cols] = (total * gate).astype(jnp.bfloat16)
        r.lg_vm[:, gates] = (total * up * gate * (1.0 - gate)).astype(jnp.bfloat16)

    pair_copy = remote(r.vec, r.pair, r.sum_send.at[0], r.sum_recv.at[0], (mate, me))
    plane_copies = [remote(r.plane.at[me], r.plane.at[me], r.sum_send.at[m], r.sum_recv.at[m], (dp, flips(me, m)))
                    for m in range(1, count)]
    line_to = [(lax.rem(dp + 2 * j, 2 * depth), me) for j in range(1, depth)]
    line_copies = [remote(r.line.at[place], r.line.at[place], r.sum_send.at[count + j], r.sum_recv.at[count + j], line_to[j])
                   for j in range(depth - 1)]

    def sum_plane():
        pair_copy.wait()
        r.plane[me] = r.vec[...] + r.pair[...]
        for copy in plane_copies:
            copy.start()

    def sum_line():
        for copy in plane_copies:
            copy.wait()
        r.line[place] = functools.reduce(jnp.add, [r.plane[f] for f in range(count)])
        for copy in line_copies:
            copy.start()

    def sum_over():
        for copy in line_copies:
            copy.wait()
        r.vec[...] = functools.reduce(jnp.add, [r.line[z] for z in range(depth)])

    def head_copies(h):
        slot, cols = lax.rem(h, 2), pl.ds(pl.multiple_of(h * size, size), size)
        copies = [pltpu.make_async_copy(src.at[:, cols], r.head_st.at[slot, n], r.head_sem.at[slot, n])
                  for n, src in enumerate((r.content, r.offset, r.keys, r.values))]
        copies.append(pltpu.make_async_copy(r.offsets.at[:, cols], r.place_st.at[slot], r.head_sem.at[slot, 4]))
        copies.append(pltpu.make_async_copy(r.probs.at[h], r.probs_st.at[slot], r.head_sem.at[slot, 5]))
        return copies

    def offsets_store(h):
        slot, cols = lax.rem(h, 2), pl.ds(pl.multiple_of(h * size, size), size)
        return pltpu.make_async_copy(r.turned_st.at[slot], r.offsets_grad.at[:, cols], r.turned_sem.at[slot])

    def attend_back(h):
        slot, cols = lax.rem(h, 2), pl.ds(pl.multiple_of(h * size, size), size)
        for copy in head_copies(h):
            copy.wait()

        @pl.when(h >= 2)
        def _():
            offsets_store(h).wait()
        content, offset, key, value = (r.head_st[slot, n] for n in range(4))
        mixed_grad, p = r.mg_vm[:, cols], r.probs_st[slot]
        key_cols = pl.ds(pl.multiple_of(h * size + width, size), size)
        value_cols = pl.ds(pl.multiple_of(h * size + 2 * width, size), size)
        prob_grad = dot_nt(mixed_grad, value)
        r.joint_vm[:, value_cols] = dot_tn(p, mixed_grad).astype(jnp.bfloat16)
        weights = p.astype(jnp.float32)
        product = weights * prob_grad
        score_grad = product - weights * jnp.sum(product, axis=1, keepdims=True)
        raw_grad = (score_grad * scale).astype(jnp.bfloat16)
        content_grad = dot_nn(raw_grad, key)
        r.joint_vm[:, key_cols] = dot_tn(raw_grad, content).astype(jnp.bfloat16)
        turn = r.turn[...]
        turned = dot_nn(turn, raw_grad)
        wide = jnp.concatenate([turned, jnp.zeros_like(turned)], axis=1)
        placed = pltpu.roll(wide, 0, 1, stride=1, stride_axis=0).astype(jnp.bfloat16)
        turned_offset = dot_nn(turn, offset).astype(jnp.bfloat16)
        r.turned_st[slot] = dot_tn(placed, turned_offset).astype(jnp.bfloat16)
        offsets_store(h).start()
        turned_grad = dot_nn(placed, r.place_st[slot])
        high = turned_grad.astype(jnp.bfloat16)
        small = (turned_grad - high.astype(jnp.float32)).astype(jnp.bfloat16)
        offset_grad = dot_nn(turn, high) + dot_nn(turn, small)
        r.joint_vm[:, cols] = (content_grad + offset_grad).astype(jnp.bfloat16)
        r.small_buf[12:13, cols] = jnp.sum(content_grad, axis=0, keepdims=True)
        r.small_buf[13:14, cols] = jnp.sum(turned_grad, axis=0, keepdims=True)

        @pl.when(h < heads - 2)
        def _():
            for copy in head_copies(h + 2):
                copy.start()

    narrow = r.small_out.shape[1]

    def columns(f):
        return pl.ds(pl.multiple_of(f * narrow, 128), narrow)

    small_pair = remote(r.small_buf, r.s_pair, r.s_send.at[0], r.s_recv.at[0], (mate, me))
    small_plane = [remote(r.s_both.at[:, columns(flips(me, m))], r.s_plane.at[me], r.s_send.at[m], r.s_recv.at[m], (dp, flips(me, m)))
                   for m in range(1, count)]
    small_line = [remote(r.s_line.at[place], r.s_line.at[place], r.s_send.at[count + j], r.s_recv.at[count + j], line_to[j])
                  for j in range(depth - 1)]

    def small_second():
        small_pair.wait()
        r.s_both[...] = r.small_buf[...] + r.s_pair[...]
        for copy in small_plane:
            copy.start()
        r.s_plane[me] = r.s_both[:, columns(me)]

    def small_third():
        for copy in small_plane:
            copy.wait()
        r.s_line[place] = functools.reduce(jnp.add, [r.s_plane[f] for f in range(count)])
        for copy in small_line:
            copy.start()

    def small_last():
        for copy in small_line:
            copy.wait()
        r.small_out[...] = functools.reduce(jnp.add, [r.s_line[z] for z in range(depth)])

    def block(n):
        return r.w_vm.at[pl.ds(n * width, width)]

    conv_loads = [loading(r.convolved, r.x, 2), loading(r.lifted, r.lifted_vm, 3), loading(r.pointwise_down, block(0), 4),
                  loading(r.pointwise_up.at[:, pl.ds(0, width)], block(1), 5),
                  loading(r.pointwise_up.at[:, pl.ds(width, width)], block(2), 6), loading(r.heads_out, block(3), 7)]
    query_loads = [loading(r.heads_in.at[:, pl.ds(n * width, width)], block(n), 9 + n) for n in range(3)]
    state_load, older_load = loading(r.x2, r.x, 8), loading(r.x1, r.x, 12)
    grad3_store, lifted_store = storing(r.og, r.out_grad3, 0), storing(r.lg_vm, r.lifted_grad, 1)
    grad2_store, joint_store = storing(r.og, r.out_grad2, 2), storing(r.joint_vm, r.joint_grad, 3)
    branch_store, frames_store = storing(r.og, r.branch1, 4), storing(r.grad, r.frames_grad, 5)

    def hidden_cols(first_col, last_col, parts):
        @pl.loop(first_col, last_col)
        def _(c):
            cols = pl.ds(pl.multiple_of(c * COLS, COLS), COLS)
            r.acc[:, cols] = functools.reduce(jnp.add, [
                dot_nt(src[:, a * width : (a + 1) * width], r.w_vm[pl.ds(pl.multiple_of(b * width + c * COLS, COLS), COLS)])
                for src, a, b in parts])

    def chain(tick):
        def when(*ticks):
            cond = functools.reduce(jnp.logical_or, [tick == t for t in ticks])
            return pl.when(cond)

        late, begin_late = tick < 6, jnp.where(tick < 2, 2 * tick, tick + 2)
        several_late = tick < 2
        tick = tick - 2

        @pl.when(jnp.logical_or(late, jnp.logical_and(tick >= 24, tick < 24 + slices)))
        def _():
            begin = jnp.where(late, begin_late, tick - 24)

            @pl.loop(0, jnp.where(several_late, 2, 1))
            def _(k):
                slice_work(begin + k, late)

        @when(4)
        def _():
            slices_over(r.inner_grad4)
            starts[0].wait()
            starts[1].wait()
            for copy in conv_loads[2:]:
                copy.start()

        @when(32)
        def _():
            r.x[...] = r.frames[...].astype(jnp.float32)
            slices_over(r.inner_grad1)

        @when(4, 12, 23, 32)
        def _():
            n = jnp.where(tick == 4, 3, jnp.where(tick == 12, 2, jnp.where(tick == 23, 1, 0)))
            norm_back(n, jnp.where(tick == 23, 0.5, 1.0))

        @when(4)
        def _():
            grad3_store.start()
            conv_loads[0].start()
            conv_loads[1].start()

        @when(5)
        def _():
            for copy in conv_loads[:3]:
                copy.wait()

        @when(5, 6)
        def _():
            @pl.loop(0, 2)
            def _(k):
                conv_first(2 * (tick - 5) + k)

        @when(6)
        def _():
            r.small_buf[5:6] = r.vec[1:2]
            r.small_buf[11:12] = r.vec[0:1]
            pair_copy.start()

        when(7)(sum_plane)
        when(8)(sum_line)

        @when(9)
        def _():
            sum_over()

        @when(9, 10)
        def _():
            @pl.loop(0, 2)
            def _(k):
                conv_second(2 * (tick - 9) + k)

        @when(10)
        def _():
            lifted_store.start()
            state_load.start()
            grad3_store.wait()

        @when(11)
        def _():
            conv_loads[3].wait()
            conv_loads[4].wait()
            hidden_cols(0, width // COLS, [(r.lg_vm, 0, 1), (r.lg_vm, 1, 2)])
            state_load.wait()
            for h in range(2):
                for copy in head_copies(h):
                    copy.start()

        @when(12)
        def _():
            lifted_store.wait()
            grad2_store.start()
            older_load.start()
            conv_loads[5].wait()

            @pl.loop(0, width // COLS)
            def _(c):
                cols = pl.ds(pl.multiple_of(c * COLS, COLS), COLS)
                r.mg_vm[:, cols] = dot_nt(r.og[...], r.w_vm[pl.ds(pl.multiple_of(3 * width + c * COLS, COLS), COLS)]).astype(jnp.bfloat16)

        @when(13)
        def _():
            for copy in query_loads:
                copy.start()

        @pl.when(jnp.logical_and(tick >= 13, tick < 13 + heads))
        def _():
            attend_back(tick - 13)

        @when(13 + heads - 1)
        def _():
            joint_store.start()
            for h in range(2):
                offsets_store(h).wait()

        when(16)(grad2_store.wait)
        when(27)(branch_store.wait)
        joint_parts = [(r.joint_vm, n, n) for n in range(3)]

        @when(21)
        def _():
            for copy in query_loads:
                copy.wait()
            older_load.wait()

        @when(21, 22)
        def _():
            begin = (width // COLS // 2) * (tick - 21)
            hidden_cols(begin, begin + width // COLS // 2, joint_parts)

        when(22)(joint_store.wait)

        @when(23)
        def _():
            branch_store.start()
            r.acc[...] = jnp.zeros_like(r.acc)
            slices_begin(r.early_down, r.early_up, r.inner1)

        @when(32)
        def _():
            frames_store.start()
            small_pair.start()

        when(34)(small_second)
        when(36)(small_third)

        @when(38)
        def _():
            small_last()
            frames_store.wait()

    barrier = pltpu.get_barrier_semaphore()
    pl.semaphore_signal(barrier, inc=1, device_id=(mate, me), device_id_type=MESH)
    for mask in range(1, count):
        pl.semaphore_signal(barrier, inc=1, device_id=(dp, flips(me, mask)), device_id_type=MESH)
    for device in line_to:
        pl.semaphore_signal(barrier, inc=1, device_id=device, device_id_type=MESH)
    starts = [loading(r.grad4, r.grad, 0), loading(r.x3, r.x, 1), loading(r.branch4, r.og, 13)]
    fetch_unit(jnp.int32(0))
    starts[2].start()
    slices_begin(r.late_down, r.late_up, r.inner4)
    starts[0].start()
    starts[1].start()
    r.acc[...] = jnp.zeros_like(r.acc)
    r.small_buf[...] = jnp.zeros_like(r.small_buf)
    r.small_buf[4:5] = r.edge_grads[0:1]
    r.small_buf[10:11] = r.edge_grads[1:2]
    r.vec[...] = jnp.zeros_like(r.vec)
    for ref in (r.padded, r.gated):
        ref[0:8] = jnp.zeros((8, COLS), jnp.float32)
        ref[8 + span : 16 + span] = jnp.zeros((8, COLS), jnp.float32)
    row = lax.broadcasted_iota(jnp.int32, (span, span), 0)
    column = lax.broadcasted_iota(jnp.int32, (span, span), 1)
    r.turn[...] = jnp.where(row + column == span - 1, 1.0, 0.0).astype(jnp.bfloat16)
    pl.semaphore_wait(barrier, 1 + count - 1 + depth - 1)
    starts[2].wait()

    @pl.loop(0, whole + at + 1)
    def _(tick):
        @pl.when(tick + 1 < whole)
        def _():
            fetch_unit(tick + 1)

        @pl.when(tick < whole)
        def _():
            first(tick)
        for lag, stage in stages:
            pl.when(jnp.logical_and(tick >= lag, tick - lag < whole))(functools.partial(stage, tick - lag))
        chain(tick)


def backward(count, depth, heads, frames, lengths, wholes, f, table, collective_id=2):
    early_up, early_down, heads_in, _, heads_out, pointwise_up, pointwise_down, late_up, late_down = wholes
    any_, vmem, smem = (pl.BlockSpec(memory_space=s) for s in (pl.ANY, pltpu.VMEM, pltpu.SMEM))
    bf, fl = jnp.bfloat16, jnp.float32
    S, dma = jax.ShapeDtypeStruct, pltpu.SemaphoreType.DMA
    V = lambda shape, dtype=bf: pltpu.VMEM(shape, dtype)
    span, width = frames.shape
    inner = early_up.shape[1]
    size, unit = width // heads, unit_cols(count)
    far = dict(
        table=table, early_up=early_up, early_down=early_down, heads_in=heads_in, heads_out=heads_out, pointwise_up=pointwise_up,
        pointwise_down=pointwise_down, late_up=late_up, late_down=late_down, active4=f.active4, branch4=f.branch4, inner4=f.inner4,
        hidden4=f.hidden4, grad4=f.grad4, x3=f.x3, convolved=f.convolved, lifted=f.lifted, swished=f.swished, hidden3=f.hidden3,
        x2=f.x2, mixed=f.mixed, content=f.content, offset=f.offset, keys=f.keys, values=f.values, probs=f.probs, offsets=f.offsets,
        hidden2=f.hidden2, x1=f.x1, active1=f.active1, inner1=f.inner1, hidden1=f.hidden1)
    near = dict(frames=frames, small_all=f.small_out, stats=f.stats, edge_grads=f.edge_grads)
    shapes = [(inner, width, span), (width, inner, span), (width, width, span), (width, 2 * width, span), (width, width, span),
              (width, width, table.shape[0]), (width, 3 * width, span), (inner, width, span), (width, inner, span)]
    units = sum((rows // count // UR) * (cols // 2 // unit) for rows, cols, _ in shapes)
    rows = f.small_out.shape[0]
    flat, tall = S((span, width), bf), S((span, inner), bf)
    far_outs = dict(packed=S((2, units, UR, unit), bf), frames_grad=S((span, width), fl), inner_grad4=tall, out_grad3=flat,
                    lifted_grad=S((span, 2 * width), bf), out_grad2=flat, offsets_grad=S(table.shape, bf),
                    joint_grad=S((span, 3 * width), bf), branch1=flat, inner_grad1=tall)
    near_outs = dict(small_out=S((rows, width // count), fl))
    vec, pair, plane, line, _, _ = sum_scratch(count, depth, width)
    bits = bits_of(count)
    deepest = max(deep for *_, deep in shapes)
    block_ring = V((CRING, count, UR, unit))
    z_ring = V((ZRING, UR, unit))
    scratch = dict(
        a_st=V((2, deepest, count * UR)), b_st=V((2, 2, deepest, unit)), st_sem=dma((2, count + 2)),
        own=V((RING, count, UR, unit), fl), snd_c=block_ring, rcv_c=block_ring,
        zsum=V((ZRING, UR, unit), fl), z_snd=z_ring, z_acc=z_ring, z_mid=z_ring, total=z_ring,
        c_send=dma((CRING,)), c_recv=dma((CRING,)), zi_send=dma((ZRING,)), za_recv=dma((ZRING,)), zm_recv=dma((ZRING,)), z_free=pltpu.SemaphoreType.REGULAR,
        loc_sem=dma((ZRING,)), mt_send=dma((ORING,)), mt_recv=dma((ORING,)), zo_send=dma((ORING,)), zo_recv=dma((ORING,)),
        d_send=dma((len(bits), 2, RING)), d_recv=dma((len(bits), 2, RING)),
        s_pair=V((rows, width), fl), s_both=V((rows, width), fl), s_plane=V((count, rows, width // count), fl),
        s_line=V((depth, rows, width // count), fl), s_send=dma((count + depth,)), s_recv=dma((count + depth,)),
        load_sem=dma((14,)), store_sem=dma((6,)), small_buf=V((rows, width), fl), sums=V((8, width), fl),
        w_vm=V((inner, width)), w_sem=dma((inner // SLICE,)), up_st=V((2, width, SLICE)), up_sem=dma((2,)),
        in_st=V((2, span, SLICE)), in_sem=dma((2,)), ig_st=V((2, span, SLICE)), ig_sem=dma((2,)),
        grad=V((span, width), fl), acc=V((span, width), fl), x=V((span, width), fl), og=V((span, width)),
        lifted_vm=V((span, 2 * width)), lg_vm=V((span, 2 * width)), padded=V((span + 16, COLS), fl), gated=V((span + 16, COLS), fl),
        vec=vec, pair=pair, plane=plane, line=line, sum_send=dma((count + depth,)), sum_recv=dma((count + depth,)),
        head_st=V((2, 4, span, size)), place_st=V((2, table.shape[0], size)), probs_st=V((2, span, span)), head_sem=dma((2, 6)),
        turned_st=V((2, table.shape[0], size)), turned_sem=dma((2,)), joint_vm=V((span, 3 * width)), mg_vm=V((span, width)),
        turn=V((span, span)))
    tiny = V((8, 128))
    rings = [V((RING, 2, count // 2 ** (j + 1), UR // 2, unit)) if j < len(bits) else tiny for j in range(3)]
    scratch.update(d_snd0=rings[0], d_snd1=rings[1], d_snd2=rings[2], d_rcv0=rings[0], d_rcv1=rings[1], d_rcv2=rings[2])
    names = [["length"] + list(near) + list(far), list(far_outs) + list(near_outs), list(scratch)]
    values = pl.pallas_call(
        functools.partial(backward_kernel, count, depth, heads, shapes, *names),
        out_shape=list(far_outs.values()) + list(near_outs.values()),
        in_specs=[smem] + [vmem] * len(near) + [any_] * len(far),
        out_specs=[any_] * len(far_outs) + [vmem] * len(near_outs),
        scratch_shapes=list(scratch.values()),
        compiler_params=pltpu.CompilerParams(collective_id=collective_id, has_side_effects=True, vmem_limit_bytes=63 * 2**20 + 2**19),
        name="backward",
    )(lengths, *near.values(), *far.values())
    return values[0], values[1], values[-1], [s[:2] for s in shapes]


HEADS = 8


def position_table(span, width):
    distance = (span - 1 - np.arange(2 * span - 1)).astype(np.float32)
    rate = np.exp(np.arange(width // 2).astype(np.float32) * np.float32(-2.0 * math.log(10000.0) / width))
    angle = distance[:, None] * rate[None, :]
    table = np.concatenate([np.sin(angle), np.cos(angle)], axis=1)
    return np.concatenate([table, np.zeros((1, width), np.float32)]).astype(jnp.bfloat16)


def body(count, depth, frames, lengths, cotangent, early_up, early_down, heads_in, offset_proj, heads_out,
         pointwise_up, pointwise_down, late_up, late_down, depthwise, norm_gains, norm_shifts, score_bias):
    _, span, width = frames.shape
    taps = depthwise.shape[0]
    table = jnp.asarray(position_table(span, width))
    small = jnp.concatenate([norm_gains, norm_shifts, score_bias, depthwise], axis=0)
    rows = small.shape[0]
    small = jnp.pad(small, ((0, 32 - rows), (0, 0)))
    wholes, f = forward(count, depth, HEADS, frames[0], cotangent[0], lengths,
                [early_up, early_down, heads_in, offset_proj, heads_out, pointwise_up, pointwise_down, late_up, late_down],
                small, table)
    packed, frames_grad, small_sum, shapes = backward(count, depth, HEADS, frames[0], lengths, wholes, f, table)
    grads, pieces = unpack(packed, small_sum, [(14, 14 + taps), (0, 6), (6, 12), (12, 14)], count, shapes)
    (late_down_grad, late_up_grad, pointwise_down_grad, pointwise_up_grad, heads_out_grad, offset_proj_grad, heads_in_grad,
     early_down_grad, early_up_grad) = grads
    return (
        f.output[None], frames_grad[None], early_up_grad, early_down_grad, heads_in_grad, offset_proj_grad, heads_out_grad,
        pointwise_up_grad, pointwise_down_grad, late_up_grad, late_down_grad, *pieces,
    )


def solution(mesh):
    item = P(("dp", "fsdp"), None, None)
    rows = P("fsdp", None)
    cols = P(None, "fsdp")
    in_specs = (item, P(("dp", "fsdp")), item) + (rows,) * 9 + (cols,) * 4
    out_specs = (item, item) + (rows,) * 9 + (cols,) * 4
    count, depth = mesh.shape["fsdp"], mesh.shape["dp"] // 2
    return jax.shard_map(functools.partial(body, count, depth), mesh=mesh, in_specs=in_specs, out_specs=out_specs, check_vma=False)
```
